256 devices in a mesh: tm: 4 (over x), lat: 8 (over y, core), lon: 8 (over z).
Axes of the slice: x: 4, y: 4, z: 8, core: 2. Of those that a mesh axis runs over, the one named last changes fastest.
Arguments:
- increment: float32 [4, 4, 8, 256, 1024], P('tm', None, None, 'lat', 'lon'), may hold values from -6 to 6
- multiplier: float32 [4, 4, 8, 256, 1024], P('tm', None, None, 'lat', 'lon'), may hold values from -6 to 6
- u_wind: float32 [4, 8, 256, 1024], P('tm', None, 'lat', 'lon'), may hold values from -0.5 to 0.5
- v_wind: float32 [4, 8, 256, 1024], P('tm', None, 'lat', 'lon'), may hold values from -0.5 to 0.5
- diffusion: float32 [4, 8], replicated, may hold values from 0.02 to 0.2
- error_var: float32 [4, 8], replicated, may hold values from 0.2 to 2
- obs_owner: int32 [524288, 1], P(('tm', 'lat', 'lon')), may hold values from 0 to 63; in each aligned block of 2048 rows (0 to 2047, 2048 to 4095, ...) at most 64 rows name the same one
- obs_cell: int32 [524288], P(('tm', 'lat', 'lon')), may hold values from 0 to 3936
- obs_layer: int32 [524288], P(('tm', 'lat', 'lon')), may hold values from 0 to 95
- obs_weight: float32 [524288, 4], P(('tm', 'lat', 'lon')), may hold values from 0 to 1
- obs_dual: float32 [524288], P(('tm', 'lat', 'lon')), may hold values from -6 to 6
- obs_error: float32 [524288], P(('tm', 'lat', 'lon')), may hold values from 0.5 to 2
Outputs:
- model_residual: float32 [4, 4, 8, 256, 1024], P('tm', None, None, 'lat', 'lon')
- obs_residual: float32 [524288], P(('tm', 'lat', 'lon'))
- state_residual: float32 [4, 4, 8, 256, 1024], P('tm', None, None, 'lat', 'lon')
- preconditioned: float32 [4, 4, 8, 256, 1024], P('tm', None, None, 'lat', 'lon')
The draws below stay inside these ranges and needn't reach their ends.
Inputs may be any that keep to these rules, and one draw needn't show every extreme that they name: `obs_owner`: among the rows of one device no block is named more than 64 times, and some block is named exactly 64 times.
All inputs are finite; a program needn't handle non-finite values.
Results may differ from the reference program's by a relative error of at most 0.000062.
Values sent between devices are 32-bit elements; how exact they have to be, the bound alone decides.
No kernel may reach another device: no remote copies, remote signals or barrier semaphores. Data moves between devices by JAX's collectives and lax.ppermute only.
A program may use at most 64 MiB of HBM per device.

```python
import math
import jax
import jax.numpy as jnp
import numpy as np

VARS = 4
LEVELS = 8
STEPS = 3
CLAT = 32
CLON = 128
OBS_DEV = 2048
SUBWIN = 4
LAT_BLOCKS = 8
LON_BLOCKS = 8
BLOCKS = 64
CAP = 64
LAT = 256
LON = 1024
OBS = 524288


def set_ends(entries, stream_key, smallest, top_value):
    longest = entries.shape.index(max(entries.shape))
    spots = []
    for shift in (0, 1):
        where = [jax.random.randint(jax.random.fold_in(stream_key, axis), (), 0, length) for axis, length in enumerate(entries.shape)]
        where[longest] = (where[longest] + shift) % entries.shape[longest]
        spots.append(tuple(where))
    return entries.at[spots[0]].set(smallest).at[spots[1]].set(top_value)


def steps_of(own_key, shape, pieces, low, largest):
    factor_of, own = 1.0, jax.random.fold_in(own_key, 6)
    for position, parts in pieces:
        draws = jnp.exp(jax.random.uniform(jax.random.fold_in(own, position), (parts,), jnp.float32, low / len(pieces), largest / len(pieces)))
        factor_of = factor_of * jnp.repeat(draws, shape[position] // parts).reshape([-1 if axis == position else 1 for axis in range(len(shape))])
    return factor_of


def deal_out(key, own, number, rows, number_of, top, most, slope):
    sequence = jax.random.permutation(key, number_of)
    heavy_load, common = portions_of(number_of, rows * top, most, slope, True), portions_of(number_of, rows * top, most, slope, False)
    places = jnp.arange(number_of)

    def named(tallies, turn):
        used = int((tallies > 0).sum())
        fixed = max(1, used // 4)
        shifted = fixed + (places - fixed + turn * (used - fixed)) % max(1, number_of - fixed)
        return jnp.zeros((number_of,), jnp.int32).at[sequence[jnp.where(places < fixed, places, shifted)]].set(jnp.asarray(tallies, jnp.int32))

    tallies = jnp.where(number % 4 == 0, named(heavy_load, number // 4), named(common, number - number // 4 - 1))
    mixed = jax.random.permutation(jax.random.fold_in(own, 3), number_of)
    source_of, receiver = mixed[0:number_of // 2 * 2:2], mixed[1:number_of // 2 * 2:2]
    room = jnp.minimum(tallies[source_of] - 1, most - tallies[receiver]) // 2
    room = jnp.where((source_of == sequence[0]) | (receiver == sequence[0]) | (tallies[receiver] == 0), 0, jnp.maximum(room, 0))
    shifted = jax.random.randint(jax.random.fold_in(own, 4), (number_of // 2,), 0, 1 << 20) % (room + 1)
    tallies = tallies.at[source_of].add(-shifted).at[receiver].add(shifted)
    members = jnp.searchsorted(jnp.cumsum(tallies), jnp.arange(rows * top), side="right").astype(jnp.int32)
    grid = members.reshape(top, rows).T
    grid = grid[jax.random.permutation(jax.random.fold_in(own, 1), rows)]
    turn = jax.random.randint(jax.random.fold_in(own, 2), (rows, 1), 0, top)
    return jnp.take_along_axis(grid, (jnp.arange(top)[None, :] + turn) % top, axis=1)


def portions_of(count, total, bound, lean, full):
    portions = [(1 << 20) // math.isqrt(grade ** lean) + 1 for grade in range(1, count + 1)]
    largest = bound if full else min(bound, max(-(-total // count), total * portions[0] // sum(portions)))
    least = 1 if total - largest >= count - 1 else 0
    given, surplus = [largest] + [least] * (count - 1), total - largest - least * (count - 1)
    while surplus > 0:
        candidates = [i for i in range(1, count) if given[i] < largest] or [i for i in range(1, count) if given[i] < bound]
        whole, left = sum([portions[i] for i in candidates]), surplus
        for i in candidates:
            more = min(bound - given[i], max(1, left * portions[i] // whole), surplus)
            given[i] = given[i] + more
            surplus = surplus - more
    return np.array(given)


def normal_values(rng, shape, deviation, bound, split=(), held_as=jnp.bfloat16):
    array = jax.random.normal(rng, shape, jnp.float32) * deviation
    if len(split) > 0:
        array = steps_of(rng, shape, split, -0.22, 0.18) * array
    return jnp.clip(array, min=-bound, max=bound).astype(held_as)


def setup_inputs(seed: int = 0) -> dict:
    key_list = jax.random.split(jax.random.key(seed), 13)
    increment = normal_values(key_list[0], (SUBWIN, VARS, LEVELS, LAT, LON), 1.0, 6.0, ((0, 4), (3, 8), (4, 8)), jnp.float32)
    multiplier = normal_values(key_list[1], (SUBWIN, VARS, LEVELS, LAT, LON), 1.0, 6.0, ((0, 4), (3, 8), (4, 8)), jnp.float32)
    u_wind = normal_values(key_list[2], (SUBWIN, LEVELS, LAT, LON), 0.2, 0.5, ((0, 4), (2, 8), (3, 8)), jnp.float32)
    v_wind = normal_values(key_list[3], (SUBWIN, LEVELS, LAT, LON), 0.2, 0.5, ((0, 4), (2, 8), (3, 8)), jnp.float32)
    diffusion = jnp.clip(jnp.exp(jax.random.uniform(key_list[4], (VARS, LEVELS), jnp.float32, math.log(0.02), math.log(0.2))), 0.02, 0.2)
    error_var = jnp.clip(jnp.exp(jax.random.uniform(key_list[5], (VARS, LEVELS), jnp.float32, math.log(0.2), math.log(2.0))), 0.2, 2.0)
    obs_owner_keys = jax.random.split(jax.random.fold_in(key_list[6], 1), OBS // OBS_DEV)
    obs_owner_turns = jax.random.permutation(jax.random.fold_in(key_list[6], 3), OBS // OBS_DEV)
    obs_owner = jax.vmap(lambda own, number: deal_out(jax.random.fold_in(key_list[6], 2), own, number, OBS_DEV, BLOCKS, 1, CAP, 2))(obs_owner_keys, obs_owner_turns).reshape((OBS, 1))
    obs_cell = set_ends(jax.random.randint(key_list[7], (OBS,), 0, (CLAT - 1) * (CLON - 1)), jax.random.fold_in(key_list[7], 1), 0, ((CLAT - 1) * (CLON - 1)) - 1).astype(jnp.int32)
    obs_layer = set_ends(jax.random.randint(key_list[8], (OBS,), 0, STEPS * VARS * LEVELS), jax.random.fold_in(key_list[8], 1), 0, (STEPS * VARS * LEVELS) - 1).astype(jnp.int32)
    obs_weight = jnp.clip(1.0 * jax.random.uniform(key_list[9], (OBS, 4), jnp.float32) ** steps_of(key_list[9], (OBS, 4), ((0, 256),), -0.2, 0.2), 0.0, 1.0)
    obs_dual = normal_values(key_list[10], (OBS,), 1.0, 6.0, ((0, 256),), jnp.float32)
    obs_error = jnp.clip(jnp.exp(math.log(2.0) - 1.3862944 * jax.random.uniform(key_list[11], (OBS,), jnp.float32) ** steps_of(key_list[11], (OBS,), ((0, 256),), -0.2, 0.2)), 0.5, 2.0)
    return dict(increment=increment, multiplier=multiplier, u_wind=u_wind, v_wind=v_wind, diffusion=diffusion, error_var=error_var, obs_owner=obs_owner, obs_cell=obs_cell, obs_layer=obs_layer, obs_weight=obs_weight, obs_dual=obs_dual, obs_error=obs_error)


def east_of(field):
    return jnp.roll(field, -1, axis=-1)


def west_of(field):
    return jnp.roll(field, 1, axis=-1)


def north_of(field):
    zeros = jnp.zeros_like(field[..., :1, :])
    return jnp.concatenate([field[..., 1:, :], zeros], axis=-2)


def south_of(field):
    zeros = jnp.zeros_like(field[..., :1, :])
    return jnp.concatenate([zeros, field[..., :-1, :]], axis=-2)


def tangent_step(field, wind_east, wind_north, diffusion):
    rate = diffusion[:, :, None, None]
    e = east_of(field)
    w = west_of(field)
    n = north_of(field)
    s = south_of(field)
    return ((1.0 - 4.0 * rate) * field + rate * (e + w + n + s)
            - 0.5 * wind_east[None] * (e - w) - 0.5 * wind_north[None] * (n - s))


def adjoint_step(field, wind_east, wind_north, diffusion):
    rate = diffusion[:, :, None, None]
    flux_east = wind_east[None] * field
    flux_north = wind_north[None] * field
    neighbours = east_of(field) + west_of(field) + north_of(field) + south_of(field)
    return ((1.0 - 4.0 * rate) * field + rate * neighbours
            + 0.5 * (east_of(flux_east) - west_of(flux_east))
            + 0.5 * (north_of(flux_north) - south_of(flux_north)))


def reference(increment, multiplier, u_wind, v_wind, diffusion, error_var, obs_owner, obs_cell, obs_layer, obs_weight, obs_dual, obs_error):
    subwin = increment.shape[0]
    lat_total = increment.shape[3]
    lon_total = increment.shape[4]
    per_window = OBS_DEV * LAT_BLOCKS * LON_BLOCKS
    error_scale = error_var[:, :, None, None]
    model_parts = []
    obs_parts = []
    state_parts = []
    previous_end = None
    for window in range(subwin):
        states = [increment[window]]
        for step_num in range(STEPS):
            states.append(tangent_step(states[-1], u_wind[window], v_wind[window], diffusion))
        residual = error_scale * multiplier[window] + increment[window]
        if window > 0:
            residual = residual - previous_end
        model_parts.append(residual)
        previous_end = states[STEPS]
        start = window * per_window
        owner_block = obs_owner[start:start + per_window, 0]
        cells = obs_cell[start:start + per_window]
        glat = (owner_block // LON_BLOCKS) * CLAT + cells // (CLON - 1)
        glon = (owner_block % LON_BLOCKS) * CLON + cells % (CLON - 1)
        base = (obs_layer[start:start + per_window] * lat_total + glat) * lon_total + glon
        trajectory = jnp.stack(states[:STEPS]).reshape(-1)
        offsets = (0, 1, lon_total, lon_total + 1)
        weights = obs_weight[start:start + per_window]
        duals = obs_dual[start:start + per_window]
        observed = jnp.zeros(base.shape, increment.dtype)
        for tile in range(4):
            observed = observed + weights[:, tile] * trajectory[base + offsets[tile]]
        obs_parts.append(obs_error[start:start + per_window] * duals + observed)
        indices = jnp.concatenate([base + offsets[tile] for tile in range(4)])
        amounts = jnp.concatenate([weights[:, tile] * duals for tile in range(4)])
        forcing = jnp.zeros(trajectory.shape, increment.dtype).at[indices].add(amounts)
        forcing = forcing.reshape((STEPS,) + increment.shape[1:])
        if window + 1 < subwin:
            adjoint = -multiplier[window + 1]
        else:
            adjoint = jnp.zeros_like(multiplier[window])
        for step_num in range(STEPS - 1, -1, -1):
            adjoint = adjoint_step(adjoint, u_wind[window], v_wind[window], diffusion) + forcing[step_num]
        state_parts.append(multiplier[window] + adjoint)
    chain_parts = [model_parts[0]]
    for window in range(1, subwin):
        carried = chain_parts[-1]
        for step_num in range(STEPS):
            carried = tangent_step(carried, u_wind[window - 1], v_wind[window - 1], diffusion)
        chain_parts.append(carried + model_parts[window])
    return (jnp.stack(model_parts), jnp.concatenate(obs_parts), jnp.stack(state_parts), jnp.stack(chain_parts))
```

```python
import functools
import jax
import jax.numpy as jnp
from jax import lax
from jax.experimental import pallas as pl
from jax.experimental.pallas import tpu as pltpu
from jax.sharding import PartitionSpec as P

STEPS = 3
F32 = jnp.float32
BF16 = jnp.bfloat16
LANES = 128
TILE = 8


def ring(axis, by):
    count = lax.axis_size(axis)
    return [(i, (i + by) % count) for i in range(count)]


def from_behind(shard, axis, by):
    size = lax.axis_size(axis)
    pairs = [(i, i + by) for i in range(size) if 0 <= i + by < size]
    return lax.ppermute(shard, axis, pairs)


def call(kernel, out_shape, *args, name, flops=0, smem=(), scratch=(), vmem=40):
    specs = [
        pl.BlockSpec(memory_space=pltpu.SMEM if i in smem else pltpu.VMEM) for i in range(len(args))
    ]
    several = isinstance(out_shape, (tuple, list))
    out_specs = pl.BlockSpec(memory_space=pltpu.VMEM)
    return pl.pallas_call(
        kernel,
        out_shape=out_shape,
        in_specs=specs,
        out_specs=[out_specs] * len(out_shape) if several else out_specs,
        scratch_shapes=list(scratch),
        compiler_params=pltpu.CompilerParams(vmem_limit_bytes=vmem * 1024 * 1024),
        cost_estimate=pl.CostEstimate(flops=flops, bytes_accessed=0, transcendentals=0),
        name=name,
    )(*args)


def sds(shape, dtype=F32):
    return jax.ShapeDtypeStruct(shape, dtype)


def iota(shape, dim):
    return lax.broadcasted_iota(jnp.int32, shape, dim)


def split_two(value):
    high = value.astype(BF16).astype(F32)
    return high, value - high


def route_kernel(owner_ref, cell_ref, layer_ref, weight_ref, dual_ref, send_ref, rank_ref, fields_ref, acc_ref, *, blocks, cap, rows, cols):
    count = owner_ref.shape[1]
    chunk = min(256, count)
    cell = cell_ref[...]
    row = ((cell.astype(F32) + 0.5) * (1.0 / (cols - 1))).astype(jnp.int32)
    key = layer_ref[...] * rows + row
    col = cell - row * (cols - 1)
    for half in range(2):
        base = half * TILE
        fields_ref[base : base + 4, :] = weight_ref[...] if half == 0 else jnp.zeros((4, count), F32)
        if half == 1:
            fields_ref[base : base + 1, :] = dual_ref[...]
            fields_ref[base + 1 : base + 2, :] = key.astype(F32)
            fields_ref[base + 2 : base + 3, :] = col.astype(F32)
        fields_ref[base + 4 : base + 8, :] = fields_ref[base : base + 4, :]
    tri = (iota((chunk, chunk), 0) < iota((chunk, chunk), 1)).astype(F32)
    tri_ones = jnp.concatenate([tri, jnp.ones((chunk, LANES), F32)], axis=1).astype(BF16)
    running = jnp.zeros((blocks, 1), F32)
    acc_ref[...] = jnp.zeros_like(acc_ref)
    pair = 2 * iota((blocks // 2, TILE, chunk), 0) + iota((blocks // 2, TILE, chunk), 1) // 4
    for part in range(count // chunk):
        here = slice(part * chunk, (part + 1) * chunk)
        owner = owner_ref[:, here]
        hit = iota((blocks, chunk), 0) == owner
        hit_f = jnp.where(hit, 1.0, 0.0)
        counted = jnp.dot(hit_f.astype(BF16), tri_ones, preferred_element_type=F32)
        before = counted[:, :chunk] + running
        running = running + counted[:, chunk : chunk + 1]
        rank = jnp.sum(jnp.where(hit, before, 0.0), axis=0, keepdims=True).astype(jnp.int32)
        rank_ref[:, here] = rank
        ranks = iota((2 * cap, chunk), 0)
        right = jnp.concatenate(
            [jnp.where(ranks == rank, 1.0, 0.0), jnp.where(ranks == rank + cap, 1.0, 0.0)], axis=1
        ).astype(BF16)
        mine = pair == owner[None]
        highs, lows = [], []
        for half in range(2):
            high, low = split_two(fields_ref[half * TILE : (half + 1) * TILE, here])
            highs.append(jnp.where(mine, high[None], 0.0).reshape(4 * blocks, chunk).astype(BF16))
            lows.append(jnp.where(mine, low[None], 0.0).reshape(4 * blocks, chunk).astype(BF16))
        for left in (jnp.concatenate(highs, axis=1), jnp.concatenate(lows, axis=1)):
            acc_ref[...] += lax.dot_general(
                left, right, (((1,), (1,)), ((), ())), preferred_element_type=F32
            )
    send_ref[...] = acc_ref[...]


def unshuffle(got_ref, slots_ref):
    tiles = slots_ref.shape[0]
    keep = (iota((TILE, LANES), 0) < 4) == (iota((TILE, LANES), 1) < 64)
    for tile in range(tiles):
        value = got_ref[tile * TILE : (tile + 1) * TILE, :]
        other = pltpu.roll(pltpu.roll(value, 4, 0), 64, 1)
        slots_ref[tile] = jnp.where(keep, value, other)


def slot_rows(slots_ref, part, tiles_each):
    def field(num):
        return jnp.concatenate(
            [slots_ref[part * tiles_each + t, num : num + 1, :] for t in range(tiles_each)], axis=1
        )

    return field


def corner_rows(row4, tops, bottoms, j):
    zero = jnp.zeros_like(tops)
    return jnp.where(row4 == j, tops, jnp.where(row4 + 1 == j, bottoms, zero))


def scatter_kernel(got_ref, forcing_ref, south_ref, north_ref, slots_ref, acc_ref, b_ref, *, groups, width, rows):
    unshuffle(got_ref, slots_ref)
    tiles = slots_ref.shape[0]
    tiles_each = min(4, tiles)
    chunk = tiles_each * LANES
    acc_ref[...] = jnp.zeros_like(acc_ref)
    zero = jnp.zeros((), F32)

    def body(part, carry):
        field = slot_rows(slots_ref, part, tiles_each)
        key = field(5).astype(jnp.int32)
        col = field(6).astype(jnp.int32)
        dual = field(4)
        group, row4 = key // 4, key % 4
        left = jnp.where(iota((groups, chunk), 0) == group, 1.0, 0.0).astype(BF16)
        cells = iota((width, chunk), 0)
        here, beside = cells == col, cells == col + 1
        for j in range(5):
            first = split_two(corner_rows(row4, field(0) * dual, field(2) * dual, j))
            second = split_two(corner_rows(row4, field(1) * dual, field(3) * dual, j))
            for term in range(2):
                b_ref[term, j * width : (j + 1) * width, :] = jnp.where(
                    here, first[term], jnp.where(beside, second[term], zero)
                ).astype(BF16)
        dims = (((1,), (1,)), ((), ()))
        acc_ref[...] += lax.dot_general(
            left, b_ref[0], dims, preferred_element_type=F32
        ) + lax.dot_general(left, b_ref[1], dims, preferred_element_type=F32)
        return carry

    lax.fori_loop(0, tiles // tiles_each, body, 0)
    for j in range(4):
        value = acc_ref[:, j * width : (j + 1) * width]
        if j == 0:
            value = value + pltpu.roll(acc_ref[:, 4 * width : 5 * width], 1, 0)
        forcing_ref[pl.ds(j, groups, stride=4), :] = value
    comps = south_ref.shape[0]
    sub = iota((TILE, width), 0)

    def edge(comp, carry):
        late = (2 * comps + comp) * rows
        early = (comps + comp) * rows
        low_late = forcing_ref[pl.ds(pl.multiple_of(late, TILE), TILE), :]
        low_early = forcing_ref[pl.ds(pl.multiple_of(early, TILE), TILE), :]
        high_late = forcing_ref[pl.ds(pl.multiple_of(late + rows - TILE, TILE), TILE), :]
        high_early = forcing_ref[pl.ds(pl.multiple_of(early + rows - TILE, TILE), TILE), :]
        south_ref[comp] = jnp.where(sub < 2, low_late, pltpu.roll(low_early, 2, 0))
        north_ref[comp] = jnp.where(sub >= 6, high_late, pltpu.roll(high_early, 6, 0))
        return carry

    lax.fori_loop(0, comps, edge, 0)


def gather_kernel(got_ref, high_ref, low_ref, out_ref, slots_ref, *, groups, width):
    unshuffle(got_ref, slots_ref)
    tiles = slots_ref.shape[0]
    tiles_each = min(4, tiles)
    chunk = tiles_each * LANES

    def body(part, carry):
        field = slot_rows(slots_ref, part, tiles_each)
        key = field(5).astype(jnp.int32)
        col = field(6).astype(jnp.int32)
        group, row4 = key // 4, key % 4
        right = jnp.where(iota((groups, chunk), 0) == group, 1.0, 0.0).astype(BF16)
        cells = iota((width, chunk), 0)
        here, beside = cells == col, cells == col + 1
        total = jnp.zeros((width, chunk), F32)
        for j in range(5):
            span = slice(j * width, (j + 1) * width)
            picked = jnp.dot(high_ref[span, :], right, preferred_element_type=F32) + jnp.dot(
                low_ref[span, :], right, preferred_element_type=F32
            )
            first = corner_rows(row4, field(0), field(2), j)
            second = corner_rows(row4, field(1), field(3), j)
            total = total + picked * jnp.where(here, first, jnp.where(beside, second, 0.0))
        value = jnp.sum(total, axis=0, keepdims=True)
        lines = []
        for t in range(tiles_each):
            line = value[:, t * LANES : (t + 1) * LANES]
            lines += [line, pltpu.roll(line, 64, 1)]
        size = 2 * tiles_each
        out_ref[pl.ds(pl.multiple_of(part * size, size), size), :] = jnp.concatenate(lines, axis=0)
        return carry

    lax.fori_loop(0, tiles // tiles_each, body, 0)


def finish_obs_kernel(back_ref, owner_ref, rank_ref, dual_ref, error_ref, out_ref):
    blocks = back_ref.shape[0]
    count = owner_ref.shape[1]
    chunk = min(512, count)
    turned = back_ref[...].T
    high, low = split_two(turned)
    high, low = high.astype(BF16), low.astype(BF16)
    for part in range(count // chunk):
        here = slice(part * chunk, (part + 1) * chunk)
        hit = jnp.where(iota((blocks, chunk), 0) == owner_ref[:, here], 1.0, 0.0).astype(BF16)
        picked = jnp.dot(high, hit, preferred_element_type=F32) + jnp.dot(
            low, hit, preferred_element_type=F32
        )
        wanted = iota((LANES, chunk), 0) == rank_ref[:, here]
        value = jnp.sum(jnp.where(wanted, picked, 0.0), axis=0, keepdims=True)
        out_ref[:, here] = error_ref[:, here] * dual_ref[:, here] + value


def shifts_of(centre, halo):
    rows = centre.shape[0]
    lane = iota((rows, LANES), 1)
    centre_e, halo_e = pltpu.roll(centre, LANES - 1, 1), pltpu.roll(halo, LANES - 1, 1)
    centre_w, halo_w = pltpu.roll(centre, 1, 1), pltpu.roll(halo, 1, 1)
    last, start = lane == LANES - 1, lane == 0
    east = (jnp.where(last, halo_e, centre_e), jnp.where(last, centre_e, halo_e))
    west = (jnp.where(start, halo_w, centre_w), jnp.where(start, centre_w, halo_w))
    return east, west


def tangent(field, half_u, half_v, rate):
    rows = field[0].shape[0]
    east, west = shifts_of(*field)
    result = []
    for part in range(2):
        north = pltpu.roll(field[part], rows - 1, 0)
        south = pltpu.roll(field[part], 1, 0)
        e, w = east[part], west[part]
        result.append(
            field[part]
            + rate * ((e + w) + (north + south) - 4.0 * field[part])
            - half_u[part] * (e - w)
            - half_v[part] * (north - south)
        )
    return result


def adjoint(field, half_u, half_v, rate):
    rows = field[0].shape[0]
    spread = [[], [], [], []]
    for part in range(2):
        g = field[part]
        thin = rate * g
        along = half_u[part] * g
        across = half_v[part] * g
        for place, value in zip(spread, (thin + along, thin - along, thin + across, thin - across)):
            place.append(value)
    east, unused = shifts_of(*spread[0])
    unused, west = shifts_of(*spread[1])
    result = []
    for part in range(2):
        north = pltpu.roll(spread[2][part], rows - 1, 0)
        south = pltpu.roll(spread[3][part], 1, 0)
        result.append(
            field[part] - 4.0 * (rate * field[part]) + (east[part] + west[part]) + (north + south)
        )
    return result


def pack_columns(acc, field, offset, width):
    lane = iota(field.shape, 1)
    inside = (lane >= offset) & (lane < offset + width)
    west = jnp.where(inside, pltpu.roll(field, offset, 1), acc[0])
    east = jnp.where(inside, pltpu.roll(field, (offset + width) % LANES, 1), acc[1])
    return west, east


def unpack_columns(east_halo, west_halo, offset, width):
    lane = iota(east_halo.shape, 1)
    east = pltpu.roll(east_halo, (2 * LANES - offset) % LANES, 1)
    west = pltpu.roll(west_halo, (2 * LANES - offset - width) % LANES, 1)
    return jnp.where(lane < width, east, jnp.where(lane >= LANES - width, west, 0.0))


def taller(south, centre, north):
    return jnp.concatenate([south, centre, north], axis=0)


def row_mask(lat, lat_count, rows, pad, width=LANES):
    row = lat * rows - pad + iota((rows + 2 * pad, width), 0)
    return jnp.where((row >= 0) & (row < lat_count * rows), 1.0, 0.0)


class RowPlan:
    def __init__(self, variables, levels, share):
        comps = variables * levels
        self.x = 0
        self.mult = self.x + comps
        self.u = self.mult + comps
        self.v = self.u + levels
        self.t0 = self.v + levels
        self.t1 = self.t0 + 2 * variables * share
        self.t2 = self.t1 + variables * share
        self.w = self.t2 + variables * share
        self.total = self.w + 3 * 2 * share


def deal_kernel(mult_ref, u_ref, v_ref, error_ref, out_ref, *, share):
    variables, levels = mult_ref.shape[:2]
    for target in range(levels // share):
        for near in range(share):
            level = target * share + near
            for var in range(variables):
                out_ref[target, var * share + near] = mult_ref[var, level] * error_ref[var, level]
            out_ref[target, variables * share + near] = u_ref[level]
            out_ref[target, (variables + 1) * share + near] = v_ref[level]


def rows_kernel(x_ref, next_ref, u_ref, v_ref, dealt_ref, low_ref, high_ref, *, plan, share):
    variables, levels, rows = x_ref.shape[:3]
    comps = variables * share
    bottom, top = slice(0, TILE), slice(rows - TILE, rows)
    for ref, rows_here, deep in (
        (low_ref, bottom, slice(0, 2 * TILE)),
        (high_ref, top, slice(rows - 2 * TILE, rows)),
    ):
        for var in range(variables):
            for level in range(levels):
                place = var * levels + level
                ref[plan.x + place] = x_ref[var, level, rows_here, :]
                ref[plan.mult + place] = next_ref[var, level, rows_here, :]
        for level in range(levels):
            ref[plan.u + level] = u_ref[level, rows_here, :]
            ref[plan.v + level] = v_ref[level, rows_here, :]
        for comp in range(comps):
            value = dealt_ref[0, comp, deep, :]
            ref[plan.t0 + 2 * comp] = value[:TILE]
            ref[plan.t0 + 2 * comp + 1] = value[TILE:]
            ref[plan.t1 + comp] = dealt_ref[1, comp, rows_here, :]
            ref[plan.t2 + comp] = dealt_ref[2, comp, rows_here, :]
        for window in range(3):
            for wind in range(2 * share):
                ref[plan.w + window * 2 * share + wind] = dealt_ref[window, comps + wind, rows_here, :]


COL_X, COL_MULT, COL_WIND, COL_T12, COL_TW, COL_T0 = range(6)


def columns_kernel(x_ref, next_ref, u_ref, v_ref, dealt_ref, south_ref, north_ref, west_ref, east_ref, *, plan, share):
    variables, levels, rows = x_ref.shape[:3]
    comps = variables * share
    tall = rows + 2 * TILE

    def blank(height):
        zero = jnp.zeros((height, LANES), F32)
        return zero, zero

    def put(place, packed):
        height = packed[0].shape[0]
        west_ref[place * tall : place * tall + height, :] = packed[0]
        east_ref[place * tall : place * tall + height, :] = packed[1]

    def grown(centre, place):
        return taller(south_ref[place], centre, north_ref[place])

    for ref, start, slot in ((x_ref, plan.x, COL_X), (next_ref, plan.mult, COL_MULT)):
        packed = blank(tall)
        for var in range(variables):
            for level in range(levels):
                place = var * levels + level
                packed = pack_columns(packed, grown(ref[var, level], start + place), 4 * place, 3)
        put(slot, packed)
    packed = blank(tall)
    for level in range(levels):
        packed = pack_columns(packed, grown(u_ref[level], plan.u + level), 4 * level, 3)
        packed = pack_columns(packed, grown(v_ref[level], plan.v + level), 4 * (levels + level), 3)
    put(COL_WIND, packed)
    packed = blank(tall)
    for comp in range(comps):
        packed = pack_columns(packed, grown(dealt_ref[1, comp], plan.t1 + comp), 8 * comp, 6)
        packed = pack_columns(packed, grown(dealt_ref[2, comp], plan.t2 + comp), 8 * (comps + comp), 3)
    put(COL_T12, packed)
    packed = blank(tall)
    for window in range(3):
        for wind in range(2 * share):
            place = window * 2 * share + wind
            packed = pack_columns(
                packed, grown(dealt_ref[window, comps + wind], plan.w + place), 8 * place, 8
            )
    put(COL_TW, packed)
    packed = blank(tall + 2 * TILE)
    for comp in range(comps):
        place = plan.t0 + 2 * comp
        south = jnp.concatenate([south_ref[place], south_ref[place + 1]], axis=0)
        north = jnp.concatenate([north_ref[place], north_ref[place + 1]], axis=0)
        packed = pack_columns(packed, taller(south, dealt_ref[0, comp], north), 16 * comp, 9)
    put(COL_T0, packed)


def forward_kernel(
    rate_ref, spot_ref, x_ref, u_ref, v_ref, south_ref, north_ref, east_ref, west_ref, high_ref, low_ref, end_ref, traj_ref, *, plan, lat_count
):
    variables, levels, rows = x_ref.shape[:3]
    comps = variables * levels
    tall = rows + 2 * TILE
    mask = row_mask(spot_ref[0], lat_count, rows, TILE)

    def extended(centre, place, slot, offset):
        whole = taller(south_ref[place], centre, north_ref[place])
        span = slice(slot * tall, (slot + 1) * tall)
        return [whole * mask, unpack_columns(east_ref[span, :], west_ref[span, :], offset, 3) * mask]

    def body(level, carry):
        half_u = [0.5 * w for w in extended(u_ref[level], plan.u + level, COL_WIND, 4 * level)]
        half_v = [0.5 * w for w in extended(v_ref[level], plan.v + level, COL_WIND, 4 * (levels + level))]
        for var in range(variables):
            comp = var * levels + level
            field = extended(x_ref[var, level], plan.x + comp, COL_X, 4 * comp)
            rate = mask * rate_ref[var, level]
            for step in range(STEPS):
                start = pl.multiple_of((step * comps + comp) * rows, TILE)
                traj_ref[pl.ds(start, rows), :] = field[0][TILE : TILE + rows]
                field = tangent(field, half_u, half_v, rate)
            end_ref[var, level] = field[0][TILE : TILE + rows]
        return carry

    lax.fori_loop(0, levels, body, 0)
    groups = STEPS * comps * rows // 4
    for j in range(5):
        if j < 4:
            turned = traj_ref[pl.ds(j, groups, stride=4), :].T
            if j == 0:
                initial = turned
        else:
            turned = pltpu.roll(initial, groups - 1, 1)
        high = turned.astype(BF16)
        high_ref[j * LANES : (j + 1) * LANES, :] = high
        low_ref[j * LANES : (j + 1) * LANES, :] = (turned - high.astype(F32)).astype(BF16)


def chain_kernel(rate_ref, spot_ref, dealt_ref, south_ref, north_ref, east_ref, west_ref, out_ref, *, plan, lat_count, share):
    rows = dealt_ref.shape[2]
    comps = out_ref.shape[1]
    variables = comps // share
    tall = rows + 2 * TILE
    mask = row_mask(spot_ref[0], lat_count, rows, TILE)
    tall_mask = row_mask(spot_ref[0], lat_count, rows, 2 * TILE)
    tile = jnp.zeros((TILE, LANES), F32)

    def halo(slot, height, offset, width):
        span = slice(slot * tall, slot * tall + height)
        return unpack_columns(east_ref[span, :], west_ref[span, :], offset, width)

    def winds(window, wind):
        place = window * 2 * share + wind
        centre = taller(south_ref[plan.w + place], dealt_ref[window, comps + wind], north_ref[plan.w + place])
        return [0.5 * mask * centre, 0.5 * mask * halo(COL_TW, tall, 8 * place, 8)]

    for near in range(share):
        half_u = [winds(window, near) for window in range(3)]
        half_v = [winds(window, share + near) for window in range(3)]
        tall_u = [taller(tile, part, tile) for part in half_u[0]]
        tall_v = [taller(tile, part, tile) for part in half_v[0]]

        def body(var, carry, near=near, half_u=half_u, half_v=half_v, tall_u=tall_u, tall_v=tall_v):
            comp = var * share + near
            rate = rate_ref[var, spot_ref[1] * share + near]
            place = plan.t0 + 2 * comp
            south = jnp.concatenate([south_ref[place], south_ref[place + 1]], axis=0)
            north = jnp.concatenate([north_ref[place], north_ref[place + 1]], axis=0)
            out_ref[0, comp] = dealt_ref[0, comp]
            field = [
                taller(south, dealt_ref[0, comp], north) * tall_mask,
                halo(COL_T0, tall + 2 * TILE, 16 * comp, 9) * tall_mask,
            ]
            for step in range(STEPS):
                field = tangent(field, tall_u, tall_v, rate * tall_mask)
            field = [part[TILE : TILE + tall] for part in field]
            for window in (1, 2):
                start = plan.t1 if window == 1 else plan.t2
                centre = taller(south_ref[start + comp], dealt_ref[window, comp], north_ref[start + comp])
                beside = halo(
                    COL_T12, tall, 8 * (comp + (window - 1) * comps), 6 if window == 1 else 3
                )
                field = [field[0] + centre * mask, field[1] + beside * mask]
                out_ref[window, comp] = field[0][TILE : TILE + rows]
                for step in range(STEPS):
                    field = tangent(field, half_u[window], half_v[window], rate * mask)
            out_ref[3, comp] = field[0][TILE : TILE + rows] + dealt_ref[3, comp]
            return carry

        lax.fori_loop(0, variables, body, 0)


def force_columns_kernel(forcing_ref, south_ref, north_ref, west_ref, east_ref, *, rows):
    comps = south_ref.shape[0]
    tall = rows + 2 * TILE
    west = jnp.zeros((tall, LANES), F32)
    packed = (west, west)
    for comp in range(comps):
        south, north = south_ref[comp], north_ref[comp]
        late = (2 * comps + comp) * rows
        early = (comps + comp) * rows
        packed = pack_columns(packed, taller(south, forcing_ref[late : late + rows, :], north), 4 * comp, 2)
        packed = pack_columns(
            packed,
            taller(pltpu.roll(south, 2, 0), forcing_ref[early : early + rows, :], pltpu.roll(north, 6, 0)),
            4 * comp + 2,
            1,
        )
    west_ref[...] = packed[0]
    east_ref[...] = packed[1]


def adjoint_kernel(
    rate_ref, spot_ref, mult_ref, next_ref, u_ref, v_ref, south_ref, north_ref, east_ref, west_ref,
    forcing_ref, force_south_ref, force_north_ref, force_east_ref, force_west_ref, out_ref, *, plan, lat_count
):
    variables, levels, rows = next_ref.shape[:3]
    comps = variables * levels
    tall = rows + 2 * TILE
    mask = row_mask(spot_ref[0], lat_count, rows, TILE)

    def extended(centre, place, slot, offset):
        whole = taller(south_ref[place], centre, north_ref[place])
        span = slice(slot * tall, (slot + 1) * tall)
        return [whole * mask, unpack_columns(east_ref[span, :], west_ref[span, :], offset, 3) * mask]

    def forced(step, comp):
        start = pl.multiple_of((step * comps + comp) * rows, TILE)
        return forcing_ref[pl.ds(start, rows), :]

    def body(level, carry):
        half_u = [0.5 * w for w in extended(u_ref[level], plan.u + level, COL_WIND, 4 * level)]
        half_v = [0.5 * w for w in extended(v_ref[level], plan.v + level, COL_WIND, 4 * (levels + level))]
        for var in range(variables):
            comp = var * levels + level
            field = [-part for part in extended(next_ref[var, level], plan.mult + comp, COL_MULT, 4 * comp)]
            rate = mask * rate_ref[var, level]
            south, north = force_south_ref[comp], force_north_ref[comp]
            field = adjoint(field, half_u, half_v, rate)
            field = [
                field[0] + taller(south, forced(2, comp), north),
                field[1] + unpack_columns(force_east_ref[...], force_west_ref[...], 4 * comp, 2),
            ]
            field = adjoint(field, half_u, half_v, rate)
            field = [
                field[0] + taller(pltpu.roll(south, 2, 0), forced(1, comp), pltpu.roll(north, 6, 0)),
                field[1] + unpack_columns(force_east_ref[...], force_west_ref[...], 4 * comp + 2, 1),
            ]
            field = adjoint(field, half_u, half_v, rate)
            out_ref[var, level] = mult_ref[var, level] + (field[0][TILE : TILE + rows] + forced(0, comp))
        return carry

    lax.fori_loop(0, levels, body, 0)


def finish_kernel(x_ref, mult_ref, prior_ref, chain_ref, error_ref, model_ref, out_ref, *, share):
    variables, levels = x_ref.shape[:2]
    for var in range(variables):
        for level in range(levels):
            x = x_ref[var, level]
            model_ref[var, level] = mult_ref[var, level] * error_ref[var, level] + x - prior_ref[var, level]
            out_ref[var, level] = x + chain_ref[level // share, var * share + level % share]


def shards(
    increment, multiplier, u_wind, v_wind, diffusion, error_var, obs_owner, obs_cell, obs_layer, obs_weight, obs_dual, obs_error
):
    x, mult = increment[0], multiplier[0]
    u, v = u_wind[0], v_wind[0]
    variables, levels, rows, width = x.shape
    comps = variables * levels
    lat_count, windows = lax.axis_size("lat"), lax.axis_size("tm")
    blocks = lat_count * lax.axis_size("lon")
    share = levels // windows
    plan = RowPlan(variables, levels, share)
    count = obs_owner.shape[0]
    cap = 2 * count // blocks
    groups = STEPS * comps * rows // 4
    tall = rows + 2 * TILE
    place = jnp.stack([lax.axis_index("lat"), lax.axis_index("tm")]).astype(jnp.int32)

    dealt = call(
        functools.partial(deal_kernel, share=share),
        sds((windows, (variables + 2) * share, rows, width)),
        mult, u, v, error_var, smem=(3,), name="deal", flops=10**9,
    )
    dealt = lax.all_to_all(dealt, "tm", split_axis=0, concat_axis=0, tiled=True)
    mult_next = from_behind(mult, "tm", -1)

    owner_row = obs_owner.reshape(1, count)
    dual_row = obs_dual.reshape(1, count)
    send, rank = call(
        functools.partial(route_kernel, blocks=blocks, cap=cap, rows=rows, cols=width),
        (sds((4 * blocks, 2 * cap)), sds((1, count), jnp.int32)),
        owner_row, obs_cell.reshape(1, count), obs_layer.reshape(1, count), obs_weight.T, dual_row,
        name="route", flops=3 * 10**9,
        scratch=(pltpu.VMEM((2 * TILE, count), F32), pltpu.VMEM((4 * blocks, 2 * cap), F32)),
    )
    got = lax.all_to_all(send, ("lat", "lon"), split_axis=0, concat_axis=0, tiled=True)

    low, high = call(
        functools.partial(rows_kernel, plan=plan, share=share),
        (sds((plan.total, TILE, width)),) * 2,
        x, mult_next, u, v, dealt, name="rows", flops=10**9,
    )
    south = lax.ppermute(high, "lat", ring("lat", 1))
    north = lax.ppermute(low, "lat", ring("lat", -1))
    west_edge, east_edge = call(
        functools.partial(columns_kernel, plan=plan, share=share),
        (sds((6 * tall + 2 * TILE, width)),) * 2,
        x, mult_next, u, v, dealt, south, north, name="columns", flops=2 * 10**9,
    )
    west = lax.ppermute(east_edge, "lon", ring("lon", 1))
    east = lax.ppermute(west_edge, "lon", ring("lon", -1))

    slots = (4 * blocks // TILE, TILE, LANES)
    forcing, force_low, force_high = call(
        functools.partial(scatter_kernel, groups=groups, width=width, rows=rows),
        (sds((4 * groups, width)), sds((comps, TILE, width)), sds((comps, TILE, width))),
        got, name="scatter", flops=10**10,
        scratch=(
            pltpu.VMEM(slots, F32),
            pltpu.VMEM((groups, 5 * width), F32),
            pltpu.VMEM((2, 5 * width, min(4, slots[0]) * LANES), BF16),
        ),
    )
    force_south = lax.ppermute(force_high, "lat", ring("lat", 1))
    force_north = lax.ppermute(force_low, "lat", ring("lat", -1))

    traj_high, traj_low, end = call(
        functools.partial(forward_kernel, plan=plan, lat_count=lat_count),
        (sds((5 * width, groups), BF16), sds((5 * width, groups), BF16), sds(x.shape)),
        diffusion, place, x, u, v, south, north, east, west, smem=(0, 1), name="forward", flops=4 * 10**9,
        scratch=(pltpu.VMEM((4 * groups, width), F32),),
    )
    prior = from_behind(end, "tm", 1)
    chain = call(
        functools.partial(chain_kernel, plan=plan, lat_count=lat_count, share=share),
        sds((windows, variables * share, rows, width)),
        diffusion, place, dealt, south, north, east, west, smem=(0, 1), name="chain", flops=4 * 10**9,
    )
    chain = lax.all_to_all(chain, "tm", split_axis=0, concat_axis=0, tiled=True)

    force_west_edge, force_east_edge = call(
        functools.partial(force_columns_kernel, rows=rows),
        (sds((tall, width)),) * 2,
        forcing, force_south, force_north, name="force_columns", flops=10**9,
    )
    force_west = lax.ppermute(force_east_edge, "lon", ring("lon", 1))
    force_east = lax.ppermute(force_west_edge, "lon", ring("lon", -1))

    observed = call(
        functools.partial(gather_kernel, groups=groups, width=width),
        sds((blocks, LANES)),
        got, traj_high, traj_low, name="gather", flops=10**10,
        scratch=(pltpu.VMEM(slots, F32),),
    )
    back = lax.all_to_all(observed, ("lat", "lon"), split_axis=0, concat_axis=0, tiled=True)

    state_res = call(
        functools.partial(adjoint_kernel, plan=plan, lat_count=lat_count),
        sds(x.shape),
        diffusion, place, mult, mult_next, u, v, south, north, east, west,
        forcing, force_south, force_north, force_east, force_west,
        smem=(0, 1), name="adjoint", flops=4 * 10**9,
    )
    model_res, summed = call(
        functools.partial(finish_kernel, share=share),
        (sds(x.shape), sds(x.shape)),
        x, mult, prior, chain, error_var, smem=(4,), name="finish", flops=10**9,
    )
    obs_res = call(
        finish_obs_kernel, sds((1, count)),
        back, owner_row, rank, dual_row, obs_error.reshape(1, count), name="finish_obs", flops=10**9,
    )
    return (model_res[None], obs_res.reshape(count), state_res[None], summed[None])


def solution(mesh):
    fields = P("tm", None, None, "lat", "lon")
    winds = P("tm", None, "lat", "lon")
    everyone = ("tm", "lat", "lon")
    in_specs = (
        fields, fields, winds, winds, P(), P(),
        P(everyone, None), P(everyone), P(everyone), P(everyone, None), P(everyone), P(everyone),
    )
    out_specs = (fields, P(everyone), fields, fields)
    return jax.shard_map(shards, mesh=mesh, in_specs=in_specs, out_specs=out_specs, check_vma=False)
```

```python
import functools
import jax
import jax.numpy as jnp
from jax import lax
from jax.experimental import pallas as pl
from jax.experimental.pallas import tpu as pltpu
from jax.sharding import PartitionSpec as P

STEPS = 3
F32 = jnp.float32
BF16 = jnp.bfloat16
LANES = 128
TILE = 8


def ring(axis, by):
    count = lax.axis_size(axis)
    return [(i, (i + by) % count) for i in range(count)]


def from_behind(shard, axis, by):
    size = lax.axis_size(axis)
    pairs = [(i, i + by) for i in range(size) if 0 <= i + by < size]
    return lax.ppermute(shard, axis, pairs)


def call(kernel, out_shape, *args, name, flops=0, smem=(), scratch=(), vmem=16):
    specs = [
        pl.BlockSpec(memory_space=pltpu.SMEM if i in smem else pltpu.VMEM) for i in range(len(args))
    ]
    several = isinstance(out_shape, (tuple, list))
    out_specs = pl.BlockSpec(memory_space=pltpu.VMEM)
    return pl.pallas_call(
        kernel,
        out_shape=out_shape,
        in_specs=specs,
        out_specs=[out_specs] * len(out_shape) if several else out_specs,
        scratch_shapes=list(scratch),
        compiler_params=pltpu.CompilerParams(vmem_limit_bytes=vmem * 1024 * 1024),
        cost_estimate=pl.CostEstimate(flops=flops, bytes_accessed=0, transcendentals=0),
        name=name,
    )(*args)


def sds(shape, dtype=F32):
    return jax.ShapeDtypeStruct(shape, dtype)


def iota(shape, dim):
    return lax.broadcasted_iota(jnp.int32, shape, dim)


def split_two(value):
    high = value.astype(BF16).astype(F32)
    return high, value - high


def route_kernel(owner_ref, cell_ref, layer_ref, weight_ref, dual_ref, send_ref, rank_ref, fields_ref, acc_ref, *, blocks, cap, rows, cols):
    count = owner_ref.shape[1]
    chunk = min(256, count)
    cell = cell_ref[...]
    row = ((cell.astype(F32) + 0.5) * (1.0 / (cols - 1))).astype(jnp.int32)
    layer = layer_ref[...]
    key = (layer // TILE * rows + row) * TILE + layer % TILE
    col = cell - row * (cols - 1)
    for half in range(2):
        base = half * TILE
        fields_ref[base : base + 4, :] = weight_ref[...] if half == 0 else jnp.zeros((4, count), F32)
        if half == 1:
            fields_ref[base : base + 1, :] = dual_ref[...]
            fields_ref[base + 1 : base + 2, :] = key.astype(F32)
            fields_ref[base + 2 : base + 3, :] = col.astype(F32)
        fields_ref[base + 4 : base + 8, :] = fields_ref[base : base + 4, :]
    tri = (iota((chunk, chunk), 0) < iota((chunk, chunk), 1)).astype(F32)
    tri_ones = jnp.concatenate([tri, jnp.ones((chunk, LANES), F32)], axis=1).astype(BF16)
    running = jnp.zeros((blocks, 1), F32)
    acc_ref[...] = jnp.zeros_like(acc_ref)
    pair = 2 * iota((blocks // 2, TILE, chunk), 0) + iota((blocks // 2, TILE, chunk), 1) // 4
    for part in range(count // chunk):
        here = slice(part * chunk, (part + 1) * chunk)
        owner = owner_ref[:, here]
        hit = iota((blocks, chunk), 0) == owner
        hit_f = jnp.where(hit, 1.0, 0.0)
        counted = jnp.dot(hit_f.astype(BF16), tri_ones, preferred_element_type=F32)
        before = counted[:, :chunk] + running
        running = running + counted[:, chunk : chunk + 1]
        rank = jnp.sum(jnp.where(hit, before, 0.0), axis=0, keepdims=True).astype(jnp.int32)
        rank_ref[:, here] = rank
        ranks = iota((2 * cap, chunk), 0)
        right = jnp.concatenate(
            [jnp.where(ranks == rank, 1.0, 0.0), jnp.where(ranks == rank + cap, 1.0, 0.0)], axis=1
        ).astype(BF16)
        mine = pair == owner[None]
        highs, lows = [], []
        for half in range(2):
            high, low = split_two(fields_ref[half * TILE : (half + 1) * TILE, here])
            highs.append(jnp.where(mine, high[None], 0.0).reshape(4 * blocks, chunk).astype(BF16))
            lows.append(jnp.where(mine, low[None], 0.0).reshape(4 * blocks, chunk).astype(BF16))
        for left in (jnp.concatenate(highs, axis=1), jnp.concatenate(lows, axis=1)):
            acc_ref[...] += lax.dot_general(
                left, right, (((1,), (1,)), ((), ())), preferred_element_type=F32
            )
    send_ref[...] = acc_ref[...]


def unshuffle(got_ref, slots_ref):
    tiles = slots_ref.shape[0]
    keep = (iota((TILE, LANES), 0) < 4) == (iota((TILE, LANES), 1) < 64)
    for tile in range(tiles):
        value = got_ref[tile * TILE : (tile + 1) * TILE, :]
        other = pltpu.roll(pltpu.roll(value, 4, 0), 64, 1)
        slots_ref[tile] = jnp.where(keep, value, other)


def slot_rows(slots_ref, part, tiles_each):
    def field(num):
        return jnp.concatenate(
            [slots_ref[part * tiles_each + t, num : num + 1, :] for t in range(tiles_each)], axis=1
        )

    return field


def corner_rows(row4, tops, bottoms, j):
    zero = jnp.zeros_like(tops)
    return jnp.where(row4 == j, tops, jnp.where(row4 + 1 == j, bottoms, zero))


def slot_places(field, rows):
    key = field(5).astype(jnp.int32)
    line = key // TILE
    group = line // 4 * TILE + key % TILE
    return group, line % 4, field(6).astype(jnp.int32)


def scatter_kernel(got_ref, forcing_ref, low_ref, high_ref, slots_ref, acc_ref, *, groups, width, rows):
    unshuffle(got_ref, slots_ref)
    tiles = slots_ref.shape[0]
    tiles_each = min(4, tiles)
    chunk = tiles_each * LANES
    dims = (((1,), (1,)), ((), ()))
    for part in range(tiles // tiles_each):
        field = slot_rows(slots_ref, part, tiles_each)
        group, row4, col = slot_places(field, rows)
        dual = field(4)
        left = jnp.where(iota((groups, chunk), 0) == group, 1.0, 0.0).astype(BF16)
        cells = iota((width, chunk), 0)
        here, beside = cells == col, cells == col + 1
        corners = [field(num) * dual for num in range(4)]
        rights = [[], []]
        for j in range(5):
            first = split_two(corner_rows(row4, corners[0], corners[2], j))
            second = split_two(corner_rows(row4, corners[1], corners[3], j))
            for term in range(2):
                rights[term].append(
                    jnp.where(here, first[term], jnp.where(beside, second[term], 0.0)).astype(BF16)
                )
        added = lax.dot_general(
            left, jnp.concatenate(rights[0], axis=0), dims, preferred_element_type=F32
        ) + lax.dot_general(left, jnp.concatenate(rights[1], axis=0), dims, preferred_element_type=F32)
        if part == 0:
            acc_ref[...] = added
        else:
            acc_ref[...] += added
    fields = forcing_ref.shape[0] // rows
    per = rows // 4
    for place in range(fields):
        for four in range(per):
            start = (place * per + four) * TILE
            for j in range(4):
                value = acc_ref[start : start + TILE, j * width : (j + 1) * width]
                if j == 0 and four > 0:
                    value = value + acc_ref[start - TILE : start, 4 * width : 5 * width]
                forcing_ref[place * rows + four * 4 + j] = value
    variables = fields // STEPS
    for var in range(variables):
        late, early = (2 * variables + var) * rows, (variables + var) * rows
        low_ref[3 * var] = forcing_ref[late]
        low_ref[3 * var + 1] = forcing_ref[late + 1]
        low_ref[3 * var + 2] = forcing_ref[early]
        high_ref[3 * var] = forcing_ref[late + rows - 2]
        high_ref[3 * var + 1] = forcing_ref[late + rows - 1]
        high_ref[3 * var + 2] = forcing_ref[early + rows - 1]


def gather_kernel(got_ref, high_ref, low_ref, out_ref, slots_ref, *, groups, width, rows):
    unshuffle(got_ref, slots_ref)
    tiles = slots_ref.shape[0]
    tiles_each = min(4, tiles)
    chunk = tiles_each * LANES
    size = 2 * tiles_each
    for part in range(tiles // tiles_each):
        field = slot_rows(slots_ref, part, tiles_each)
        group, row4, col = slot_places(field, rows)
        right = jnp.where(iota((groups, chunk), 0) == group, 1.0, 0.0).astype(BF16)
        cells = iota((width, chunk), 0)
        here, beside = cells == col, cells == col + 1
        total = jnp.zeros((width, chunk), F32)
        for j in range(5):
            span = slice(j * width, (j + 1) * width)
            picked = jnp.dot(high_ref[span, :], right, preferred_element_type=F32) + jnp.dot(
                low_ref[span, :], right, preferred_element_type=F32
            )
            first = corner_rows(row4, field(0), field(2), j)
            second = corner_rows(row4, field(1), field(3), j)
            total = total + picked * jnp.where(here, first, jnp.where(beside, second, 0.0))
        value = jnp.sum(total, axis=0, keepdims=True)
        lines = []
        for t in range(tiles_each):
            line = value[:, t * LANES : (t + 1) * LANES]
            lines += [line, pltpu.roll(line, 64, 1)]
        out_ref[part * size : (part + 1) * size, :] = jnp.concatenate(lines, axis=0)


def finish_obs_kernel(back_ref, owner_ref, rank_ref, dual_ref, error_ref, out_ref):
    blocks = back_ref.shape[0]
    count = owner_ref.shape[1]
    chunk = min(512, count)
    turned = back_ref[...].T
    high, low = split_two(turned)
    high, low = high.astype(BF16), low.astype(BF16)
    for part in range(count // chunk):
        here = slice(part * chunk, (part + 1) * chunk)
        hit = jnp.where(iota((blocks, chunk), 0) == owner_ref[:, here], 1.0, 0.0).astype(BF16)
        picked = jnp.dot(high, hit, preferred_element_type=F32) + jnp.dot(
            low, hit, preferred_element_type=F32
        )
        wanted = iota((LANES, chunk), 0) == rank_ref[:, here]
        value = jnp.sum(jnp.where(wanted, picked, 0.0), axis=0, keepdims=True)
        out_ref[:, here] = error_ref[:, here] * dual_ref[:, here] + value


class Plan:
    def __init__(self, variables):
        own = [("x", var, 3) for var in range(variables)]
        own += [("next", var, 3) for var in range(variables)]
        own += [("u", 0, 3), ("v", 0, 3)]
        dealt = [("mult", 0, 9), ("mult", 1, 6), ("mult", 2, 3)]
        for window, wide in ((0, 8), (1, 5), (2, 2)):
            dealt += [("du", window, wide), ("dv", window, wide)]
        self.fields = {}
        tile = lane = 0
        for place, (name, num, wide) in enumerate(own + dealt):
            if place < len(own):
                source = ("own", place)
            elif name == "mult":
                source = ("dealt", num)
            else:
                source = ("dealt", 4 + 2 * num + (name == "dv"))
            self.fields[name, num] = (source, wide, tile, lane)
            tile += wide
            lane += wide
        self.tiles = tile
        self.own = len(own)
        self.deep = 9


def by_comp(shape, value_of):
    sub = iota(shape, 0)
    result = jnp.zeros(shape, F32)
    for comp in range(TILE):
        result = jnp.where(sub == comp, value_of(comp), result)
    return result


def sides(spot_ref, lat_count):
    lat = spot_ref[0]
    return jnp.where(lat > 0, 1.0, 0.0), jnp.where(lat < lat_count - 1, 1.0, 0.0)


def unpack(east, west, lane0, wide):
    lane = iota(east.shape, 2)
    from_east = pltpu.roll(east, (LANES - lane0) % LANES, 2)
    from_west = pltpu.roll(west, (LANES - lane0 - wide) % LANES, 2)
    return jnp.where(lane < wide, from_east, jnp.where(lane >= LANES - wide, from_west, 0.0))


def spans(rows, ring, edge_masks):
    result = []
    if ring:
        result.append((0, ring, edge_masks[0]))
    result += [(ring + start, 4, None) for start in range(0, rows, 4)]
    if ring:
        result.append((ring + rows, ring, edge_masks[1]))
    return result


def masked(value, mask):
    return value if mask is None else value * mask


def load_field(dst_ref, plan, name, num, refs, rows, edge_masks, scale=None):
    (kind, place), wide, tile, lane0 = plan.fields[name, num]
    source_ref = refs[kind]
    for start, size, mask in spans(rows, wide, edge_masks):
        if start < wide:
            centre = refs["south"][tile : tile + wide]
        elif start >= wide + rows:
            centre = refs["north"][tile : tile + wide]
        else:
            first = place * rows + start - wide
            centre = source_ref[first : first + size]
        at = plan.deep - wide + start
        beside = unpack(refs["east"][at : at + size], refs["west"][at : at + size], lane0, wide)
        for part, value in enumerate((centre, beside)):
            if scale is not None:
                value = value * scale
            dst_ref[part, start : start + size] = masked(value, mask)


def east_west(centre_e, halo_e, centre_w, halo_w):
    lane = iota(centre_e.shape, 2)
    ce, he = pltpu.roll(centre_e, LANES - 1, 2), pltpu.roll(halo_e, LANES - 1, 2)
    cw, hw = pltpu.roll(centre_w, 1, 2), pltpu.roll(halo_w, 1, 2)
    last, start = lane == LANES - 1, lane == 0
    east = (jnp.where(last, he, ce), jnp.where(last, ce, he))
    west = (jnp.where(start, hw, cw), jnp.where(start, cw, hw))
    return east, west


def tangent(src_ref, dst_ref, u_ref, v_ref, wind_ring, rate, rows, ring, edge_masks):
    parts = 1 if ring == 0 else 2
    for start, size, mask in spans(rows, ring, edge_masks):
        field = [src_ref[part, start : start + size + 2] for part in range(2)]
        middle = [part[1:-1] for part in field]
        east, west = east_west(*middle, *middle)
        wind = slice(wind_ring - ring + start, wind_ring - ring + start + size)
        for part in range(parts):
            north, south = field[part][2:], field[part][:-2]
            e, w, f = east[part], west[part], middle[part]
            value = (
                f
                + rate * ((e + w) + (north + south) - 4.0 * f)
                - u_ref[part, wind] * (e - w)
                - v_ref[part, wind] * (north - south)
            )
            dst_ref[part, start : start + size] = masked(value, mask)


def adjoint(src_ref, dst_ref, u_ref, v_ref, wind_ring, rate, rows, ring, edge_masks, add):
    parts = 1 if ring == 0 else 2
    for start, size, mask in spans(rows, ring, edge_masks):
        first = wind_ring - ring - 1 + start
        eastward, westward, result = [], [], []
        for part in range(2):
            field = src_ref[part, start : start + size + 2]
            thin = rate * field
            across = v_ref[part, first : first + size + 2] * field
            along = u_ref[part, first + 1 : first + 1 + size] * field[1:-1]
            eastward.append(thin[1:-1] + along)
            westward.append(thin[1:-1] - along)
            result.append(
                field[1:-1] - 4.0 * thin[1:-1] + (thin[2:] + across[2:]) + (thin[:-2] - across[:-2])
            )
        east, west = east_west(*eastward, *westward)
        extra = add(start, size)
        for part in range(parts):
            value = result[part] + (east[part] + west[part]) + extra[part]
            dst_ref[part, start : start + size] = masked(value, mask)


def deal_kernel(mult_ref, u_ref, v_ref, error_ref, spot_ref, *out_refs, rows, variables, levels):
    windows = len(out_refs)
    share = levels // windows
    for shift, out_ref in enumerate(out_refs):
        target = lax.rem(spot_ref[1] + shift, windows)
        for near in range(share):
            level = target * share + near
            for var in range(variables):
                start = pl.multiple_of((var * levels + level) * rows, TILE)
                value = mult_ref[pl.ds(start, rows), :] * error_ref[var, level]
                out_ref[pl.ds(near * variables + var, rows, stride=TILE), :] = value
            start = pl.multiple_of(level * rows, TILE)
            for num, ref in enumerate((u_ref, v_ref)):
                out_ref[pl.ds(rows * TILE + num * share + near, rows, stride=2 * share), :] = ref[
                    pl.ds(start, rows), :
                ]


def rows_kernel(
    spot_ref, x_ref, next_ref, u_ref, v_ref, *refs, plan, rows, variables, levels, windows
):
    dealt_refs, (own_ref, dealt_ref, low_ref, high_ref) = refs[:windows], refs[windows:]
    share = levels // windows
    has_next = jnp.where(spot_ref[1] < windows - 1, 1.0, 0.0)
    place = 0
    for ref, count in ((x_ref, variables), (next_ref, variables), (u_ref, 1), (v_ref, 1)):
        for num in range(count):
            for level in range(levels):
                value = ref[(num * levels + level) * rows : (num * levels + level + 1) * rows, :]
                if ref is next_ref:
                    value = value * has_next
                own_ref[pl.ds(place * rows * TILE + level, rows, stride=TILE), :] = value
            place += 1
    whole = rows * TILE
    sub = iota((TILE, LANES), 0)
    for shift, ref in enumerate(dealt_refs):
        window = lax.rem(spot_ref[1] - shift + windows, windows)
        start = pl.multiple_of(window * whole, TILE)
        dealt_ref[pl.ds(start, whole), :] = ref[:whole, :]
        start = (windows + 2 * window) * whole
        for row in range(rows):
            line = whole + row * 2 * share
            for num in range(2):
                near, far = ref[line + num * share : line + num * share + 1, :], ref[
                    line + num * share + share - 1 : line + num * share + share, :
                ]
                at = pl.multiple_of(start + num * whole + row * TILE, TILE)
                dealt_ref[pl.ds(at, TILE), :] = jnp.where(sub < TILE // share, near, far)
    for (kind, place), wide, tile, lane0 in plan.fields.values():
        ref = own_ref if kind == "own" else dealt_ref
        for num in range(wide):
            at = (place * rows + num) * TILE
            low_ref[tile + num] = ref[at : at + TILE, :]
            at = (place * rows + rows - wide + num) * TILE
            high_ref[tile + num] = ref[at : at + TILE, :]


def columns_kernel(own_ref, dealt_ref, south_ref, north_ref, west_ref, east_ref, *, plan, rows):
    deep = plan.deep
    for first in range(0, rows + 2 * deep, 2):
        size = 2
        west = jnp.zeros((size, TILE, LANES), F32)
        east = west
        lane = iota(west.shape, 2)
        for (kind, place), wide, tile, lane0 in plan.fields.values():
            tiles = []
            for row in range(first - deep, first - deep + size):
                if row < -wide or row >= rows + wide:
                    tiles.append(None)
                elif row < 0:
                    tiles.append(south_ref[tile + wide + row])
                elif row >= rows:
                    tiles.append(north_ref[tile + row - rows])
                else:
                    tiles.append((own_ref if kind == "own" else dealt_ref)[place * rows + row])
            if all(t is None for t in tiles):
                continue
            tiles = [jnp.zeros((TILE, LANES), F32) if t is None else t for t in tiles]
            field = jnp.stack(tiles)
            inside = (lane >= lane0) & (lane < lane0 + wide)
            west = jnp.where(inside, pltpu.roll(field, lane0, 2), west)
            east = jnp.where(inside, pltpu.roll(field, (lane0 + wide) % LANES, 2), east)
        west_ref[first : first + size] = west
        east_ref[first : first + size] = east


def forward_kernel(
    rate_ref, spot_ref, own_ref, south_ref, north_ref, east_ref, west_ref,
    high_ref, low_ref, end_ref, traj_ref, u_ref, v_ref, a_ref, b_ref, *, plan, lat_count, rows
):
    variables = end_ref.shape[0] // rows
    masks = sides(spot_ref, lat_count)
    refs = {"own": own_ref, "south": south_ref, "north": north_ref, "east": east_ref, "west": west_ref}
    load_field(u_ref, plan, "u", 0, refs, rows, masks, 0.5)
    load_field(v_ref, plan, "v", 0, refs, rows, masks, 0.5)
    for var in range(variables):
        rate = by_comp((TILE, LANES), lambda level: rate_ref[var, level])[None]
        load_field(a_ref.at[var], plan, "x", var, refs, rows, masks)
        here, there = a_ref.at[var], b_ref.at[var]
        for step in range(STEPS):
            ring = STEPS - 1 - step
            traj_ref[(step * variables + var) * rows : (step * variables + var + 1) * rows] = here[
                0, ring + 1 : ring + 1 + rows
            ]
            tangent(here, there, u_ref, v_ref, 3, rate, rows, ring, masks)
            here, there = there, here
        end_ref[var * rows : (var + 1) * rows] = here[0, 0:rows]
    groups = high_ref.shape[1]
    for j in range(5):
        if j < 4:
            tiles = [traj_ref[place * 4 + j] for place in range(groups // TILE)]
            turned = jnp.concatenate(tiles, axis=0).T
            if j == 0:
                initial = turned
        else:
            turned = pltpu.roll(initial, groups - TILE, 1)
        high = turned.astype(BF16)
        high_ref[j * LANES : (j + 1) * LANES, :] = high
        low_ref[j * LANES : (j + 1) * LANES, :] = (turned - high.astype(F32)).astype(BF16)


def chain_kernel(
    rate_ref, spot_ref, dealt_ref, south_ref, north_ref, east_ref, west_ref, *refs, plan, lat_count, rows, variables, windows
):
    out_refs, (u_ref, v_ref, a_ref, b_ref, m_ref, q_ref) = refs[:windows], refs[windows:]
    share = TILE // variables
    masks = sides(spot_ref, lat_count)
    rate = by_comp(
        (TILE, LANES), lambda comp: rate_ref[comp % variables, spot_ref[1] * share + comp // variables]
    )[None]
    refs = {"dealt": dealt_ref, "south": south_ref, "north": north_ref, "east": east_ref, "west": west_ref}
    load_field(a_ref, plan, "mult", 0, refs, rows, masks)
    here, there = a_ref, b_ref
    q_ref[0] = dealt_ref[0:rows]
    for window in range(windows - 1):
        ring = 3 * (windows - 1 - window)
        load_field(u_ref, plan, "du", window, refs, rows, masks, 0.5)
        load_field(v_ref, plan, "dv", window, refs, rows, masks, 0.5)
        wind_ring = ring - 1
        for step in range(STEPS):
            ring -= 1
            tangent(here, there, u_ref, v_ref, wind_ring, rate, rows, ring, masks)
            here, there = there, here
        if window + 1 < windows - 1:
            load_field(m_ref, plan, "mult", window + 1, refs, rows, masks)
            for start in range(0, rows + 2 * ring, 2):
                for part in range(2):
                    here[part, start : start + 2] = (
                        here[part, start : start + 2] + m_ref[part, start : start + 2]
                    )
            q_ref[window + 1] = here[0, ring : ring + rows]
        else:
            q_ref[window + 1] = here[0, 0:rows] + dealt_ref[(window + 1) * rows : (window + 2) * rows]
    for shift, out_ref in enumerate(out_refs):
        out_ref[...] = q_ref[lax.rem(spot_ref[1] + shift, windows)]


def force_columns_kernel(forcing_ref, south_ref, north_ref, west_ref, east_ref, *, rows):
    variables = south_ref.shape[0] // 3

    def tile_of(var, step, row):
        if row < 0:
            return south_ref[3 * var + (2 + row if step == 2 else 2)]
        if row >= rows:
            return north_ref[3 * var + (row - rows if step == 2 else 2)]
        return forcing_ref[(step * variables + var) * rows + row]

    for row in range(-2, rows + 2):
        west = jnp.zeros((TILE, LANES), F32)
        east = west
        lane = iota(west.shape, 1)
        for var in range(variables):
            for step, wide, lane0 in ((2, 2, 4 * var), (1, 1, 4 * var + 2)):
                if row < -wide or row >= rows + wide:
                    continue
                field = tile_of(var, step, row)
                inside = (lane >= lane0) & (lane < lane0 + wide)
                west = jnp.where(inside, pltpu.roll(field, lane0, 1), west)
                east = jnp.where(inside, pltpu.roll(field, (lane0 + wide) % LANES, 1), east)
        west_ref[row + 2] = west
        east_ref[row + 2] = east


def adjoint_kernel(
    rate_ref, spot_ref, mult_ref, own_ref, south_ref, north_ref, east_ref, west_ref,
    forcing_ref, force_south_ref, force_north_ref, force_east_ref, force_west_ref, out_ref,
    u_ref, v_ref, a_ref, b_ref, *, plan, lat_count, rows, levels
):
    variables = force_south_ref.shape[0] // 3
    masks = sides(spot_ref, lat_count)
    refs = {"own": own_ref, "south": south_ref, "north": north_ref, "east": east_ref, "west": west_ref}
    load_field(u_ref, plan, "u", 0, refs, rows, masks, 0.5)
    load_field(v_ref, plan, "v", 0, refs, rows, masks, 0.5)
    for var in range(variables):
        rate = by_comp((TILE, LANES), lambda level: rate_ref[var, level])[None]
        here, there = a_ref.at[var], b_ref.at[var]
        load_field(here, plan, "next", var, refs, rows, masks, -1.0)
        for step in (2, 1, 0):

            def add(start, size, step=step, var=var):
                base = (step * variables + var) * rows
                if step == 0:
                    return (forcing_ref[base + start : base + start + size],)
                if start < step:
                    first = 3 * var + (0 if step == 2 else 2)
                    centre = force_south_ref[first : first + size]
                elif start >= step + rows:
                    first = 3 * var + (0 if step == 2 else 2)
                    centre = force_north_ref[first : first + size]
                else:
                    centre = forcing_ref[base + start - step : base + start - step + size]
                at = 2 - step + start
                beside = unpack(
                    force_east_ref[at : at + size], force_west_ref[at : at + size],
                    4 * var + (0 if step == 2 else 2), step,
                )
                return centre, beside

            adjoint(here, there, u_ref, v_ref, 3, rate, rows, step, masks, add)
            here, there = there, here
        for row in range(rows):
            span = pl.ds(var * levels * rows + row, levels, stride=rows)
            out_ref[span, :] = mult_ref[span, :] + here[0, row]


def finish_kernel(x_ref, mult_ref, prior_ref, error_ref, spot_ref, *refs, rows, variables, levels):
    chain_refs, (model_ref, out_ref) = refs[:-2], refs[-2:]
    windows = len(chain_refs)
    share = levels // windows
    has_prior = jnp.where(spot_ref[1] > 0, 1.0, 0.0)
    for var in range(variables):
        for level in range(levels):
            span = slice((var * levels + level) * rows, (var * levels + level + 1) * rows)
            prior = prior_ref[pl.ds(var * rows * TILE + level, rows, stride=TILE), :]
            model_ref[span, :] = mult_ref[span, :] * error_ref[var, level] + x_ref[span, :] - has_prior * prior
    for shift, ref in enumerate(chain_refs):
        source = lax.rem(spot_ref[1] - shift + windows, windows)
        for near in range(share):
            for var in range(variables):
                start = pl.multiple_of((var * levels + source * share + near) * rows, TILE)
                out_ref[pl.ds(start, rows), :] = (
                    x_ref[pl.ds(start, rows), :] + ref[pl.ds(near * variables + var, rows, stride=TILE), :]
                )


def shards(
    increment, multiplier, u_wind, v_wind, diffusion, error_var, obs_owner, obs_cell, obs_layer, obs_weight, obs_dual, obs_error
):
    variables, levels, rows, width = increment.shape[1:]
    flat = (variables * levels * rows, width)
    x, mult = increment.reshape(flat), multiplier.reshape(flat)
    u, v = u_wind.reshape(levels * rows, width), v_wind.reshape(levels * rows, width)
    lat_count, windows = lax.axis_size("lat"), lax.axis_size("tm")
    blocks = lat_count * lax.axis_size("lon")
    plan = Plan(variables)
    count = obs_owner.shape[0]
    cap = 2 * count // blocks
    groups = STEPS * variables * levels * rows // 4
    spot = jnp.stack([lax.axis_index("lat"), lax.axis_index("tm")]).astype(jnp.int32)

    def planes(ring):
        return pltpu.VMEM((2, rows + 2 * ring, TILE, LANES), F32)

    def tiles(array):
        return array.reshape(array.shape[0] // TILE, TILE, width)

    def lines(array):
        return array.reshape(array.shape[0] * TILE, width)

    owner_row = obs_owner.reshape(1, count)
    dual_row = obs_dual.reshape(1, count)
    send, rank = call(
        functools.partial(route_kernel, blocks=blocks, cap=cap, rows=rows, cols=width),
        (sds((4 * blocks, 2 * cap)), sds((1, count), jnp.int32)),
        owner_row, obs_cell.reshape(1, count), obs_layer.reshape(1, count), obs_weight.T, dual_row,
        name="route", flops=3 * 10**9,
        scratch=(pltpu.VMEM((2 * TILE, count), F32), pltpu.VMEM((4 * blocks, 2 * cap), F32)),
    )
    got = lax.all_to_all(send, ("lat", "lon"), split_axis=0, concat_axis=0, tiled=True)

    dealt = call(
        functools.partial(deal_kernel, rows=rows, variables=variables, levels=levels),
        (sds((rows * (TILE + 2 * levels // windows), width)),) * windows,
        mult, u, v, error_var, spot, smem=(3, 4), name="deal", flops=10**9,
    )
    dealt = [lax.ppermute(part, "tm", ring("tm", shift)) if shift else part for shift, part in enumerate(dealt)]
    mult_next = lax.ppermute(mult, "tm", ring("tm", -1))

    own, dealt, low, high = call(
        functools.partial(rows_kernel, plan=plan, rows=rows, variables=variables, levels=levels, windows=windows),
        (
            sds((plan.own * rows * TILE, width)), sds((3 * windows * rows * TILE, width)),
            sds((plan.tiles, TILE, width)), sds((plan.tiles, TILE, width)),
        ),
        spot, x, mult_next, u, v, *dealt, smem=(0,), name="rows", flops=10**9,
    )
    own, dealt = tiles(own), tiles(dealt)
    south = lax.ppermute(high, "lat", ring("lat", 1))
    north = lax.ppermute(low, "lat", ring("lat", -1))
    west_edge, east_edge = call(
        functools.partial(columns_kernel, plan=plan, rows=rows),
        (sds((rows + 2 * plan.deep, TILE, width)),) * 2,
        own, dealt, south, north, name="columns", flops=2 * 10**9,
    )
    west = lax.ppermute(east_edge, "lon", ring("lon", 1))
    east = lax.ppermute(west_edge, "lon", ring("lon", -1))

    slots = pltpu.VMEM((4 * blocks // TILE, TILE, LANES), F32)
    force_edges = sds((3 * variables, TILE, width))
    forcing, force_low, force_high = call(
        functools.partial(scatter_kernel, groups=groups, width=width, rows=rows),
        (sds((4 * groups // TILE, TILE, width)), force_edges, force_edges),
        got, name="scatter", flops=10**10,
        scratch=(slots, pltpu.VMEM((groups, 5 * width), F32)),
    )
    force_south = lax.ppermute(force_high, "lat", ring("lat", 1))
    force_north = lax.ppermute(force_low, "lat", ring("lat", -1))

    stage = pltpu.VMEM((variables, 2, rows + 6, TILE, LANES), F32)
    traj_high, traj_low, end = call(
        functools.partial(forward_kernel, plan=plan, lat_count=lat_count, rows=rows),
        (sds((5 * width, groups), BF16), sds((5 * width, groups), BF16), sds((variables * rows, TILE, width))),
        diffusion, spot, own, south, north, east, west, smem=(0, 1), name="forward", flops=3 * 10**9,
        scratch=(pltpu.VMEM((4 * groups // TILE, TILE, width), F32), planes(3), planes(3), stage, stage),
    )
    prior = lax.ppermute(lines(end), "tm", ring("tm", 1))
    chain = call(
        functools.partial(
            chain_kernel, plan=plan, lat_count=lat_count, rows=rows, variables=variables, windows=windows
        ),
        (sds((rows, TILE, width)),) * windows,
        diffusion, spot, dealt, south, north, east, west, smem=(0, 1), name="chain", flops=3 * 10**9,
        scratch=(planes(8), planes(8), planes(9), planes(9), planes(6), pltpu.VMEM((windows, rows, TILE, LANES), F32)),
    )
    chain = [
        lax.ppermute(lines(part), "tm", ring("tm", shift)) if shift else lines(part)
        for shift, part in enumerate(chain)
    ]

    force_west_edge, force_east_edge = call(
        functools.partial(force_columns_kernel, rows=rows),
        (sds((rows + 4, TILE, width)),) * 2,
        forcing, force_south, force_north, name="force_columns", flops=10**9,
    )
    force_west = lax.ppermute(force_east_edge, "lon", ring("lon", 1))
    force_east = lax.ppermute(force_west_edge, "lon", ring("lon", -1))

    observed = call(
        functools.partial(gather_kernel, groups=groups, width=width, rows=rows),
        sds((blocks, LANES)),
        got, traj_high, traj_low, name="gather", flops=10**10,
        scratch=(slots,),
    )
    back = lax.all_to_all(observed, ("lat", "lon"), split_axis=0, concat_axis=0, tiled=True)

    state_res = call(
        functools.partial(adjoint_kernel, plan=plan, lat_count=lat_count, rows=rows, levels=levels),
        sds(flat),
        diffusion, spot, mult, own, south, north, east, west,
        forcing, force_south, force_north, force_east, force_west,
        smem=(0, 1), name="adjoint", flops=3 * 10**9,
        scratch=(planes(3), planes(3), stage, stage),
    )
    model_res, summed = call(
        functools.partial(finish_kernel, rows=rows, variables=variables, levels=levels),
        (sds(flat), sds(flat)),
        x, mult, prior, error_var, spot, *chain, smem=(3, 4), name="finish", flops=10**9,
    )
    obs_res = call(
        finish_obs_kernel, sds((1, count)),
        back, owner_row, rank, dual_row, obs_error.reshape(1, count), name="finish_obs", flops=10**9,
    )
    whole = increment.shape
    return (model_res.reshape(whole), obs_res.reshape(count), state_res.reshape(whole), summed.reshape(whole))


def solution(mesh):
    fields = P("tm", None, None, "lat", "lon")
    winds = P("tm", None, "lat", "lon")
    everyone = ("tm", "lat", "lon")
    in_specs = (
        fields, fields, winds, winds, P(), P(),
        P(everyone, None), P(everyone), P(everyone), P(everyone, None), P(everyone), P(everyone),
    )
    out_specs = (fields, P(everyone), fields, fields)
    return jax.shard_map(shards, mesh=mesh, in_specs=in_specs, out_specs=out_specs, check_vma=False)
```

```python
import functools
import jax
import jax.numpy as jnp
from jax import lax
from jax.experimental import pallas as pl
from jax.experimental.pallas import tpu as pltpu
from jax.sharding import PartitionSpec as P

STEPS = 3
F32 = jnp.float32
BF16 = jnp.bfloat16
LANES = 128
TILE = 8

COST = {
    "entry": 6 * 10**9, "columns": 10**9, "scatter": 5 * 10**9, "rows": 2 * 10**9, "forward": 4 * 10**9,
    "gather": 5 * 10**9, "chain": 4 * 10**9, "final": 6 * 10**9, "finish_obs": 10**9,
}


def ring(axis, by):
    count = lax.axis_size(axis)
    return [(i, (i + by) % count) for i in range(count)]


def from_behind(shard, axis, by):
    size = lax.axis_size(axis)
    pairs = [(i, i + by) for i in range(size) if 0 <= i + by < size]
    return lax.ppermute(shard, axis, pairs)


def call(kernel, out_shape, *args, name, flops=0, smem=(), hbm=(), loose=(), hbm_outs=(), scratch=(), vmem=16):
    def spec(num, far, free=()):
        space = pltpu.HBM if num in far else pl.ANY if num in free else pltpu.VMEM
        return pl.BlockSpec(memory_space=space)

    specs = [
        pl.BlockSpec(memory_space=pltpu.SMEM) if i in smem else spec(i, hbm, loose) for i in range(len(args))
    ]
    several = isinstance(out_shape, (tuple, list))
    return pl.pallas_call(
        kernel,
        out_shape=out_shape,
        in_specs=specs,
        out_specs=[spec(i, hbm_outs) for i in range(len(out_shape))] if several else spec(0, hbm_outs),
        scratch_shapes=list(scratch),
        compiler_params=pltpu.CompilerParams(vmem_limit_bytes=vmem * 1024 * 1024),
        cost_estimate=pl.CostEstimate(flops=flops, bytes_accessed=0, transcendentals=0),
        name=name,
    )(*args)


def sds(shape, dtype=F32):
    return jax.ShapeDtypeStruct(shape, dtype)


def iota(shape, dim):
    return lax.broadcasted_iota(jnp.int32, shape, dim)


def split_two(value):
    high = value.astype(BF16).astype(F32)
    return high, value - high


def route(owner_ref, cell_ref, layer_ref, weight_ref, dual_ref, send_ref, rank_ref, fields_ref, acc_ref, blocks, cap, rows, cols):
    count = owner_ref.shape[1]
    chunk = min(256, count)
    cell = cell_ref[...]
    row = ((cell.astype(F32) + 0.5) * (1.0 / (cols - 1))).astype(jnp.int32)
    layer = layer_ref[...]
    key = (layer // TILE * rows + row) * TILE + layer % TILE
    col = cell - row * (cols - 1)
    for half in range(2):
        base = half * TILE
        fields_ref[base : base + 4, :] = weight_ref[...] if half == 0 else jnp.zeros((4, count), F32)
        if half == 1:
            fields_ref[base : base + 1, :] = dual_ref[...]
            fields_ref[base + 1 : base + 2, :] = key.astype(F32)
            fields_ref[base + 2 : base + 3, :] = col.astype(F32)
        fields_ref[base + 4 : base + 8, :] = fields_ref[base : base + 4, :]
    tri = (iota((chunk, chunk), 0) < iota((chunk, chunk), 1)).astype(F32)
    tri_ones = jnp.concatenate([tri, jnp.ones((chunk, LANES), F32)], axis=1).astype(BF16)
    running = jnp.zeros((blocks, 1), F32)
    acc_ref[...] = jnp.zeros_like(acc_ref)
    pair = 2 * iota((blocks // 2, TILE, chunk), 0) + iota((blocks // 2, TILE, chunk), 1) // 4
    for part in range(count // chunk):
        here = slice(part * chunk, (part + 1) * chunk)
        owner = owner_ref[:, here]
        hit = iota((blocks, chunk), 0) == owner
        hit_f = jnp.where(hit, 1.0, 0.0)
        counted = jnp.dot(hit_f.astype(BF16), tri_ones, preferred_element_type=F32)
        before = counted[:, :chunk] + running
        running = running + counted[:, chunk : chunk + 1]
        rank = jnp.sum(jnp.where(hit, before, 0.0), axis=0, keepdims=True).astype(jnp.int32)
        rank_ref[0:1, here] = rank
        rank_ref[1:2, here] = owner
        ranks = iota((2 * cap, chunk), 0)
        right = jnp.concatenate(
            [jnp.where(ranks == rank, 1.0, 0.0), jnp.where(ranks == rank + cap, 1.0, 0.0)], axis=1
        ).astype(BF16)
        mine = pair == owner[None]
        highs, lows = [], []
        for half in range(2):
            high, low = split_two(fields_ref[half * TILE : (half + 1) * TILE, here])
            highs.append(jnp.where(mine, high[None], 0.0).reshape(4 * blocks, chunk).astype(BF16))
            lows.append(jnp.where(mine, low[None], 0.0).reshape(4 * blocks, chunk).astype(BF16))
        for left in (jnp.concatenate(highs, axis=1), jnp.concatenate(lows, axis=1)):
            acc_ref[...] += lax.dot_general(
                left, right, (((1,), (1,)), ((), ())), preferred_element_type=F32
            )
    send_ref[...] = acc_ref[...]


def unshuffle(got_ref, slots_ref):
    tiles = slots_ref.shape[0]
    keep = (iota((TILE, LANES), 0) < 4) == (iota((TILE, LANES), 1) < 64)
    for tile in range(tiles):
        value = got_ref[tile * TILE : (tile + 1) * TILE, :]
        other = pltpu.roll(pltpu.roll(value, 4, 0), 64, 1)
        slots_ref[tile] = jnp.where(keep, value, other)


def slot_rows(slots_ref, part, tiles_each):
    def field(num):
        return jnp.concatenate(
            [slots_ref[part * tiles_each + t, num : num + 1, :] for t in range(tiles_each)], axis=1
        )

    return field


def corner_rows(row4, tops, bottoms, j):
    zero = jnp.zeros_like(tops)
    return jnp.where(row4 == j, tops, jnp.where(row4 + 1 == j, bottoms, zero))


def slot_places(field, rows):
    key = field(5).astype(jnp.int32)
    line = key // TILE
    group = line // 4 * TILE + key % TILE
    return group, line % 4, field(6).astype(jnp.int32)


def scatter_kernel(got_ref, forcing_ref, slots_ref, acc_ref, *, groups, width, rows):
    unshuffle(got_ref, slots_ref)
    tiles = slots_ref.shape[0]
    tiles_each = min(4, tiles)
    chunk = tiles_each * LANES
    dims = (((1,), (1,)), ((), ()))
    for part in range(tiles // tiles_each):
        field = slot_rows(slots_ref, part, tiles_each)
        group, row4, col = slot_places(field, rows)
        dual = field(4)
        left = jnp.where(iota((groups, chunk), 0) == group, 1.0, 0.0).astype(BF16)
        cells = iota((width, chunk), 0)
        here, beside = cells == col, cells == col + 1
        corners = [field(num) * dual for num in range(4)]
        rights = [[], []]
        for j in range(5):
            first = split_two(corner_rows(row4, corners[0], corners[2], j))
            second = split_two(corner_rows(row4, corners[1], corners[3], j))
            for term in range(2):
                rights[term].append(
                    jnp.where(here, first[term], jnp.where(beside, second[term], 0.0)).astype(BF16)
                )
        added = lax.dot_general(
            left, jnp.concatenate(rights[0] + rights[1], axis=0), dims, preferred_element_type=F32
        )
        if part == 0:
            acc_ref[...] = added
        else:
            acc_ref[...] += added
    fields = forcing_ref.shape[0] // rows
    per = rows // 4

    def term_sum(start, j):
        span = slice(start, start + TILE)
        return acc_ref[span, j * width : (j + 1) * width] + acc_ref[span, (j + 5) * width : (j + 6) * width]

    for place in range(fields):
        for four in range(per):
            start = (place * per + four) * TILE
            for j in range(4):
                value = term_sum(start, j)
                if j == 0 and four > 0:
                    value = value + term_sum(start - TILE, 4)
                forcing_ref[place * rows + four * 4 + j] = value


def gather_kernel(got_ref, traj_ref, earlier_ref, unused_ref, out_ref, slots_ref, picked_ref, *, groups, width, rows, half):
    unshuffle(got_ref, slots_ref)
    tiles = slots_ref.shape[0]
    tiles_each = min(4, tiles // 2)
    chunk = tiles_each * LANES
    size = 2 * tiles_each
    if half == 1:
        out_ref[:tiles, :] = earlier_ref[...]
    parts = tiles // tiles_each // 2
    for part in range(half * parts, (half + 1) * parts):
        field = slot_rows(slots_ref, part, tiles_each)
        group, row4, col = slot_places(field, rows)
        right = jnp.where(iota((groups, chunk), 0) == group, 1.0, 0.0).astype(BF16)
        cells = iota((width, chunk), 0)
        here, beside = cells == col, cells == col + 1
        total = jnp.zeros((width, chunk), F32)
        picked_ref[part % 2] = jnp.dot(traj_ref[...], right, preferred_element_type=F32)
        for j in range(5):
            picked = (
                picked_ref[part % 2, j * width : (j + 1) * width]
                + picked_ref[part % 2, (j + 5) * width : (j + 6) * width]
            )
            first = corner_rows(row4, field(0), field(2), j)
            second = corner_rows(row4, field(1), field(3), j)
            total = total + picked * jnp.where(here, first, jnp.where(beside, second, 0.0))
        value = jnp.sum(total, axis=0, keepdims=True)
        lines = []
        for t in range(tiles_each):
            line = value[:, t * LANES : (t + 1) * LANES]
            lines += [line, pltpu.roll(line, 64, 1)]
        out_ref[part * size : (part + 1) * size, :] = jnp.concatenate(lines, axis=0)


def finish_obs_kernel(back_ref, rank_ref, base_ref, out_ref):
    blocks = back_ref.shape[0]
    count = base_ref.shape[1]
    chunk = min(512, count)
    high, low = split_two(back_ref[...].T)
    high, low = high.astype(BF16), low.astype(BF16)
    for part in range(count // chunk):
        here = slice(part * chunk, (part + 1) * chunk)
        hit = jnp.where(iota((blocks, chunk), 0) == rank_ref[1:2, here], 1.0, 0.0).astype(BF16)
        picked = jnp.dot(high, hit, preferred_element_type=F32) + jnp.dot(
            low, hit, preferred_element_type=F32
        )
        wanted = iota((LANES, chunk), 0) == rank_ref[0:1, here]
        value = jnp.sum(jnp.where(wanted, picked, 0.0), axis=0, keepdims=True)
        out_ref[:, here] = base_ref[:, here] + value


class Plan:
    def __init__(self, fields):
        self.fields = {}
        tile = 0
        for name, num, source, wide in fields:
            self.fields[name, num] = (source, wide, tile, tile)
            tile += wide
        self.tiles = tile
        self.deep = max(wide for name, num, source, wide in fields)


def own_plan(variables):
    fields = [("x", var, ("own", var), 3) for var in range(variables)]
    fields += [("u", 0, ("own", variables), 3), ("v", 0, ("own", variables + 1), 3)]
    return Plan(fields)


def later_plan(variables, windows):
    fields = [("next", var, ("next", var), 3) for var in range(variables)]
    for window, wide in ((0, 9), (1, 6), (2, 3)):
        fields.append(("mult", window, ("dealt", window), wide))
    for window, wide in ((0, 8), (1, 5), (2, 2)):
        fields.append(("du", window, ("dealt", windows + 2 * window), wide))
        fields.append(("dv", window, ("dealt", windows + 2 * window + 1), wide))
    for step in (2, 1):
        for var in range(variables):
            fields.append((("force", step), var, ("forcing", step * variables + var), step))
    return Plan(fields)


def by_comp(shape, value_of):
    sub = iota(shape, 0)
    result = jnp.zeros(shape, F32)
    for comp in range(TILE):
        result = jnp.where(sub == comp, value_of(comp), result)
    return result


def sides(spot_ref, lat_count):
    lat = spot_ref[0]
    return jnp.where(lat > 0, 1.0, 0.0), jnp.where(lat < lat_count - 1, 1.0, 0.0)


def unpack(east, west, lane0, wide):
    lane = iota(east.shape, 2)
    from_east = pltpu.roll(east, (LANES - lane0) % LANES, 2)
    from_west = pltpu.roll(west, (LANES - lane0 - wide) % LANES, 2)
    return jnp.where(lane < wide, from_east, jnp.where(lane >= LANES - wide, from_west, 0.0))


def spans(rows, ring, edge_masks):
    result = []
    if ring:
        result.append((0, ring, edge_masks[0]))
    result += [(ring + start, 4, None) for start in range(0, rows, 4)]
    if ring:
        result.append((ring + rows, ring, edge_masks[1]))
    return result


def masked(value, mask):
    return value if mask is None else value * mask


def load_field(dst_ref, plan, name, num, refs, rows, edge_masks, scale=None):
    (kind, place), wide, tile, lane0 = plan.fields[name, num]
    source_ref = refs[kind]
    for start, size, mask in spans(rows, wide, edge_masks):
        if start < wide:
            centre = refs["south"][tile : tile + wide]
        elif start >= wide + rows:
            centre = refs["north"][tile : tile + wide]
        else:
            first = place * rows + start - wide
            centre = source_ref[first : first + size]
        at = plan.deep - wide + start
        beside = unpack(refs["east"][at : at + size], refs["west"][at : at + size], lane0, wide)
        for part, value in enumerate((centre, beside)):
            if scale is not None:
                value = value * scale
            dst_ref[part, start : start + size] = masked(value, mask)


def east_west(centre_e, halo_e, centre_w, halo_w):
    lane = iota(centre_e.shape, 2)
    ce, he = pltpu.roll(centre_e, LANES - 1, 2), pltpu.roll(halo_e, LANES - 1, 2)
    cw, hw = pltpu.roll(centre_w, 1, 2), pltpu.roll(halo_w, 1, 2)
    last, start = lane == LANES - 1, lane == 0
    east = (jnp.where(last, he, ce), jnp.where(last, ce, he))
    west = (jnp.where(start, hw, cw), jnp.where(start, cw, hw))
    return east, west


def tangent(src_ref, dst_ref, u_ref, v_ref, wind_ring, rate, rows, ring, edge_masks):
    parts = 1 if ring == 0 else 2
    for start, size, mask in spans(rows, ring, edge_masks):
        field = [src_ref[part, start : start + size + 2] for part in range(2)]
        middle = [part[1:-1] for part in field]
        east, west = east_west(*middle, *middle)
        wind = slice(wind_ring - ring + start, wind_ring - ring + start + size)
        for part in range(parts):
            north, south = field[part][2:], field[part][:-2]
            e, w, f = east[part], west[part], middle[part]
            value = (
                f
                + rate * ((e + w) + (north + south) - 4.0 * f)
                - u_ref[part, wind] * (e - w)
                - v_ref[part, wind] * (north - south)
            )
            dst_ref[part, start : start + size] = masked(value, mask)


def adjoint(src_ref, dst_ref, u_ref, v_ref, wind_ring, rate, rows, ring, edge_masks, add):
    parts = 1 if ring == 0 else 2
    for start, size, mask in spans(rows, ring, edge_masks):
        first = wind_ring - ring - 1 + start
        eastward, westward, result = [], [], []
        for part in range(2):
            field = src_ref[part, start : start + size + 2]
            thin = rate * field
            across = v_ref[part, first : first + size + 2] * field
            along = u_ref[part, first + 1 : first + 1 + size] * field[1:-1]
            eastward.append(thin[1:-1] + along)
            westward.append(thin[1:-1] - along)
            result.append(
                field[1:-1] - 4.0 * thin[1:-1] + (thin[2:] + across[2:]) + (thin[:-2] - across[:-2])
            )
        east, west = east_west(*eastward, *westward)
        extra = add(start, size)
        for part in range(parts):
            value = result[part] + (east[part] + west[part]) + extra[part]
            dst_ref[part, start : start + size] = masked(value, mask)


def edges(plan, sources, rows, low_ref, high_ref, west_ref, east_ref):
    def tile_at(kind, place, row):
        at = (place * rows + row) * TILE
        return sources[kind][at : at + TILE, :]

    for (kind, place), wide, tile, lane0 in plan.fields.values():
        for num in range(wide):
            low_ref[tile + num] = tile_at(kind, place, num)
            high_ref[tile + num] = tile_at(kind, place, rows - wide + num)
    for row in range(rows):
        packed = None
        for (kind, place), wide, tile, lane0 in plan.fields.values():
            packed = pack(packed, tile_at(kind, place, row), lane0, wide)
        west_ref[row], east_ref[row] = packed


def entry_kernel(
    error_ref, spot_ref, owner_hbm, cell_hbm, layer_hbm, weight_hbm, dual_hbm, noise_hbm, mult_hbm, u_hbm, v_hbm, x_hbm,
    send_ref, rank_ref, base_ref, own_ref, low_ref, high_ref, west_ref, east_ref, *refs,
    plan, rows, variables, levels, windows, blocks, cap
):
    part_refs, refs = refs[:windows], refs[windows:]
    (owner_ref, cell_ref, layer_ref, weight_ref, dual_ref, noise_ref, mult_ref, u_ref, v_ref, x_ref) = refs[:10]
    fields_ref, acc_ref, sems = refs[10:]
    pairs = (
        (owner_hbm, owner_ref), (cell_hbm, cell_ref), (layer_hbm, layer_ref), (weight_hbm, weight_ref),
        (dual_hbm, dual_ref), (noise_hbm, noise_ref), (mult_hbm, mult_ref), (u_hbm, u_ref), (v_hbm, v_ref),
        (x_hbm, x_ref),
    )
    copies = [pltpu.make_async_copy(src, dst, sems.at[num]) for num, (src, dst) in enumerate(pairs)]
    for copy in copies:
        copy.start()
    for copy in copies[:6]:
        copy.wait()
    width = mult_ref.shape[1]
    base_ref[...] = noise_ref[...] * dual_ref[...]
    route(
        owner_ref, cell_ref, layer_ref, weight_ref, dual_ref, send_ref, rank_ref, fields_ref, acc_ref,
        blocks, cap, rows, width,
    )
    for copy in copies[6:]:
        copy.wait()
    share = levels // windows
    for shift, part_ref in enumerate(part_refs):
        target = lax.rem(spot_ref[1] + shift, windows)
        whole = shift == windows - 1
        first = variables * levels * rows if whole else rows * TILE
        if whole:
            part_ref[:first, :] = mult_ref[...]
        for near in range(share):
            level = target * share + near
            for var in range(0 if whole else variables):
                start = pl.multiple_of((var * levels + level) * rows, TILE)
                value = mult_ref[pl.ds(start, rows), :] * error_ref[var, level]
                part_ref[pl.ds(near * variables + var, rows, stride=TILE), :] = value
            start = pl.multiple_of(level * rows, TILE)
            for num, ref in enumerate((u_ref, v_ref)):
                part_ref[pl.ds(first + num * share + near, rows, stride=2 * share), :] = ref[
                    pl.ds(start, rows), :
                ]
    place = 0
    for ref, count in ((x_ref, variables), (u_ref, 1), (v_ref, 1)):
        for num in range(count):
            for level in range(levels):
                value = ref[(num * levels + level) * rows : (num * levels + level + 1) * rows, :]
                own_ref[pl.ds(place * rows * TILE + level, rows, stride=TILE), :] = value
            place += 1
    edges(plan, {"own": own_ref}, rows, low_ref, high_ref, west_ref, east_ref)


def rows_kernel(error_ref, spot_ref, forcing_ref, *refs, plan, rows, variables, levels, windows):
    part_refs, (next_ref, dealt_ref, low_ref, high_ref, west_ref, east_ref) = refs[:windows], refs[windows:]
    share = levels // windows
    has_next = jnp.where(spot_ref[1] < windows - 1, 1.0, 0.0)
    after_ref = part_refs[-1]
    for var in range(variables):
        for level in range(levels):
            start = (var * levels + level) * rows
            next_ref[pl.ds(var * rows * TILE + level, rows, stride=TILE), :] = (
                after_ref[start : start + rows, :] * has_next
            )
    whole = rows * TILE
    sub = iota((TILE, LANES), 0)
    for shift, ref in enumerate(part_refs):
        window = lax.rem(spot_ref[1] - shift + windows, windows)
        start = pl.multiple_of(window * whole, TILE)
        if ref is after_ref:
            first = variables * levels * rows
            for near in range(share):
                level = spot_ref[1] * share + near
                for var in range(variables):
                    at = pl.multiple_of((var * levels + level) * rows, TILE)
                    dealt_ref[pl.ds(start + near * variables + var, rows, stride=TILE), :] = (
                        ref[pl.ds(at, rows), :] * error_ref[var, level]
                    )
        else:
            first = whole
            dealt_ref[pl.ds(start, whole), :] = ref[:whole, :]
        start = (windows + 2 * window) * whole
        for row in range(rows):
            line = first + row * 2 * share
            for num in range(2):
                near, far = ref[line + num * share : line + num * share + 1, :], ref[
                    line + num * share + share - 1 : line + num * share + share, :
                ]
                at = pl.multiple_of(start + num * whole + row * TILE, TILE)
                dealt_ref[pl.ds(at, TILE), :] = jnp.where(sub < TILE // share, near, far)
    sources = {"next": next_ref, "dealt": dealt_ref, "forcing": forcing_ref}
    edges(plan, sources, rows, low_ref, high_ref, west_ref, east_ref)


def pack(packed, field, lane0, wide):
    lane = iota(field.shape, 1)
    inside = (lane >= lane0) & (lane < lane0 + wide)
    if packed is None:
        packed = (jnp.zeros_like(field), jnp.zeros_like(field))
    west = jnp.where(inside, pltpu.roll(field, lane0, 1), packed[0])
    east = jnp.where(inside, pltpu.roll(field, (lane0 + wide) % LANES, 1), packed[1])
    return west, east


def columns_kernel(unused_ref, south_ref, north_ref, west_inner_ref, east_inner_ref, west_ref, east_ref, *, plan, rows):
    deep = plan.deep
    west_ref[deep : deep + rows] = west_inner_ref[...]
    east_ref[deep : deep + rows] = east_inner_ref[...]
    for away in range(deep):
        low = high = None
        for source, wide, tile, lane0 in plan.fields.values():
            if away < wide:
                low = pack(low, south_ref[tile + wide - 1 - away], lane0, wide)
                high = pack(high, north_ref[tile + away], lane0, wide)
        west_ref[deep - 1 - away], east_ref[deep - 1 - away] = low
        west_ref[deep + rows + away], east_ref[deep + rows + away] = high


def chain_kernel(
    rate_ref, spot_ref, unused_ref, dealt_ref, south_ref, north_ref, east_ref, west_ref, *refs, plan, lat_count, rows, variables, windows
):
    out_refs, (u_ref, v_ref, a_ref, b_ref, m_ref, q_ref) = refs[:windows], refs[windows:]
    share = TILE // variables
    masks = sides(spot_ref, lat_count)
    rate = by_comp(
        (TILE, LANES), lambda comp: rate_ref[comp % variables, spot_ref[1] * share + comp // variables]
    )[None]
    refs = {"dealt": dealt_ref, "south": south_ref, "north": north_ref, "east": east_ref, "west": west_ref}
    load_field(a_ref, plan, "mult", 0, refs, rows, masks)
    here, there = a_ref, b_ref
    q_ref[0] = dealt_ref[0:rows]
    for window in range(windows - 1):
        ring = 3 * (windows - 1 - window)
        load_field(u_ref, plan, "du", window, refs, rows, masks, 0.5)
        load_field(v_ref, plan, "dv", window, refs, rows, masks, 0.5)
        wind_ring = ring - 1
        for step in range(STEPS):
            ring -= 1
            tangent(here, there, u_ref, v_ref, wind_ring, rate, rows, ring, masks)
            here, there = there, here
        if window + 1 < windows - 1:
            load_field(m_ref, plan, "mult", window + 1, refs, rows, masks)
            for start in range(0, rows + 2 * ring, 2):
                for part in range(2):
                    here[part, start : start + 2] = (
                        here[part, start : start + 2] + m_ref[part, start : start + 2]
                    )
            q_ref[window + 1] = here[0, ring : ring + rows]
        else:
            q_ref[window + 1] = here[0, 0:rows] + dealt_ref[(window + 1) * rows : (window + 2) * rows]
    for shift, out_ref in enumerate(out_refs):
        out_ref[...] = q_ref[lax.rem(spot_ref[1] + shift, windows)]


def forward_kernel(
    rate_ref, spot_ref, unused_ref, own_ref, south_ref, north_ref, east_ref, west_ref,
    terms_ref, end_ref, traj_ref, u_ref, v_ref, a_ref, b_ref, *, plan, lat_count, rows, variables
):
    masks = sides(spot_ref, lat_count)
    refs = {"own": own_ref, "south": south_ref, "north": north_ref, "east": east_ref, "west": west_ref}
    load_field(u_ref, plan, "u", 0, refs, rows, masks, 0.5)
    load_field(v_ref, plan, "v", 0, refs, rows, masks, 0.5)
    for var in range(variables):
        rate = by_comp((TILE, LANES), lambda level: rate_ref[var, level])[None]
        load_field(a_ref.at[var], plan, "x", var, refs, rows, masks)
        here, there = a_ref.at[var], b_ref.at[var]
        for step in range(STEPS):
            ring = STEPS - 1 - step
            traj_ref[(step * variables + var) * rows : (step * variables + var + 1) * rows] = here[
                0, ring + 1 : ring + 1 + rows
            ]
            tangent(here, there, u_ref, v_ref, 3, rate, rows, ring, masks)
            here, there = there, here
        end_ref[var * rows : (var + 1) * rows] = here[0, 0:rows]
    groups = terms_ref.shape[1]
    for j in range(5):
        if j < 4:
            tiles = [traj_ref[place * 4 + j] for place in range(groups // TILE)]
            turned = jnp.concatenate(tiles, axis=0).T
            if j == 0:
                initial = turned
        else:
            turned = pltpu.roll(initial, groups - TILE, 1)
        high = turned.astype(BF16)
        terms_ref[j * LANES : (j + 1) * LANES, :] = high
        low = (turned - high.astype(F32)).astype(BF16)
        terms_ref[(j + 5) * LANES : (j + 6) * LANES, :] = low


def final_kernel(
    rate_ref, error_ref, spot_ref, x_hbm, mult_hbm, own_ref, south_ref, north_ref, east_ref, west_ref,
    next_ref, later_south_ref, later_north_ref, later_east_ref, later_west_ref, forcing_ref, prior_ref, *refs,
    plan, later, lat_count, rows, variables, levels, windows
):
    chain_refs, refs = refs[:windows], refs[windows:]
    out_hbms, (x_ref, mult_ref), stages, refs = refs[:3], refs[3:5], refs[5:8], refs[8:]
    state_ref, model_ref, sum_ref = stages
    u_ref, v_ref, a_ref, b_ref, in_sems, out_sems = refs
    copies = [
        pltpu.make_async_copy(src, dst, in_sems.at[num])
        for num, (src, dst) in enumerate(((x_hbm, x_ref), (mult_hbm, mult_ref)))
    ]
    for copy in copies:
        copy.start()
    sent = []

    def send(num, var):
        span = pl.ds(var * levels * rows, levels * rows)
        copy = pltpu.make_async_copy(
            stages[num].at[span], out_hbms[num].at[span], out_sems.at[num * variables + var]
        )
        copy.start()
        sent.append(copy)

    masks = sides(spot_ref, lat_count)
    refs = {"own": own_ref, "south": south_ref, "north": north_ref, "east": east_ref, "west": west_ref}
    later_refs = {
        "next": next_ref, "south": later_south_ref, "north": later_north_ref, "east": later_east_ref, "west": later_west_ref,
    }
    load_field(u_ref, plan, "u", 0, refs, rows, masks, 0.5)
    load_field(v_ref, plan, "v", 0, refs, rows, masks, 0.5)
    for copy in copies:
        copy.wait()
    share = levels // windows
    has_prior = jnp.where(spot_ref[1] > 0, 1.0, 0.0)
    for var in range(variables):
        for level in range(levels):
            span = slice((var * levels + level) * rows, (var * levels + level + 1) * rows)
            prior = prior_ref[pl.ds(var * rows * TILE + level, rows, stride=TILE), :]
            model_ref[span, :] = mult_ref[span, :] * error_ref[var, level] + x_ref[span, :] - has_prior * prior
        send(1, var)
    for shift, ref in enumerate(chain_refs):
        source = lax.rem(spot_ref[1] - shift + windows, windows)
        for near in range(share):
            for var in range(variables):
                start = pl.multiple_of((var * levels + source * share + near) * rows, TILE)
                sum_ref[pl.ds(start, rows), :] = (
                    x_ref[pl.ds(start, rows), :] + ref[pl.ds(near * variables + var, rows, stride=TILE), :]
                )
    for var in range(variables):
        send(2, var)
    for var in range(variables):
        rate = by_comp((TILE, LANES), lambda level: rate_ref[var, level])[None]
        here, there = a_ref.at[var], b_ref.at[var]
        load_field(here, later, "next", var, later_refs, rows, masks, -1.0)
        for step in (2, 1, 0):

            def add(start, size, step=step, var=var):
                base = (step * variables + var) * rows
                if step == 0:
                    return (forcing_ref[base + start : base + start + size],)
                tile = later.fields[("force", step), var][2]
                if start < step:
                    centre = later_south_ref[tile : tile + size]
                elif start >= step + rows:
                    centre = later_north_ref[tile : tile + size]
                else:
                    centre = forcing_ref[base + start - step : base + start - step + size]
                span = slice(later.deep - step + start, later.deep - step + start + size)
                beside = unpack(later_east_ref[span], later_west_ref[span], tile, step)
                return centre, beside

            adjoint(here, there, u_ref, v_ref, 3, rate, rows, step, masks, add)
            here, there = there, here
        for row in range(rows):
            span = pl.ds(var * levels * rows + row, levels, stride=rows)
            state_ref[span, :] = mult_ref[span, :] + here[0, row]
        send(0, var)
    for copy in sent:
        copy.wait()


def shards(
    increment, multiplier, u_wind, v_wind, diffusion, error_var, obs_owner, obs_cell, obs_layer, obs_weight, obs_dual, obs_error
):
    variables, levels, rows, width = increment.shape[1:]
    flat = (variables * levels * rows, width)
    x, mult = increment.reshape(flat), multiplier.reshape(flat)
    u, v = u_wind.reshape(levels * rows, width), v_wind.reshape(levels * rows, width)
    lat_count, windows = lax.axis_size("lat"), lax.axis_size("tm")
    blocks = lat_count * lax.axis_size("lon")
    plan, later = own_plan(variables), later_plan(variables, lax.axis_size("tm"))
    own_fields = variables + 2
    count = obs_owner.shape[0]
    cap = 2 * count // blocks
    groups = STEPS * variables * levels * rows // 4
    spot = jnp.stack([lax.axis_index("lat"), lax.axis_index("tm")]).astype(jnp.int32)

    def planes(ring):
        return pltpu.VMEM((2, rows + 2 * ring, TILE, LANES), F32)

    def tiles(array):
        return array.reshape(array.shape[0] // TILE, TILE, width)

    def lines(array):
        return array.reshape(array.shape[0] * TILE, width)

    row = (1, count)
    share = levels // windows
    part_rows = rows * (TILE + 2 * share)
    wholes = [sds((part_rows, width))] * (windows - 1) + [sds((flat[0] + rows * 2 * share, width))]
    def buffers(plan):
        row_edges, inner = sds((plan.tiles, TILE, width)), sds((rows, TILE, width))
        return [row_edges, row_edges, inner, inner]

    def over(axis, low, high):
        return lax.ppermute(high, axis, ring(axis, 1)), lax.ppermute(low, axis, ring(axis, -1))

    def columns(plan, unused, south, north, west_inner, east_inner):
        return call(
            functools.partial(columns_kernel, plan=plan, rows=rows),
            (sds((rows + 2 * plan.deep, TILE, width)),) * 2,
            unused, south, north, west_inner, east_inner, name="columns", flops=COST["columns"], loose=(0,),
        )

    send, rank, base, own, low, high, west_inner, east_inner, *parts = call(
        functools.partial(
            entry_kernel, plan=plan, rows=rows, variables=variables, levels=levels, windows=windows, blocks=blocks, cap=cap
        ),
        [
            sds((4 * blocks, 2 * cap)), sds((2, count), jnp.int32), sds(row), sds((own_fields * rows * TILE, width)),
            *buffers(plan), *wholes,
        ],
        error_var, spot, obs_owner.reshape(row), obs_cell.reshape(row), obs_layer.reshape(row), obs_weight.T,
        obs_dual.reshape(row), obs_error.reshape(row), mult, u, v, x,
        name="entry", flops=COST["entry"], smem=(0, 1), hbm=range(2, 12), vmem=60,
        scratch=(
            *[pltpu.VMEM(row, jnp.int32)] * 3, pltpu.VMEM((4, count), F32), *[pltpu.VMEM(row, F32)] * 2,
            pltpu.VMEM(flat, F32), *[pltpu.VMEM((levels * rows, width), F32)] * 2, pltpu.VMEM(flat, F32),
            pltpu.VMEM((2 * TILE, count), F32), pltpu.VMEM((4 * blocks, 2 * cap), F32), pltpu.SemaphoreType.DMA((10,)),
        ),
    )
    south, north = over("lat", low, high)
    got = lax.all_to_all(send, ("lat", "lon"), split_axis=0, concat_axis=0, tiled=True)
    parts = [lax.ppermute(part, "tm", ring("tm", shift)) if shift else part for shift, part in enumerate(parts)]
    west, east = over("lon", *columns(plan, got, south, north, west_inner, east_inner))

    slots = pltpu.VMEM((4 * blocks // TILE, TILE, LANES), F32)
    forcing = call(
        functools.partial(scatter_kernel, groups=groups, width=width, rows=rows),
        sds((4 * groups // TILE, TILE, width)),
        got, name="scatter", flops=COST["scatter"],
        scratch=(slots, pltpu.VMEM((groups, 10 * width), F32)),
    )
    after, dealt, low, high, west_inner, east_inner = call(
        functools.partial(rows_kernel, plan=later, rows=rows, variables=variables, levels=levels, windows=windows),
        [sds(flat), sds((3 * windows * rows * TILE, width)), *buffers(later)],
        error_var, spot, lines(forcing), *parts, smem=(0, 1), name="rows", flops=COST["rows"],
    )
    own, after, dealt = tiles(own), tiles(after), tiles(dealt)
    later_south, later_north = over("lat", low, high)

    stage = pltpu.VMEM((variables, 2, rows + 6, TILE, LANES), F32)
    sizes = dict(lat_count=lat_count, rows=rows, variables=variables)
    terms, end = call(
        functools.partial(forward_kernel, plan=plan, **sizes),
        (sds((10 * width, groups), BF16), sds((variables * rows, TILE, width))),
        diffusion, spot, low, own, south, north, east, west, smem=(0, 1), loose=(2,), name="forward", flops=COST["forward"],
        scratch=(pltpu.VMEM((4 * groups // TILE, TILE, width), F32), planes(3), planes(3), stage, stage),
    )
    prior = lax.ppermute(lines(end), "tm", ring("tm", 1))
    edges_later = columns(later, terms, later_south, later_north, west_inner, east_inner)
    later_west, later_east = over("lon", *edges_later)

    def gather(half, earlier, unused):
        return call(
            functools.partial(gather_kernel, groups=groups, width=width, rows=rows, half=half),
            sds((blocks // 2 * (half + 1), LANES)),
            got, terms, earlier, unused, name="gather", flops=COST["gather"], loose=(2, 3) if half == 0 else (3,),
            scratch=(slots, pltpu.VMEM((2, 10 * width, min(512, cap * blocks // 2)), F32)),
        )

    observed = gather(0, spot, edges_later[0])
    chained = call(
        functools.partial(chain_kernel, plan=later, windows=windows, **sizes),
        [sds((rows, TILE, width))] * windows,
        diffusion, spot, observed, dealt, later_south, later_north, later_east, later_west,
        smem=(0, 1), loose=(2,), name="chain", flops=COST["chain"],
        scratch=(planes(8), planes(8), planes(9), planes(9), planes(6), pltpu.VMEM((windows, rows, TILE, LANES), F32)),
    )
    observed = gather(1, observed, chained[0])
    chained = [
        lax.ppermute(lines(part), "tm", ring("tm", shift)) if shift else lines(part)
        for shift, part in enumerate(chained)
    ]
    back = lax.all_to_all(observed, ("lat", "lon"), split_axis=0, concat_axis=0, tiled=True)

    dma = pltpu.SemaphoreType.DMA
    state_res, model_res, summed = call(
        functools.partial(
            final_kernel, plan=plan, later=later, levels=levels, windows=windows, **sizes
        ),
        [sds(flat)] * 3,
        diffusion, error_var, spot, x, mult, own, south, north, east, west,
        after, later_south, later_north, later_east, later_west, forcing, prior, *chained,
        smem=(0, 1, 2), hbm=(3, 4), hbm_outs=(0, 1, 2), name="final", flops=COST["final"],
        scratch=(
            *[pltpu.VMEM(flat, F32)] * 5, planes(3), planes(3), stage, stage, dma((2,)), dma((3 * variables,)),
        ),
    )
    obs_res = call(finish_obs_kernel, sds(row), back, rank, base, name="finish_obs", flops=COST["finish_obs"])
    whole = increment.shape
    return (model_res.reshape(whole), obs_res.reshape(count), state_res.reshape(whole), summed.reshape(whole))


def solution(mesh):
    fields = P("tm", None, None, "lat", "lon")
    winds = P("tm", None, "lat", "lon")
    everyone = ("tm", "lat", "lon")
    in_specs = (
        fields, fields, winds, winds, P(), P(),
        P(everyone, None), P(everyone), P(everyone), P(everyone, None), P(everyone), P(everyone),
    )
    out_specs = (fields, P(everyone), fields, fields)
    return jax.shard_map(shards, mesh=mesh, in_specs=in_specs, out_specs=out_specs, check_vma=False)
```

```python
import functools
import jax
import jax.numpy as jnp
from jax import lax
from jax.experimental import pallas as pl
from jax.experimental.pallas import tpu as pltpu
from jax.sharding import PartitionSpec as P

STEPS = 3
F32 = jnp.float32
BF16 = jnp.bfloat16
LANES = 128
TILE = 8

COST = {
    "entry": 6 * 10**9, "columns": 10**9, "scatter": 5 * 10**9, "rows": 2 * 10**9, "forward": 4 * 10**9,
    "gather": 5 * 10**9, "chain": 4 * 10**9, "final": 30 * 10**9, "finish_obs": 10**9,
}


def ring(axis, by):
    count = lax.axis_size(axis)
    return [(i, (i + by) % count) for i in range(count)]


def from_behind(shard, axis, by):
    size = lax.axis_size(axis)
    pairs = [(i, i + by) for i in range(size) if 0 <= i + by < size]
    return lax.ppermute(shard, axis, pairs)


def call(kernel, out_shape, *args, name, flops=0, smem=(), hbm=(), loose=(), hbm_outs=(), scratch=(), vmem=16):
    def spec(num, far, free=()):
        space = pltpu.HBM if num in far else pl.ANY if num in free else pltpu.VMEM
        return pl.BlockSpec(memory_space=space)

    specs = [
        pl.BlockSpec(memory_space=pltpu.SMEM) if i in smem else spec(i, hbm, loose) for i in range(len(args))
    ]
    several = isinstance(out_shape, (tuple, list))
    return pl.pallas_call(
        kernel,
        out_shape=out_shape,
        in_specs=specs,
        out_specs=[spec(i, hbm_outs) for i in range(len(out_shape))] if several else spec(0, hbm_outs),
        scratch_shapes=list(scratch),
        compiler_params=pltpu.CompilerParams(vmem_limit_bytes=vmem * 1024 * 1024),
        cost_estimate=pl.CostEstimate(flops=flops, bytes_accessed=0, transcendentals=0),
        name=name,
    )(*args)


def sds(shape, dtype=F32):
    return jax.ShapeDtypeStruct(shape, dtype)


def iota(shape, dim):
    return lax.broadcasted_iota(jnp.int32, shape, dim)


def split_two(value):
    high = value.astype(BF16).astype(F32)
    return high, value - high


def route(owner_ref, cell_ref, layer_ref, weight_ref, dual_ref, send_ref, rank_ref, fields_ref, acc_ref, blocks, cap, rows, cols):
    count = owner_ref.shape[1]
    chunk = min(256, count)
    cell = cell_ref[...]
    row = ((cell.astype(F32) + 0.5) * (1.0 / (cols - 1))).astype(jnp.int32)
    layer = layer_ref[...]
    key = (layer // TILE * rows + row) * TILE + layer % TILE
    col = cell - row * (cols - 1)
    for half in range(2):
        base = half * TILE
        fields_ref[base : base + 4, :] = weight_ref[...] if half == 0 else jnp.zeros((4, count), F32)
        if half == 1:
            fields_ref[base : base + 1, :] = dual_ref[...]
            fields_ref[base + 1 : base + 2, :] = key.astype(F32)
            fields_ref[base + 2 : base + 3, :] = col.astype(F32)
        fields_ref[base + 4 : base + 8, :] = fields_ref[base : base + 4, :]
    tri = (iota((chunk, chunk), 0) < iota((chunk, chunk), 1)).astype(F32)
    tri_ones = jnp.concatenate([tri, jnp.ones((chunk, LANES), F32)], axis=1).astype(BF16)
    running = jnp.zeros((blocks, 1), F32)
    acc_ref[...] = jnp.zeros_like(acc_ref)
    pair = 2 * iota((blocks // 2, TILE, chunk), 0) + iota((blocks // 2, TILE, chunk), 1) // 4
    for part in range(count // chunk):
        here = slice(part * chunk, (part + 1) * chunk)
        owner = owner_ref[:, here]
        hit = iota((blocks, chunk), 0) == owner
        hit_f = jnp.where(hit, 1.0, 0.0)
        counted = jnp.dot(hit_f.astype(BF16), tri_ones, preferred_element_type=F32)
        before = counted[:, :chunk] + running
        running = running + counted[:, chunk : chunk + 1]
        rank = jnp.sum(jnp.where(hit, before, 0.0), axis=0, keepdims=True).astype(jnp.int32)
        rank_ref[0:1, here] = rank
        rank_ref[1:2, here] = owner
        ranks = iota((2 * cap, chunk), 0)
        right = jnp.concatenate(
            [jnp.where(ranks == rank, 1.0, 0.0), jnp.where(ranks == rank + cap, 1.0, 0.0)], axis=1
        ).astype(BF16)
        mine = pair == owner[None]
        highs, lows = [], []
        for half in range(2):
            high, low = split_two(fields_ref[half * TILE : (half + 1) * TILE, here])
            highs.append(jnp.where(mine, high[None], 0.0).reshape(4 * blocks, chunk).astype(BF16))
            lows.append(jnp.where(mine, low[None], 0.0).reshape(4 * blocks, chunk).astype(BF16))
        for left in (jnp.concatenate(highs, axis=1), jnp.concatenate(lows, axis=1)):
            acc_ref[...] += lax.dot_general(
                left, right, (((1,), (1,)), ((), ())), preferred_element_type=F32
            )
    send_ref[...] = acc_ref[...]


def unshuffle(got_ref, slots_ref):
    tiles = slots_ref.shape[0]
    keep = (iota((TILE, LANES), 0) < 4) == (iota((TILE, LANES), 1) < 64)
    for tile in range(tiles):
        value = got_ref[tile * TILE : (tile + 1) * TILE, :]
        other = pltpu.roll(pltpu.roll(value, 4, 0), 64, 1)
        slots_ref[tile] = jnp.where(keep, value, other)


def slot_rows(slots_ref, part, tiles_each):
    def field(num):
        return jnp.concatenate(
            [slots_ref[part * tiles_each + t, num : num + 1, :] for t in range(tiles_each)], axis=1
        )

    return field


def corner_rows(row4, tops, bottoms, j):
    zero = jnp.zeros_like(tops)
    return jnp.where(row4 == j, tops, jnp.where(row4 + 1 == j, bottoms, zero))


def slot_places(field, rows):
    key = field(5).astype(jnp.int32)
    line = key // TILE
    group = line // 4 * TILE + key % TILE
    return group, line % 4, field(6).astype(jnp.int32)


def scatter_kernel(got_ref, forcing_ref, slots_ref, acc_ref, *, groups, width, rows):
    unshuffle(got_ref, slots_ref)
    tiles = slots_ref.shape[0]
    tiles_each = min(4, tiles)
    chunk = tiles_each * LANES
    dims = (((1,), (1,)), ((), ()))
    for part in range(tiles // tiles_each):
        field = slot_rows(slots_ref, part, tiles_each)
        group, row4, col = slot_places(field, rows)
        dual = field(4)
        left = jnp.where(iota((groups, chunk), 0) == group, 1.0, 0.0).astype(BF16)
        cells = iota((width, chunk), 0)
        here, beside = cells == col, cells == col + 1
        corners = [field(num) * dual for num in range(4)]
        rights = [[], []]
        for j in range(5):
            first = split_two(corner_rows(row4, corners[0], corners[2], j))
            second = split_two(corner_rows(row4, corners[1], corners[3], j))
            for term in range(2):
                rights[term].append(
                    jnp.where(here, first[term], jnp.where(beside, second[term], 0.0)).astype(BF16)
                )
        added = lax.dot_general(
            left, jnp.concatenate(rights[0] + rights[1], axis=0), dims, preferred_element_type=F32
        )
        if part == 0:
            acc_ref[...] = added
        else:
            acc_ref[...] += added
    fields = forcing_ref.shape[0] // rows
    per = rows // 4

    def term_sum(start, j):
        span = slice(start, start + TILE)
        return acc_ref[span, j * width : (j + 1) * width] + acc_ref[span, (j + 5) * width : (j + 6) * width]

    for place in range(fields):
        for four in range(per):
            start = (place * per + four) * TILE
            for j in range(4):
                value = term_sum(start, j)
                if j == 0 and four > 0:
                    value = value + term_sum(start - TILE, 4)
                forcing_ref[place * rows + four * 4 + j] = value


def gather_kernel(got_ref, traj_ref, earlier_ref, unused_ref, out_ref, slots_ref, picked_ref, *, groups, width, rows, half):
    unshuffle(got_ref, slots_ref)
    tiles = slots_ref.shape[0]
    tiles_each = min(4, tiles // 2)
    chunk = tiles_each * LANES
    size = 2 * tiles_each
    if half == 1:
        out_ref[:tiles, :] = earlier_ref[...]
    parts = tiles // tiles_each // 2
    for part in range(half * parts, (half + 1) * parts):
        field = slot_rows(slots_ref, part, tiles_each)
        group, row4, col = slot_places(field, rows)
        right = jnp.where(iota((groups, chunk), 0) == group, 1.0, 0.0).astype(BF16)
        cells = iota((width, chunk), 0)
        here, beside = cells == col, cells == col + 1
        total = jnp.zeros((width, chunk), F32)
        picked_ref[part % 2] = jnp.dot(traj_ref[...], right, preferred_element_type=F32)
        for j in range(5):
            picked = (
                picked_ref[part % 2, j * width : (j + 1) * width]
                + picked_ref[part % 2, (j + 5) * width : (j + 6) * width]
            )
            first = corner_rows(row4, field(0), field(2), j)
            second = corner_rows(row4, field(1), field(3), j)
            total = total + picked * jnp.where(here, first, jnp.where(beside, second, 0.0))
        value = jnp.sum(total, axis=0, keepdims=True)
        lines = []
        for t in range(tiles_each):
            line = value[:, t * LANES : (t + 1) * LANES]
            lines += [line, pltpu.roll(line, 64, 1)]
        out_ref[part * size : (part + 1) * size, :] = jnp.concatenate(lines, axis=0)


def finish_obs_kernel(unused_ref, back_ref, rank_ref, base_ref, out_ref):
    blocks = back_ref.shape[0]
    count = base_ref.shape[1]
    chunk = min(512, count)
    high, low = split_two(back_ref[...].T)
    high, low = high.astype(BF16), low.astype(BF16)
    for part in range(count // chunk):
        here = slice(part * chunk, (part + 1) * chunk)
        hit = jnp.where(iota((blocks, chunk), 0) == rank_ref[1:2, here], 1.0, 0.0).astype(BF16)
        picked = jnp.dot(high, hit, preferred_element_type=F32) + jnp.dot(
            low, hit, preferred_element_type=F32
        )
        wanted = iota((LANES, chunk), 0) == rank_ref[0:1, here]
        value = jnp.sum(jnp.where(wanted, picked, 0.0), axis=0, keepdims=True)
        out_ref[:, here] = base_ref[:, here] + value


class Plan:
    def __init__(self, fields):
        self.fields = {}
        tile = 0
        for name, num, source, wide in fields:
            self.fields[name, num] = (source, wide, tile, tile)
            tile += wide
        self.tiles = tile
        self.deep = max(wide for name, num, source, wide in fields)


def own_plan(variables):
    fields = [("x", var, ("own", var), 3) for var in range(variables)]
    fields += [("u", 0, ("own", variables), 3), ("v", 0, ("own", variables + 1), 3)]
    return Plan(fields)


def later_plan(variables, windows):
    fields = [("next", var, ("next", var), 3) for var in range(variables)]
    for window, wide in ((0, 9), (1, 6), (2, 3)):
        fields.append(("mult", window, ("dealt", window), wide))
    for window, wide in ((0, 8), (1, 5), (2, 2)):
        fields.append(("du", window, ("dealt", windows + 2 * window), wide))
        fields.append(("dv", window, ("dealt", windows + 2 * window + 1), wide))
    for step in (2, 1):
        for var in range(variables):
            fields.append((("force", step), var, ("forcing", step * variables + var), step))
    return Plan(fields)


def by_comp(shape, value_of):
    sub = iota(shape, 0)
    result = jnp.zeros(shape, F32)
    for comp in range(TILE):
        result = jnp.where(sub == comp, value_of(comp), result)
    return result


def sides(lat_count):
    lat = lax.axis_index("lat")
    return jnp.where(lat > 0, 1.0, 0.0), jnp.where(lat < lat_count - 1, 1.0, 0.0)


def unpack(east, west, lane0, wide):
    lane = iota(east.shape, 2)
    from_east = pltpu.roll(east, (LANES - lane0) % LANES, 2)
    from_west = pltpu.roll(west, (LANES - lane0 - wide) % LANES, 2)
    return jnp.where(lane < wide, from_east, jnp.where(lane >= LANES - wide, from_west, 0.0))


def spans(rows, ring, edge_masks):
    result = []
    if ring:
        result.append((0, ring, edge_masks[0]))
    result += [(ring + start, 4, None) for start in range(0, rows, 4)]
    if ring:
        result.append((ring + rows, ring, edge_masks[1]))
    return result


def masked(value, mask):
    return value if mask is None else value * mask


def load_field(dst_ref, plan, name, num, refs, rows, edge_masks, scale=None):
    (kind, place), wide, tile, lane0 = plan.fields[name, num]
    source_ref = refs[kind]
    for start, size, mask in spans(rows, wide, edge_masks):
        if start < wide:
            centre = refs["south"][tile : tile + wide]
        elif start >= wide + rows:
            centre = refs["north"][tile : tile + wide]
        else:
            first = place * rows + start - wide
            centre = source_ref[first : first + size]
        at = plan.deep - wide + start
        beside = unpack(refs["east"][at : at + size], refs["west"][at : at + size], lane0, wide)
        for part, value in enumerate((centre, beside)):
            if scale is not None:
                value = value * scale
            dst_ref[part, start : start + size] = masked(value, mask)


def east_west(centre_e, halo_e, centre_w, halo_w):
    lane = iota(centre_e.shape, 2)
    ce, he = pltpu.roll(centre_e, LANES - 1, 2), pltpu.roll(halo_e, LANES - 1, 2)
    cw, hw = pltpu.roll(centre_w, 1, 2), pltpu.roll(halo_w, 1, 2)
    last, start = lane == LANES - 1, lane == 0
    east = (jnp.where(last, he, ce), jnp.where(last, ce, he))
    west = (jnp.where(start, hw, cw), jnp.where(start, cw, hw))
    return east, west


def tangent(src_ref, dst_ref, u_ref, v_ref, wind_ring, rate, rows, ring, edge_masks):
    parts = 1 if ring == 0 else 2
    for start, size, mask in spans(rows, ring, edge_masks):
        field = [src_ref[part, start : start + size + 2] for part in range(2)]
        middle = [part[1:-1] for part in field]
        east, west = east_west(*middle, *middle)
        wind = slice(wind_ring - ring + start, wind_ring - ring + start + size)
        for part in range(parts):
            north, south = field[part][2:], field[part][:-2]
            e, w, f = east[part], west[part], middle[part]
            value = (
                f
                + rate * ((e + w) + (north + south) - 4.0 * f)
                - u_ref[part, wind] * (e - w)
                - v_ref[part, wind] * (north - south)
            )
            dst_ref[part, start : start + size] = masked(value, mask)


def adjoint(src_ref, dst_ref, u_ref, v_ref, wind_ring, rate, rows, ring, edge_masks, add):
    parts = 1 if ring == 0 else 2
    for start, size, mask in spans(rows, ring, edge_masks):
        first = wind_ring - ring - 1 + start
        eastward, westward, result = [], [], []
        for part in range(2):
            field = src_ref[part, start : start + size + 2]
            thin = rate * field
            across = v_ref[part, first : first + size + 2] * field
            along = u_ref[part, first + 1 : first + 1 + size] * field[1:-1]
            eastward.append(thin[1:-1] + along)
            westward.append(thin[1:-1] - along)
            result.append(
                field[1:-1] - 4.0 * thin[1:-1] + (thin[2:] + across[2:]) + (thin[:-2] - across[:-2])
            )
        east, west = east_west(*eastward, *westward)
        extra = add(start, size)
        for part in range(parts):
            value = result[part] + (east[part] + west[part]) + extra[part]
            dst_ref[part, start : start + size] = masked(value, mask)


def edges(plan, sources, rows, low_ref, high_ref, west_ref, east_ref):
    def tile_at(kind, place, row):
        at = (place * rows + row) * TILE
        return sources[kind][at : at + TILE, :]

    for (kind, place), wide, tile, lane0 in plan.fields.values():
        for num in range(wide):
            low_ref[tile + num] = tile_at(kind, place, num)
            high_ref[tile + num] = tile_at(kind, place, rows - wide + num)
    for row in range(rows):
        packed = None
        for (kind, place), wide, tile, lane0 in plan.fields.values():
            packed = pack(packed, tile_at(kind, place, row), lane0, wide)
        west_ref[row], east_ref[row] = packed


def entry_kernel(
    error_ref, owner_hbm, cell_hbm, layer_hbm, weight_hbm, dual_hbm, noise_hbm, mult_hbm, u_hbm, v_hbm, x_hbm,
    send_ref, rank_ref, base_ref, own_ref, low_ref, high_ref, west_ref, east_ref, *refs,
    plan, rows, variables, levels, windows, blocks, cap
):
    part_refs, refs = refs[:windows], refs[windows:]
    (owner_ref, cell_ref, layer_ref, weight_ref, dual_ref, noise_ref, mult_ref, u_ref, v_ref, x_ref) = refs[:10]
    fields_ref, acc_ref, sems = refs[10:]
    pairs = (
        (owner_hbm, owner_ref), (cell_hbm, cell_ref), (layer_hbm, layer_ref), (weight_hbm, weight_ref),
        (dual_hbm, dual_ref), (noise_hbm, noise_ref), (mult_hbm, mult_ref), (u_hbm, u_ref), (v_hbm, v_ref),
        (x_hbm, x_ref),
    )
    copies = [pltpu.make_async_copy(src, dst, sems.at[num]) for num, (src, dst) in enumerate(pairs)]
    for copy in copies:
        copy.start()
    for copy in copies[:6]:
        copy.wait()
    width = mult_ref.shape[1]
    base_ref[...] = noise_ref[...] * dual_ref[...]
    route(
        owner_ref, cell_ref, layer_ref, weight_ref, dual_ref, send_ref, rank_ref, fields_ref, acc_ref,
        blocks, cap, rows, width,
    )
    for copy in copies[6:]:
        copy.wait()
    share = levels // windows
    for shift, part_ref in enumerate(part_refs):
        target = lax.rem(lax.axis_index("tm") + shift, windows)
        whole = shift == windows - 1
        first = variables * levels * rows if whole else rows * TILE
        if whole:
            part_ref[:first, :] = mult_ref[...]
        for near in range(share):
            level = target * share + near
            for var in range(0 if whole else variables):
                start = pl.multiple_of((var * levels + level) * rows, TILE)
                value = mult_ref[pl.ds(start, rows), :] * error_ref[var, level]
                part_ref[pl.ds(near * variables + var, rows, stride=TILE), :] = value
            start = pl.multiple_of(level * rows, TILE)
            for num, ref in enumerate((u_ref, v_ref)):
                part_ref[pl.ds(first + num * share + near, rows, stride=2 * share), :] = ref[
                    pl.ds(start, rows), :
                ]
    place = 0
    for ref, count in ((x_ref, variables), (u_ref, 1), (v_ref, 1)):
        for num in range(count):
            for level in range(levels):
                value = ref[(num * levels + level) * rows : (num * levels + level + 1) * rows, :]
                own_ref[pl.ds(place * rows * TILE + level, rows, stride=TILE), :] = value
            place += 1
    edges(plan, {"own": own_ref}, rows, low_ref, high_ref, west_ref, east_ref)


def rows_kernel(error_ref, forcing_ref, *refs, plan, rows, variables, levels, windows):
    part_refs, (next_ref, dealt_ref, low_ref, high_ref, west_ref, east_ref) = refs[:windows], refs[windows:]
    share = levels // windows
    has_next = jnp.where(lax.axis_index("tm") < windows - 1, 1.0, 0.0)
    after_ref = part_refs[-1]
    for var in range(variables):
        for level in range(levels):
            start = (var * levels + level) * rows
            next_ref[pl.ds(var * rows * TILE + level, rows, stride=TILE), :] = (
                after_ref[start : start + rows, :] * has_next
            )
    whole = rows * TILE
    sub = iota((TILE, LANES), 0)
    for shift, ref in enumerate(part_refs):
        window = lax.rem(lax.axis_index("tm") - shift + windows, windows)
        start = pl.multiple_of(window * whole, TILE)
        if ref is after_ref:
            first = variables * levels * rows
            for near in range(share):
                level = lax.axis_index("tm") * share + near
                for var in range(variables):
                    at = pl.multiple_of((var * levels + level) * rows, TILE)
                    dealt_ref[pl.ds(start + near * variables + var, rows, stride=TILE), :] = (
                        ref[pl.ds(at, rows), :] * error_ref[var, level]
                    )
        else:
            first = whole
            dealt_ref[pl.ds(start, whole), :] = ref[:whole, :]
        start = (windows + 2 * window) * whole
        for row in range(rows):
            line = first + row * 2 * share
            for num in range(2):
                near, far = ref[line + num * share : line + num * share + 1, :], ref[
                    line + num * share + share - 1 : line + num * share + share, :
                ]
                at = pl.multiple_of(start + num * whole + row * TILE, TILE)
                dealt_ref[pl.ds(at, TILE), :] = jnp.where(sub < TILE // share, near, far)
    sources = {"next": next_ref, "dealt": dealt_ref, "forcing": forcing_ref}
    edges(plan, sources, rows, low_ref, high_ref, west_ref, east_ref)


def pack(packed, field, lane0, wide):
    lane = iota(field.shape, 1)
    inside = (lane >= lane0) & (lane < lane0 + wide)
    if packed is None:
        packed = (jnp.zeros_like(field), jnp.zeros_like(field))
    west = jnp.where(inside, pltpu.roll(field, lane0, 1), packed[0])
    east = jnp.where(inside, pltpu.roll(field, (lane0 + wide) % LANES, 1), packed[1])
    return west, east


def columns_kernel(unused_ref, south_ref, north_ref, west_inner_ref, east_inner_ref, west_ref, east_ref, *, plan, rows):
    deep = plan.deep
    west_ref[deep : deep + rows] = west_inner_ref[...]
    east_ref[deep : deep + rows] = east_inner_ref[...]
    for away in range(deep):
        low = high = None
        for source, wide, tile, lane0 in plan.fields.values():
            if away < wide:
                low = pack(low, south_ref[tile + wide - 1 - away], lane0, wide)
                high = pack(high, north_ref[tile + away], lane0, wide)
        west_ref[deep - 1 - away], east_ref[deep - 1 - away] = low
        west_ref[deep + rows + away], east_ref[deep + rows + away] = high


def chain_kernel(
    rate_ref, unused_ref, dealt_ref, south_ref, north_ref, east_ref, west_ref, *refs, plan, lat_count, rows, variables, windows
):
    out_refs, (u_ref, v_ref, a_ref, b_ref, m_ref, q_ref) = refs[:windows], refs[windows:]
    share = TILE // variables
    masks = sides(lat_count)
    rate = by_comp(
        (TILE, LANES), lambda comp: rate_ref[comp % variables, lax.axis_index("tm") * share + comp // variables]
    )[None]
    refs = {"dealt": dealt_ref, "south": south_ref, "north": north_ref, "east": east_ref, "west": west_ref}
    load_field(a_ref, plan, "mult", 0, refs, rows, masks)
    here, there = a_ref, b_ref
    q_ref[0] = dealt_ref[0:rows]
    for window in range(windows - 1):
        ring = 3 * (windows - 1 - window)
        load_field(u_ref, plan, "du", window, refs, rows, masks, 0.5)
        load_field(v_ref, plan, "dv", window, refs, rows, masks, 0.5)
        wind_ring = ring - 1
        for step in range(STEPS):
            ring -= 1
            tangent(here, there, u_ref, v_ref, wind_ring, rate, rows, ring, masks)
            here, there = there, here
        if window + 1 < windows - 1:
            load_field(m_ref, plan, "mult", window + 1, refs, rows, masks)
            for start in range(0, rows + 2 * ring, 2):
                for part in range(2):
                    here[part, start : start + 2] = (
                        here[part, start : start + 2] + m_ref[part, start : start + 2]
                    )
            q_ref[window + 1] = here[0, ring : ring + rows]
        else:
            q_ref[window + 1] = here[0, 0:rows] + dealt_ref[(window + 1) * rows : (window + 2) * rows]
    for shift, out_ref in enumerate(out_refs):
        out_ref[...] = q_ref[lax.rem(lax.axis_index("tm") + shift, windows)]


def forward_kernel(
    rate_ref, unused_ref, own_ref, south_ref, north_ref, east_ref, west_ref,
    terms_ref, end_ref, traj_ref, u_ref, v_ref, a_ref, b_ref, *, plan, lat_count, rows, variables
):
    masks = sides(lat_count)
    refs = {"own": own_ref, "south": south_ref, "north": north_ref, "east": east_ref, "west": west_ref}
    load_field(u_ref, plan, "u", 0, refs, rows, masks, 0.5)
    load_field(v_ref, plan, "v", 0, refs, rows, masks, 0.5)
    for var in range(variables):
        rate = by_comp((TILE, LANES), lambda level: rate_ref[var, level])[None]
        load_field(a_ref.at[var], plan, "x", var, refs, rows, masks)
        here, there = a_ref.at[var], b_ref.at[var]
        for step in range(STEPS):
            ring = STEPS - 1 - step
            traj_ref[(step * variables + var) * rows : (step * variables + var + 1) * rows] = here[
                0, ring + 1 : ring + 1 + rows
            ]
            tangent(here, there, u_ref, v_ref, 3, rate, rows, ring, masks)
            here, there = there, here
        end_ref[var * rows : (var + 1) * rows] = here[0, 0:rows]
    groups = terms_ref.shape[1]
    for j in range(5):
        if j < 4:
            tiles = [traj_ref[place * 4 + j] for place in range(groups // TILE)]
            turned = jnp.concatenate(tiles, axis=0).T
            if j == 0:
                initial = turned
        else:
            turned = pltpu.roll(initial, groups - TILE, 1)
        high = turned.astype(BF16)
        terms_ref[j * LANES : (j + 1) * LANES, :] = high
        low = (turned - high.astype(F32)).astype(BF16)
        terms_ref[(j + 5) * LANES : (j + 6) * LANES, :] = low


def final_kernel(
    rate_ref, error_ref, x_hbm, mult_hbm, own_ref, south_ref, north_ref, east_ref, west_ref,
    next_ref, later_south_ref, later_north_ref, later_east_ref, later_west_ref, forcing_ref, prior_ref, *refs,
    plan, later, lat_count, rows, variables, levels, windows
):
    chain_refs, refs = refs[:windows], refs[windows:]
    out_hbms, (x_ref, mult_ref), stages, refs = refs[:3], refs[3:5], refs[5:8], refs[8:]
    state_ref, model_ref, sum_ref = stages
    u_ref, v_ref, a_ref, b_ref, in_sems, out_sems = refs
    copies = [
        pltpu.make_async_copy(src, dst, in_sems.at[num])
        for num, (src, dst) in enumerate(((x_hbm, x_ref), (mult_hbm, mult_ref)))
    ]
    for copy in copies:
        copy.start()
    sent = []

    def send(num, var):
        span = pl.ds(var * levels * rows, levels * rows)
        copy = pltpu.make_async_copy(
            stages[num].at[span], out_hbms[num].at[span], out_sems.at[num * variables + var]
        )
        copy.start()
        sent.append(copy)

    masks = sides(lat_count)
    refs = {"own": own_ref, "south": south_ref, "north": north_ref, "east": east_ref, "west": west_ref}
    later_refs = {
        "next": next_ref, "south": later_south_ref, "north": later_north_ref, "east": later_east_ref, "west": later_west_ref,
    }
    load_field(u_ref, plan, "u", 0, refs, rows, masks, 0.5)
    load_field(v_ref, plan, "v", 0, refs, rows, masks, 0.5)
    for copy in copies:
        copy.wait()
    share = levels // windows
    has_prior = jnp.where(lax.axis_index("tm") > 0, 1.0, 0.0)
    for var in range(variables):
        for level in range(levels):
            span = slice((var * levels + level) * rows, (var * levels + level + 1) * rows)
            prior = prior_ref[pl.ds(var * rows * TILE + level, rows, stride=TILE), :]
            model_ref[span, :] = mult_ref[span, :] * error_ref[var, level] + x_ref[span, :] - has_prior * prior
        send(1, var)
    for shift, ref in enumerate(chain_refs):
        source = lax.rem(lax.axis_index("tm") - shift + windows, windows)
        for near in range(share):
            for var in range(variables):
                start = pl.multiple_of((var * levels + source * share + near) * rows, TILE)
                sum_ref[pl.ds(start, rows), :] = (
                    x_ref[pl.ds(start, rows), :] + ref[pl.ds(near * variables + var, rows, stride=TILE), :]
                )
    for var in range(variables):
        send(2, var)
    for var in range(variables):
        rate = by_comp((TILE, LANES), lambda level: rate_ref[var, level])[None]
        here, there = a_ref.at[var], b_ref.at[var]
        load_field(here, later, "next", var, later_refs, rows, masks, -1.0)
        for step in (2, 1, 0):

            def add(start, size, step=step, var=var):
                base = (step * variables + var) * rows
                if step == 0:
                    return (forcing_ref[base + start : base + start + size],)
                tile = later.fields[("force", step), var][2]
                if start < step:
                    centre = later_south_ref[tile : tile + size]
                elif start >= step + rows:
                    centre = later_north_ref[tile : tile + size]
                else:
                    centre = forcing_ref[base + start - step : base + start - step + size]
                span = slice(later.deep - step + start, later.deep - step + start + size)
                beside = unpack(later_east_ref[span], later_west_ref[span], tile, step)
                return centre, beside

            adjoint(here, there, u_ref, v_ref, 3, rate, rows, step, masks, add)
            here, there = there, here
        for row in range(rows):
            span = pl.ds(var * levels * rows + row, levels, stride=rows)
            state_ref[span, :] = mult_ref[span, :] + here[0, row]
        send(0, var)
    for copy in sent:
        copy.wait()


def shards(
    increment, multiplier, u_wind, v_wind, diffusion, error_var, obs_owner, obs_cell, obs_layer, obs_weight, obs_dual, obs_error
):
    variables, levels, rows, width = increment.shape[1:]
    flat = (variables * levels * rows, width)
    x, mult = increment.reshape(flat), multiplier.reshape(flat)
    u, v = u_wind.reshape(levels * rows, width), v_wind.reshape(levels * rows, width)
    lat_count, windows = lax.axis_size("lat"), lax.axis_size("tm")
    blocks = lat_count * lax.axis_size("lon")
    plan, later = own_plan(variables), later_plan(variables, lax.axis_size("tm"))
    own_fields = variables + 2
    count = obs_owner.shape[0]
    cap = 2 * count // blocks
    groups = STEPS * variables * levels * rows // 4

    def planes(ring):
        return pltpu.VMEM((2, rows + 2 * ring, TILE, LANES), F32)

    def tiles(array):
        return array.reshape(array.shape[0] // TILE, TILE, width)

    def lines(array):
        return array.reshape(array.shape[0] * TILE, width)

    row = (1, count)
    share = levels // windows
    part_rows = rows * (TILE + 2 * share)
    wholes = [sds((part_rows, width))] * (windows - 1) + [sds((flat[0] + rows * 2 * share, width))]
    def buffers(plan):
        row_edges, inner = sds((plan.tiles, TILE, width)), sds((rows, TILE, width))
        return [row_edges, row_edges, inner, inner]

    def over(axis, low, high):
        return lax.ppermute(high, axis, ring(axis, 1)), lax.ppermute(low, axis, ring(axis, -1))

    def columns(plan, unused, south, north, west_inner, east_inner):
        return call(
            functools.partial(columns_kernel, plan=plan, rows=rows),
            (sds((rows + 2 * plan.deep, TILE, width)),) * 2,
            unused, south, north, west_inner, east_inner, name="columns", flops=COST["columns"], loose=(0,),
        )

    send, rank, base, own, low, high, west_inner, east_inner, *parts = call(
        functools.partial(
            entry_kernel, plan=plan, rows=rows, variables=variables, levels=levels, windows=windows, blocks=blocks, cap=cap
        ),
        [
            sds((4 * blocks, 2 * cap)), sds((2, count), jnp.int32), sds(row), sds((own_fields * rows * TILE, width)),
            *buffers(plan), *wholes,
        ],
        error_var, obs_owner.reshape(row), obs_cell.reshape(row), obs_layer.reshape(row), obs_weight.T,
        obs_dual.reshape(row), obs_error.reshape(row), mult, u, v, x,
        name="entry", flops=COST["entry"], smem=(0,), hbm=range(1, 11), vmem=60,
        scratch=(
            *[pltpu.VMEM(row, jnp.int32)] * 3, pltpu.VMEM((4, count), F32), *[pltpu.VMEM(row, F32)] * 2,
            pltpu.VMEM(flat, F32), *[pltpu.VMEM((levels * rows, width), F32)] * 2, pltpu.VMEM(flat, F32),
            pltpu.VMEM((2 * TILE, count), F32), pltpu.VMEM((4 * blocks, 2 * cap), F32), pltpu.SemaphoreType.DMA((10,)),
        ),
    )
    south, north = over("lat", low, high)
    got = lax.all_to_all(send, ("lat", "lon"), split_axis=0, concat_axis=0, tiled=True)
    parts = [lax.ppermute(part, "tm", ring("tm", shift)) if shift else part for shift, part in enumerate(parts)]
    west, east = over("lon", *columns(plan, got, south, north, west_inner, east_inner))

    slots = pltpu.VMEM((4 * blocks // TILE, TILE, LANES), F32)
    forcing = call(
        functools.partial(scatter_kernel, groups=groups, width=width, rows=rows),
        sds((4 * groups // TILE, TILE, width)),
        got, name="scatter", flops=COST["scatter"],
        scratch=(slots, pltpu.VMEM((groups, 10 * width), F32)),
    )
    after, dealt, low, high, west_inner, east_inner = call(
        functools.partial(rows_kernel, plan=later, rows=rows, variables=variables, levels=levels, windows=windows),
        [sds(flat), sds((3 * windows * rows * TILE, width)), *buffers(later)],
        error_var, lines(forcing), *parts, smem=(0,), name="rows", flops=COST["rows"],
    )
    own, after, dealt = tiles(own), tiles(after), tiles(dealt)
    later_south, later_north = over("lat", low, high)

    stage = pltpu.VMEM((variables, 2, rows + 6, TILE, LANES), F32)
    sizes = dict(lat_count=lat_count, rows=rows, variables=variables)
    terms, end = call(
        functools.partial(forward_kernel, plan=plan, **sizes),
        (sds((10 * width, groups), BF16), sds((variables * rows, TILE, width))),
        diffusion, low, own, south, north, east, west, smem=(0,), loose=(1,), name="forward", flops=COST["forward"],
        scratch=(pltpu.VMEM((4 * groups // TILE, TILE, width), F32), planes(3), planes(3), stage, stage),
    )
    prior = lax.ppermute(lines(end), "tm", ring("tm", 1))
    edges_later = columns(later, terms, later_south, later_north, west_inner, east_inner)
    later_west, later_east = over("lon", *edges_later)

    def gather(half, earlier, unused):
        return call(
            functools.partial(gather_kernel, groups=groups, width=width, rows=rows, half=half),
            sds((blocks // 2 * (half + 1), LANES)),
            got, terms, earlier, unused, name="gather", flops=COST["gather"], loose=(2, 3) if half == 0 else (3,),
            scratch=(slots, pltpu.VMEM((2, 10 * width, min(512, cap * blocks // 2)), F32)),
        )

    observed = gather(0, edges_later[0], edges_later[0])
    chained = call(
        functools.partial(chain_kernel, plan=later, windows=windows, **sizes),
        [sds((rows, TILE, width))] * windows,
        diffusion, observed, dealt, later_south, later_north, later_east, later_west,
        smem=(0,), loose=(1,), name="chain", flops=COST["chain"],
        scratch=(planes(8), planes(8), planes(9), planes(9), planes(6), pltpu.VMEM((windows, rows, TILE, LANES), F32)),
    )
    observed = gather(1, observed, chained[0])
    chained = [
        lax.ppermute(lines(part), "tm", ring("tm", shift)) if shift else lines(part)
        for shift, part in enumerate(chained)
    ]
    back = lax.all_to_all(observed, ("lat", "lon"), split_axis=0, concat_axis=0, tiled=True)

    dma = pltpu.SemaphoreType.DMA
    state_res, model_res, summed = call(
        functools.partial(
            final_kernel, plan=plan, later=later, levels=levels, windows=windows, **sizes
        ),
        [sds(flat)] * 3,
        diffusion, error_var, x, mult, own, south, north, east, west,
        after, later_south, later_north, later_east, later_west, forcing, prior, *chained,
        smem=(0, 1), hbm=(2, 3), hbm_outs=(0, 1, 2), name="final", flops=COST["final"],
        scratch=(
            *[pltpu.VMEM(flat, F32)] * 5, planes(3), planes(3), stage, stage, dma((2,)), dma((3 * variables,)),
        ),
    )
    obs_res = call(
        finish_obs_kernel, sds(row), state_res, back, rank, base, name="finish_obs", flops=COST["finish_obs"], loose=(0,),
    )
    whole = increment.shape
    return (model_res.reshape(whole), obs_res.reshape(count), state_res.reshape(whole), summed.reshape(whole))


def solution(mesh):
    fields = P("tm", None, None, "lat", "lon")
    winds = P("tm", None, "lat", "lon")
    everyone = ("tm", "lat", "lon")
    in_specs = (
        fields, fields, winds, winds, P(), P(),
        P(everyone, None), P(everyone), P(everyone), P(everyone, None), P(everyone), P(everyone),
    )
    out_specs = (fields, P(everyone), fields, fields)
    return jax.shard_map(shards, mesh=mesh, in_specs=in_specs, out_specs=out_specs, check_vma=False)
```

```python
import functools
import jax
import jax.numpy as jnp
from jax import lax
from jax.experimental import pallas as pl
from jax.experimental.pallas import tpu as pltpu
from jax.sharding import PartitionSpec as P

STEPS = 3
F32 = jnp.float32
BF16 = jnp.bfloat16
LANES = 128
TILE = 8

COST = {
    "entry": 6 * 10**9, "columns": 10**9, "scatter": 5 * 10**9, "rows": 2 * 10**9, "forward": 4 * 10**9,
    "gather": 5 * 10**9, "chain": 4 * 10**9, "final": 30 * 10**9, "finish_obs": 10**9,
}


def ring(axis, by):
    count = lax.axis_size(axis)
    return [(i, (i + by) % count) for i in range(count)]


def from_behind(shard, axis, by):
    size = lax.axis_size(axis)
    pairs = [(i, i + by) for i in range(size) if 0 <= i + by < size]
    return lax.ppermute(shard, axis, pairs)


def call(kernel, out_shape, *args, name, flops=0, smem=(), hbm=(), loose=(), hbm_outs=(), scratch=(), vmem=16):
    def spec(num, far, free=()):
        space = pltpu.HBM if num in far else pl.ANY if num in free else pltpu.VMEM
        return pl.BlockSpec(memory_space=space)

    specs = [
        pl.BlockSpec(memory_space=pltpu.SMEM) if i in smem else spec(i, hbm, loose) for i in range(len(args))
    ]
    several = isinstance(out_shape, (tuple, list))
    return pl.pallas_call(
        kernel,
        out_shape=out_shape,
        in_specs=specs,
        out_specs=[spec(i, hbm_outs) for i in range(len(out_shape))] if several else spec(0, hbm_outs),
        scratch_shapes=list(scratch),
        compiler_params=pltpu.CompilerParams(vmem_limit_bytes=vmem * 1024 * 1024),
        cost_estimate=pl.CostEstimate(flops=flops, bytes_accessed=0, transcendentals=0),
        name=name,
    )(*args)


def sds(shape, dtype=F32):
    return jax.ShapeDtypeStruct(shape, dtype)


def iota(shape, dim):
    return lax.broadcasted_iota(jnp.int32, shape, dim)


def split_two(value):
    high = value.astype(BF16).astype(F32)
    return high, value - high


def route(owner_ref, cell_ref, layer_ref, weight_ref, dual_ref, send_ref, rank_ref, fields_ref, acc_ref, blocks, cap, rows, cols):
    count = owner_ref.shape[1]
    chunk = min(256, count)
    cell = cell_ref[...]
    row = ((cell.astype(F32) + 0.5) * (1.0 / (cols - 1))).astype(jnp.int32)
    layer = layer_ref[...]
    key = (layer // TILE * rows + row) * TILE + layer % TILE
    col = cell - row * (cols - 1)
    for half in range(2):
        base = half * TILE
        fields_ref[base : base + 4, :] = weight_ref[...] if half == 0 else jnp.zeros((4, count), F32)
        if half == 1:
            fields_ref[base : base + 1, :] = dual_ref[...]
            fields_ref[base + 1 : base + 2, :] = key.astype(F32)
            fields_ref[base + 2 : base + 3, :] = col.astype(F32)
        fields_ref[base + 4 : base + 8, :] = fields_ref[base : base + 4, :]
    tri = (iota((chunk, chunk), 0) < iota((chunk, chunk), 1)).astype(F32)
    tri_ones = jnp.concatenate([tri, jnp.ones((chunk, LANES), F32)], axis=1).astype(BF16)
    running = jnp.zeros((blocks, 1), F32)
    acc_ref[...] = jnp.zeros_like(acc_ref)
    pair = 2 * iota((blocks // 2, TILE, chunk), 0) + iota((blocks // 2, TILE, chunk), 1) // 4
    for part in range(count // chunk):
        here = slice(part * chunk, (part + 1) * chunk)
        owner = owner_ref[:, here]
        hit = iota((blocks, chunk), 0) == owner
        hit_f = jnp.where(hit, 1.0, 0.0)
        counted = jnp.dot(hit_f.astype(BF16), tri_ones, preferred_element_type=F32)
        before = counted[:, :chunk] + running
        running = running + counted[:, chunk : chunk + 1]
        rank = jnp.sum(jnp.where(hit, before, 0.0), axis=0, keepdims=True).astype(jnp.int32)
        rank_ref[0:1, here] = rank
        rank_ref[1:2, here] = owner
        ranks = iota((2 * cap, chunk), 0)
        right = jnp.concatenate(
            [jnp.where(ranks == rank, 1.0, 0.0), jnp.where(ranks == rank + cap, 1.0, 0.0)], axis=1
        ).astype(BF16)
        mine = pair == owner[None]
        highs, lows = [], []
        for half in range(2):
            high, low = split_two(fields_ref[half * TILE : (half + 1) * TILE, here])
            highs.append(jnp.where(mine, high[None], 0.0).reshape(4 * blocks, chunk).astype(BF16))
            lows.append(jnp.where(mine, low[None], 0.0).reshape(4 * blocks, chunk).astype(BF16))
        for left in (jnp.concatenate(highs, axis=1), jnp.concatenate(lows, axis=1)):
            acc_ref[...] += lax.dot_general(
                left, right, (((1,), (1,)), ((), ())), preferred_element_type=F32
            )
    send_ref[...] = acc_ref[...]


def unshuffle(got_ref, slots_ref):
    tiles = slots_ref.shape[0]
    keep = (iota((TILE, LANES), 0) < 4) == (iota((TILE, LANES), 1) < 64)
    for tile in range(tiles):
        value = got_ref[tile * TILE : (tile + 1) * TILE, :]
        other = pltpu.roll(pltpu.roll(value, 4, 0), 64, 1)
        slots_ref[tile] = jnp.where(keep, value, other)


def slot_rows(slots_ref, part, tiles_each):
    def field(num):
        return jnp.concatenate(
            [slots_ref[part * tiles_each + t, num : num + 1, :] for t in range(tiles_each)], axis=1
        )

    return field


def corner_rows(row4, tops, bottoms, j):
    zero = jnp.zeros_like(tops)
    return jnp.where(row4 == j, tops, jnp.where(row4 + 1 == j, bottoms, zero))


def slot_places(field, rows):
    key = field(5).astype(jnp.int32)
    line = key // TILE
    group = line // 4 * TILE + key % TILE
    return group, line % 4, field(6).astype(jnp.int32)


def scatter_kernel(got_ref, forcing_ref, slots_ref, acc_ref, *, groups, width, rows):
    unshuffle(got_ref, slots_ref)
    tiles = slots_ref.shape[0]
    tiles_each = min(4, tiles)
    chunk = tiles_each * LANES
    dims = (((1,), (1,)), ((), ()))
    for part in range(tiles // tiles_each):
        field = slot_rows(slots_ref, part, tiles_each)
        group, row4, col = slot_places(field, rows)
        dual = field(4)
        left = jnp.where(iota((groups, chunk), 0) == group, 1.0, 0.0).astype(BF16)
        cells = iota((width, chunk), 0)
        here, beside = cells == col, cells == col + 1
        corners = [field(num) * dual for num in range(4)]
        rights = [[], []]
        for j in range(5):
            first = split_two(corner_rows(row4, corners[0], corners[2], j))
            second = split_two(corner_rows(row4, corners[1], corners[3], j))
            for term in range(2):
                rights[term].append(
                    jnp.where(here, first[term], jnp.where(beside, second[term], 0.0)).astype(BF16)
                )
        added = lax.dot_general(
            left, jnp.concatenate(rights[0] + rights[1], axis=0), dims, preferred_element_type=F32
        )
        if part == 0:
            acc_ref[...] = added
        else:
            acc_ref[...] += added
    fields = forcing_ref.shape[0] // rows
    per = rows // 4

    def term_sum(start, j):
        span = slice(start, start + TILE)
        return acc_ref[span, j * width : (j + 1) * width] + acc_ref[span, (j + 5) * width : (j + 6) * width]

    for place in range(fields):
        for four in range(per):
            start = (place * per + four) * TILE
            for j in range(4):
                value = term_sum(start, j)
                if j == 0 and four > 0:
                    value = value + term_sum(start - TILE, 4)
                forcing_ref[place * rows + four * 4 + j] = value


def gather_kernel(got_ref, traj_ref, earlier_ref, unused_ref, out_ref, slots_ref, picked_ref, *, groups, width, rows, half):
    unshuffle(got_ref, slots_ref)
    tiles = slots_ref.shape[0]
    tiles_each = min(4, tiles // 2)
    chunk = tiles_each * LANES
    size = 2 * tiles_each
    if half == 1:
        out_ref[:tiles, :] = earlier_ref[...]
    parts = tiles // tiles_each // 2
    for part in range(half * parts, (half + 1) * parts):
        field = slot_rows(slots_ref, part, tiles_each)
        group, row4, col = slot_places(field, rows)
        right = jnp.where(iota((groups, chunk), 0) == group, 1.0, 0.0).astype(BF16)
        cells = iota((width, chunk), 0)
        here, beside = cells == col, cells == col + 1
        total = jnp.zeros((width, chunk), F32)
        picked_ref[part % 2] = jnp.dot(traj_ref[...], right, preferred_element_type=F32)
        for j in range(5):
            picked = (
                picked_ref[part % 2, j * width : (j + 1) * width]
                + picked_ref[part % 2, (j + 5) * width : (j + 6) * width]
            )
            first = corner_rows(row4, field(0), field(2), j)
            second = corner_rows(row4, field(1), field(3), j)
            total = total + picked * jnp.where(here, first, jnp.where(beside, second, 0.0))
        value = jnp.sum(total, axis=0, keepdims=True)
        lines = []
        for t in range(tiles_each):
            line = value[:, t * LANES : (t + 1) * LANES]
            lines += [line, pltpu.roll(line, 64, 1)]
        out_ref[part * size : (part + 1) * size, :] = jnp.concatenate(lines, axis=0)


def finish_obs_kernel(unused_ref, back_ref, rank_ref, base_ref, out_ref):
    blocks = back_ref.shape[0]
    count = base_ref.shape[1]
    chunk = min(512, count)
    high, low = split_two(back_ref[...].T)
    high, low = high.astype(BF16), low.astype(BF16)
    for part in range(count // chunk):
        here = slice(part * chunk, (part + 1) * chunk)
        hit = jnp.where(iota((blocks, chunk), 0) == rank_ref[1:2, here], 1.0, 0.0).astype(BF16)
        picked = jnp.dot(high, hit, preferred_element_type=F32) + jnp.dot(
            low, hit, preferred_element_type=F32
        )
        wanted = iota((LANES, chunk), 0) == rank_ref[0:1, here]
        value = jnp.sum(jnp.where(wanted, picked, 0.0), axis=0, keepdims=True)
        out_ref[:, here] = base_ref[:, here] + value


class Plan:
    def __init__(self, fields):
        self.fields = {}
        tile = 0
        for name, num, source, wide in fields:
            self.fields[name, num] = (source, wide, tile, tile)
            tile += wide
        self.tiles = tile
        self.deep = max(wide for name, num, source, wide in fields)


def own_plan(variables):
    fields = [("x", var, ("own", var), 3) for var in range(variables)]
    fields += [("u", 0, ("own", variables), 3), ("v", 0, ("own", variables + 1), 3)]
    return Plan(fields)


def later_plan(variables, windows):
    fields = [("next", var, ("next", var), 3) for var in range(variables)]
    for window, wide in ((0, 9), (1, 6), (2, 3)):
        fields.append(("mult", window, ("dealt", window), wide))
    for window, wide in ((0, 8), (1, 5), (2, 2)):
        fields.append(("du", window, ("dealt", windows + 2 * window), wide))
        fields.append(("dv", window, ("dealt", windows + 2 * window + 1), wide))
    for step in (2, 1):
        for var in range(variables):
            fields.append((("force", step), var, ("forcing", step * variables + var), step))
    return Plan(fields)


def by_comp(shape, value_of):
    sub = iota(shape, 0)
    result = jnp.zeros(shape, F32)
    for comp in range(TILE):
        result = jnp.where(sub == comp, value_of(comp), result)
    return result


def sides(lat_count):
    lat = lax.axis_index("lat")
    return jnp.where(lat > 0, 1.0, 0.0), jnp.where(lat < lat_count - 1, 1.0, 0.0)


def unpack(east, west, lane0, wide):
    lane = iota(east.shape, 2)
    from_east = pltpu.roll(east, (LANES - lane0) % LANES, 2)
    from_west = pltpu.roll(west, (LANES - lane0 - wide) % LANES, 2)
    return jnp.where(lane < wide, from_east, jnp.where(lane >= LANES - wide, from_west, 0.0))


def spans(rows, ring, edge_masks):
    result = []
    if ring:
        result.append((0, ring, edge_masks[0]))
    result += [(ring + start, 4, None) for start in range(0, rows, 4)]
    if ring:
        result.append((ring + rows, ring, edge_masks[1]))
    return result


def masked(value, mask):
    return value if mask is None else value * mask


def load_field(dst_ref, plan, name, num, refs, rows, edge_masks, scale=None):
    (kind, place), wide, tile, lane0 = plan.fields[name, num]
    source_ref = refs[kind]
    for start, size, mask in spans(rows, wide, edge_masks):
        if start < wide:
            centre = refs["south"][tile : tile + wide]
        elif start >= wide + rows:
            centre = refs["north"][tile : tile + wide]
        else:
            first = place * rows + start - wide
            centre = source_ref[first : first + size]
        at = plan.deep - wide + start
        beside = unpack(refs["east"][at : at + size], refs["west"][at : at + size], lane0, wide)
        for part, value in enumerate((centre, beside)):
            if scale is not None:
                value = value * scale
            dst_ref[part, start : start + size] = masked(value, mask)


def east_west(centre_e, halo_e, centre_w, halo_w):
    lane = iota(centre_e.shape, 2)
    ce, he = pltpu.roll(centre_e, LANES - 1, 2), pltpu.roll(halo_e, LANES - 1, 2)
    cw, hw = pltpu.roll(centre_w, 1, 2), pltpu.roll(halo_w, 1, 2)
    last, start = lane == LANES - 1, lane == 0
    east = (jnp.where(last, he, ce), jnp.where(last, ce, he))
    west = (jnp.where(start, hw, cw), jnp.where(start, cw, hw))
    return east, west


def tangent(src_ref, dst_ref, u_ref, v_ref, wind_ring, rate, rows, ring, edge_masks):
    parts = 1 if ring == 0 else 2
    for start, size, mask in spans(rows, ring, edge_masks):
        field = [src_ref[part, start : start + size + 2] for part in range(2)]
        middle = [part[1:-1] for part in field]
        east, west = east_west(*middle, *middle)
        wind = slice(wind_ring - ring + start, wind_ring - ring + start + size)
        for part in range(parts):
            north, south = field[part][2:], field[part][:-2]
            e, w, f = east[part], west[part], middle[part]
            value = (
                f
                + rate * ((e + w) + (north + south) - 4.0 * f)
                - u_ref[part, wind] * (e - w)
                - v_ref[part, wind] * (north - south)
            )
            dst_ref[part, start : start + size] = masked(value, mask)


def adjoint(src_ref, dst_ref, u_ref, v_ref, wind_ring, rate, rows, ring, edge_masks, add):
    parts = 1 if ring == 0 else 2
    for start, size, mask in spans(rows, ring, edge_masks):
        first = wind_ring - ring - 1 + start
        eastward, westward, result = [], [], []
        for part in range(2):
            field = src_ref[part, start : start + size + 2]
            thin = rate * field
            across = v_ref[part, first : first + size + 2] * field
            along = u_ref[part, first + 1 : first + 1 + size] * field[1:-1]
            eastward.append(thin[1:-1] + along)
            westward.append(thin[1:-1] - along)
            result.append(
                field[1:-1] - 4.0 * thin[1:-1] + (thin[2:] + across[2:]) + (thin[:-2] - across[:-2])
            )
        east, west = east_west(*eastward, *westward)
        extra = add(start, size)
        for part in range(parts):
            value = result[part] + (east[part] + west[part]) + extra[part]
            dst_ref[part, start : start + size] = masked(value, mask)


def edges(plan, sources, rows, low_ref, high_ref, west_ref, east_ref):
    def tile_at(kind, place, row):
        at = (place * rows + row) * TILE
        return sources[kind][at : at + TILE, :]

    for (kind, place), wide, tile, lane0 in plan.fields.values():
        for num in range(wide):
            low_ref[tile + num] = tile_at(kind, place, num)
            high_ref[tile + num] = tile_at(kind, place, rows - wide + num)
    for row in range(rows):
        packed = None
        for (kind, place), wide, tile, lane0 in plan.fields.values():
            packed = pack(packed, tile_at(kind, place, row), lane0, wide)
        west_ref[row], east_ref[row] = packed


def entry_kernel(
    error_ref, owner_hbm, cell_hbm, layer_hbm, weight_hbm, dual_hbm, noise_hbm, mult_hbm, u_hbm, v_hbm, x_hbm,
    send_ref, rank_ref, base_ref, own_ref, low_ref, high_ref, west_ref, east_ref, *refs,
    plan, rows, variables, levels, windows, blocks, cap
):
    part_refs, refs = refs[:windows], refs[windows:]
    (owner_ref, cell_ref, layer_ref, weight_ref, dual_ref, noise_ref, mult_ref, u_ref, v_ref, x_ref) = refs[:10]
    fields_ref, acc_ref, sems = refs[10:]
    pairs = (
        (owner_hbm, owner_ref), (cell_hbm, cell_ref), (layer_hbm, layer_ref), (weight_hbm, weight_ref),
        (dual_hbm, dual_ref), (noise_hbm, noise_ref), (mult_hbm, mult_ref), (u_hbm, u_ref), (v_hbm, v_ref),
        (x_hbm, x_ref),
    )
    copies = [pltpu.make_async_copy(src, dst, sems.at[num]) for num, (src, dst) in enumerate(pairs)]
    for copy in copies:
        copy.start()
    for copy in copies[:6]:
        copy.wait()
    width = mult_ref.shape[1]
    base_ref[...] = noise_ref[...] * dual_ref[...]
    route(
        owner_ref, cell_ref, layer_ref, weight_ref, dual_ref, send_ref, rank_ref, fields_ref, acc_ref,
        blocks, cap, rows, width,
    )
    for copy in copies[6:]:
        copy.wait()
    share = levels // windows
    for shift, part_ref in enumerate(part_refs):
        target = lax.rem(lax.axis_index("tm") + shift, windows)
        whole = shift == windows - 1
        first = variables * levels * rows if whole else rows * TILE
        if whole:
            part_ref[:first, :] = mult_ref[...]
        for near in range(share):
            level = target * share + near
            for var in range(0 if whole else variables):
                start = pl.multiple_of((var * levels + level) * rows, TILE)
                value = mult_ref[pl.ds(start, rows), :] * error_ref[var, level]
                part_ref[pl.ds(near * variables + var, rows, stride=TILE), :] = value
            start = pl.multiple_of(level * rows, TILE)
            for num, ref in enumerate((u_ref, v_ref)):
                part_ref[pl.ds(first + num * share + near, rows, stride=2 * share), :] = ref[
                    pl.ds(start, rows), :
                ]
    place = 0
    for ref, count in ((x_ref, variables), (u_ref, 1), (v_ref, 1)):
        for num in range(count):
            for level in range(levels):
                value = ref[(num * levels + level) * rows : (num * levels + level + 1) * rows, :]
                own_ref[pl.ds(place * rows * TILE + level, rows, stride=TILE), :] = value
            place += 1
    edges(plan, {"own": own_ref}, rows, low_ref, high_ref, west_ref, east_ref)


def rows_kernel(error_ref, forcing_ref, *refs, plan, rows, variables, levels, windows):
    part_refs, (next_ref, dealt_ref, low_ref, high_ref, west_ref, east_ref) = refs[:windows], refs[windows:]
    share = levels // windows
    has_next = jnp.where(lax.axis_index("tm") < windows - 1, 1.0, 0.0)
    after_ref = part_refs[-1]
    for var in range(variables):
        for level in range(levels):
            start = (var * levels + level) * rows
            next_ref[pl.ds(var * rows * TILE + level, rows, stride=TILE), :] = (
                after_ref[start : start + rows, :] * has_next
            )
    whole = rows * TILE
    sub = iota((TILE, LANES), 0)
    for shift, ref in enumerate(part_refs):
        window = lax.rem(lax.axis_index("tm") - shift + windows, windows)
        start = pl.multiple_of(window * whole, TILE)
        if ref is after_ref:
            first = variables * levels * rows
            for near in range(share):
                level = lax.axis_index("tm") * share + near
                for var in range(variables):
                    at = pl.multiple_of((var * levels + level) * rows, TILE)
                    dealt_ref[pl.ds(start + near * variables + var, rows, stride=TILE), :] = (
                        ref[pl.ds(at, rows), :] * error_ref[var, level]
                    )
        else:
            first = whole
            dealt_ref[pl.ds(start, whole), :] = ref[:whole, :]
        start = (windows + 2 * window) * whole
        for row in range(rows):
            line = first + row * 2 * share
            for num in range(2):
                near, far = ref[line + num * share : line + num * share + 1, :], ref[
                    line + num * share + share - 1 : line + num * share + share, :
                ]
                at = pl.multiple_of(start + num * whole + row * TILE, TILE)
                dealt_ref[pl.ds(at, TILE), :] = jnp.where(sub < TILE // share, near, far)
    sources = {"next": next_ref, "dealt": dealt_ref, "forcing": forcing_ref}
    edges(plan, sources, rows, low_ref, high_ref, west_ref, east_ref)


def pack(packed, field, lane0, wide):
    lane = iota(field.shape, 1)
    inside = (lane >= lane0) & (lane < lane0 + wide)
    if packed is None:
        packed = (jnp.zeros_like(field), jnp.zeros_like(field))
    west = jnp.where(inside, pltpu.roll(field, lane0, 1), packed[0])
    east = jnp.where(inside, pltpu.roll(field, (lane0 + wide) % LANES, 1), packed[1])
    return west, east


def columns_kernel(unused_ref, south_ref, north_ref, west_inner_ref, east_inner_ref, west_ref, east_ref, *, plan, rows):
    deep = plan.deep
    west_ref[deep : deep + rows] = west_inner_ref[...]
    east_ref[deep : deep + rows] = east_inner_ref[...]
    for away in range(deep):
        low = high = None
        for source, wide, tile, lane0 in plan.fields.values():
            if away < wide:
                low = pack(low, south_ref[tile + wide - 1 - away], lane0, wide)
                high = pack(high, north_ref[tile + away], lane0, wide)
        west_ref[deep - 1 - away], east_ref[deep - 1 - away] = low
        west_ref[deep + rows + away], east_ref[deep + rows + away] = high


def chain_kernel(
    rate_ref, unused_ref, dealt_ref, south_ref, north_ref, east_ref, west_ref, *refs, plan, lat_count, rows, variables, windows
):
    out_refs, (u_ref, v_ref, a_ref, b_ref, m_ref, q_ref) = refs[:windows], refs[windows:]
    share = TILE // variables
    masks = sides(lat_count)
    rate = by_comp(
        (TILE, LANES), lambda comp: rate_ref[comp % variables, lax.axis_index("tm") * share + comp // variables]
    )[None]
    refs = {"dealt": dealt_ref, "south": south_ref, "north": north_ref, "east": east_ref, "west": west_ref}
    load_field(a_ref, plan, "mult", 0, refs, rows, masks)
    here, there = a_ref, b_ref
    q_ref[0] = dealt_ref[0:rows]
    for window in range(windows - 1):
        ring = 3 * (windows - 1 - window)
        load_field(u_ref, plan, "du", window, refs, rows, masks, 0.5)
        load_field(v_ref, plan, "dv", window, refs, rows, masks, 0.5)
        wind_ring = ring - 1
        for step in range(STEPS):
            ring -= 1
            tangent(here, there, u_ref, v_ref, wind_ring, rate, rows, ring, masks)
            here, there = there, here
        if window + 1 < windows - 1:
            load_field(m_ref, plan, "mult", window + 1, refs, rows, masks)
            for start in range(0, rows + 2 * ring, 2):
                for part in range(2):
                    here[part, start : start + 2] = (
                        here[part, start : start + 2] + m_ref[part, start : start + 2]
                    )
            q_ref[window + 1] = here[0, ring : ring + rows]
        else:
            q_ref[window + 1] = here[0, 0:rows] + dealt_ref[(window + 1) * rows : (window + 2) * rows]
    for shift, out_ref in enumerate(out_refs):
        out_ref[...] = q_ref[lax.rem(lax.axis_index("tm") + shift, windows)]


def forward_kernel(
    rate_ref, unused_ref, own_ref, south_ref, north_ref, east_ref, west_ref,
    terms_ref, end_ref, traj_ref, u_ref, v_ref, a_ref, b_ref, *, plan, lat_count, rows, variables
):
    masks = sides(lat_count)
    refs = {"own": own_ref, "south": south_ref, "north": north_ref, "east": east_ref, "west": west_ref}
    load_field(u_ref, plan, "u", 0, refs, rows, masks, 0.5)
    load_field(v_ref, plan, "v", 0, refs, rows, masks, 0.5)
    for var in range(variables):
        rate = by_comp((TILE, LANES), lambda level: rate_ref[var, level])[None]
        load_field(a_ref.at[var], plan, "x", var, refs, rows, masks)
        here, there = a_ref.at[var], b_ref.at[var]
        for step in range(STEPS):
            ring = STEPS - 1 - step
            traj_ref[(step * variables + var) * rows : (step * variables + var + 1) * rows] = here[
                0, ring + 1 : ring + 1 + rows
            ]
            tangent(here, there, u_ref, v_ref, 3, rate, rows, ring, masks)
            here, there = there, here
        end_ref[var * rows : (var + 1) * rows] = here[0, 0:rows]
    groups = terms_ref.shape[1]
    for j in range(5):
        if j < 4:
            tiles = [traj_ref[place * 4 + j] for place in range(groups // TILE)]
            turned = jnp.concatenate(tiles, axis=0).T
            if j == 0:
                initial = turned
        else:
            turned = pltpu.roll(initial, groups - TILE, 1)
        high = turned.astype(BF16)
        terms_ref[j * LANES : (j + 1) * LANES, :] = high
        low = (turned - high.astype(F32)).astype(BF16)
        terms_ref[(j + 5) * LANES : (j + 6) * LANES, :] = low


def final_kernel(
    rate_ref, error_ref, x_hbm, mult_hbm, own_ref, south_ref, north_ref, east_ref, west_ref,
    next_ref, later_south_ref, later_north_ref, later_east_ref, later_west_ref, forcing_ref, prior_ref, *refs,
    plan, later, lat_count, rows, variables, levels, windows
):
    chain_refs, refs = refs[:windows], refs[windows:]
    out_hbms, (x_ref, mult_ref), stages, refs = refs[:3], refs[3:5], refs[5:8], refs[8:]
    state_ref, model_ref, sum_ref = stages
    u_ref, v_ref, a_ref, b_ref, in_sems, out_sems = refs
    copies = [
        pltpu.make_async_copy(src, dst, in_sems.at[num])
        for num, (src, dst) in enumerate(((x_hbm, x_ref), (mult_hbm, mult_ref)))
    ]
    for copy in copies:
        copy.start()
    sent = []

    def send(num, var):
        span = pl.ds(var * levels * rows, levels * rows)
        copy = pltpu.make_async_copy(
            stages[num].at[span], out_hbms[num].at[span], out_sems.at[num * variables + var]
        )
        copy.start()
        sent.append(copy)

    masks = sides(lat_count)
    refs = {"own": own_ref, "south": south_ref, "north": north_ref, "east": east_ref, "west": west_ref}
    later_refs = {
        "next": next_ref, "south": later_south_ref, "north": later_north_ref, "east": later_east_ref, "west": later_west_ref,
    }
    load_field(u_ref, plan, "u", 0, refs, rows, masks, 0.5)
    load_field(v_ref, plan, "v", 0, refs, rows, masks, 0.5)
    for copy in copies:
        copy.wait()
    share = levels // windows
    has_prior = jnp.where(lax.axis_index("tm") > 0, 1.0, 0.0)
    for var in range(variables):
        for level in range(levels):
            span = slice((var * levels + level) * rows, (var * levels + level + 1) * rows)
            prior = prior_ref[pl.ds(var * rows * TILE + level, rows, stride=TILE), :]
            model_ref[span, :] = mult_ref[span, :] * error_ref[var, level] + x_ref[span, :] - has_prior * prior
        send(1, var)
    for shift, ref in enumerate(chain_refs):
        source = lax.rem(lax.axis_index("tm") - shift + windows, windows)
        for near in range(share):
            for var in range(variables):
                start = pl.multiple_of((var * levels + source * share + near) * rows, TILE)
                sum_ref[pl.ds(start, rows), :] = (
                    x_ref[pl.ds(start, rows), :] + ref[pl.ds(near * variables + var, rows, stride=TILE), :]
                )
    for var in range(variables):
        send(2, var)
    for var in range(variables):
        rate = by_comp((TILE, LANES), lambda level: rate_ref[var, level])[None]
        here, there = a_ref.at[var], b_ref.at[var]
        load_field(here, later, "next", var, later_refs, rows, masks, -1.0)
        for step in (2, 1, 0):

            def add(start, size, step=step, var=var):
                base = (step * variables + var) * rows
                if step == 0:
                    return (forcing_ref[base + start : base + start + size],)
                tile = later.fields[("force", step), var][2]
                if start < step:
                    centre = later_south_ref[tile : tile + size]
                elif start >= step + rows:
                    centre = later_north_ref[tile : tile + size]
                else:
                    centre = forcing_ref[base + start - step : base + start - step + size]
                span = slice(later.deep - step + start, later.deep - step + start + size)
                beside = unpack(later_east_ref[span], later_west_ref[span], tile, step)
                return centre, beside

            adjoint(here, there, u_ref, v_ref, 3, rate, rows, step, masks, add)
            here, there = there, here
        for row in range(rows):
            span = pl.ds(var * levels * rows + row, levels, stride=rows)
            state_ref[span, :] = mult_ref[span, :] + here[0, row]
        send(0, var)
    for copy in sent:
        copy.wait()


def shards(
    increment, multiplier, u_wind, v_wind, diffusion, error_var, obs_owner, obs_cell, obs_layer, obs_weight, obs_dual, obs_error
):
    variables, levels, rows, width = increment.shape[1:]
    flat = (variables * levels * rows, width)
    x, mult = increment.reshape(flat), multiplier.reshape(flat)
    u, v = u_wind.reshape(levels * rows, width), v_wind.reshape(levels * rows, width)
    lat_count, windows = lax.axis_size("lat"), lax.axis_size("tm")
    blocks = lat_count * lax.axis_size("lon")
    plan, later = own_plan(variables), later_plan(variables, lax.axis_size("tm"))
    own_fields = variables + 2
    count = obs_owner.shape[0]
    cap = 2 * count // blocks
    groups = STEPS * variables * levels * rows // 4

    def planes(ring):
        return pltpu.VMEM((2, rows + 2 * ring, TILE, LANES), F32)

    def tiles(array):
        return array.reshape(array.shape[0] // TILE, TILE, width)

    def lines(array):
        return array.reshape(array.shape[0] * TILE, width)

    row = (1, count)
    share = levels // windows
    part_rows = rows * (TILE + 2 * share)
    wholes = [sds((part_rows, width))] * (windows - 1) + [sds((flat[0] + rows * 2 * share, width))]
    def buffers(plan):
        row_edges, inner = sds((plan.tiles, TILE, width)), sds((rows, TILE, width))
        return [row_edges, row_edges, inner, inner]

    def over(axis, low, high):
        return lax.ppermute(high, axis, ring(axis, 1)), lax.ppermute(low, axis, ring(axis, -1))

    def columns(plan, unused, south, north, west_inner, east_inner):
        return call(
            functools.partial(columns_kernel, plan=plan, rows=rows),
            (sds((rows + 2 * plan.deep, TILE, width)),) * 2,
            unused, south, north, west_inner, east_inner, name="columns", flops=COST["columns"], loose=(0,),
        )

    send, rank, base, own, low, high, west_inner, east_inner, *parts = call(
        functools.partial(
            entry_kernel, plan=plan, rows=rows, variables=variables, levels=levels, windows=windows, blocks=blocks, cap=cap
        ),
        [
            sds((4 * blocks, 2 * cap)), sds((2, count), jnp.int32), sds(row), sds((own_fields * rows * TILE, width)),
            *buffers(plan), *wholes,
        ],
        error_var, obs_owner.reshape(row), obs_cell.reshape(row), obs_layer.reshape(row), obs_weight.T,
        obs_dual.reshape(row), obs_error.reshape(row), mult, u, v, x,
        name="entry", flops=COST["entry"], smem=(0,), hbm=range(1, 11), vmem=60,
        scratch=(
            *[pltpu.VMEM(row, jnp.int32)] * 3, pltpu.VMEM((4, count), F32), *[pltpu.VMEM(row, F32)] * 2,
            pltpu.VMEM(flat, F32), *[pltpu.VMEM((levels * rows, width), F32)] * 2, pltpu.VMEM(flat, F32),
            pltpu.VMEM((2 * TILE, count), F32), pltpu.VMEM((4 * blocks, 2 * cap), F32), pltpu.SemaphoreType.DMA((10,)),
        ),
    )
    south, north = over("lat", low, high)
    got = lax.all_to_all(send, ("lat", "lon"), split_axis=0, concat_axis=0, tiled=True)
    parts = [lax.ppermute(part, "tm", ring("tm", shift)) if shift else part for shift, part in enumerate(parts)]
    west, east = over("lon", *columns(plan, got, south, north, west_inner, east_inner))

    slots = pltpu.VMEM((4 * blocks // TILE, TILE, LANES), F32)
    forcing = call(
        functools.partial(scatter_kernel, groups=groups, width=width, rows=rows),
        sds((4 * groups // TILE, TILE, width)),
        got, name="scatter", flops=COST["scatter"],
        scratch=(slots, pltpu.VMEM((groups, 10 * width), F32)),
    )
    after, dealt, low, high, west_inner, east_inner = call(
        functools.partial(rows_kernel, plan=later, rows=rows, variables=variables, levels=levels, windows=windows),
        [sds(flat), sds((3 * windows * rows * TILE, width)), *buffers(later)],
        error_var, lines(forcing), *parts, smem=(0,), name="rows", flops=COST["rows"],
    )
    own, after, dealt = tiles(own), tiles(after), tiles(dealt)
    later_south, later_north = over("lat", low, high)

    stage = pltpu.VMEM((variables, 2, rows + 6, TILE, LANES), F32)
    sizes = dict(lat_count=lat_count, rows=rows, variables=variables)
    terms, end = call(
        functools.partial(forward_kernel, plan=plan, **sizes),
        (sds((10 * width, groups), BF16), sds((variables * rows, TILE, width))),
        diffusion, low, own, south, north, east, west, smem=(0,), loose=(1,), name="forward", flops=COST["forward"],
        scratch=(pltpu.VMEM((4 * groups // TILE, TILE, width), F32), planes(3), planes(3), stage, stage),
    )
    prior = lax.ppermute(lines(end), "tm", ring("tm", 1))
    edges_later = columns(later, terms, later_south, later_north, west_inner, east_inner)
    later_west, later_east = over("lon", *edges_later)

    def gather(half, earlier, unused):
        return call(
            functools.partial(gather_kernel, groups=groups, width=width, rows=rows, half=half),
            sds((blocks // 2 * (half + 1), LANES)),
            got, terms, earlier, unused, name="gather", flops=COST["gather"], loose=(2, 3) if half == 0 else (3,),
            scratch=(slots, pltpu.VMEM((2, 10 * width, min(512, cap * blocks // 2)), F32)),
        )

    observed = gather(0, edges_later[0], edges_later[0])
    chained = call(
        functools.partial(chain_kernel, plan=later, windows=windows, **sizes),
        [sds((rows, TILE, width))] * windows,
        diffusion, observed, dealt, later_south, later_north, later_east, later_west,
        smem=(0,), loose=(1,), name="chain", flops=COST["chain"],
        scratch=(planes(8), planes(8), planes(9), planes(9), planes(6), pltpu.VMEM((windows, rows, TILE, LANES), F32)),
    )
    observed = gather(1, observed, chained[0])
    chained = [
        lax.ppermute(lines(part), "tm", ring("tm", shift)) if shift else lines(part)
        for shift, part in enumerate(chained)
    ]
    back = lax.all_to_all(observed, ("lat", "lon"), split_axis=0, concat_axis=0, tiled=True)

    dma = pltpu.SemaphoreType.DMA
    state_res, model_res, summed = call(
        functools.partial(
            final_kernel, plan=plan, later=later, levels=levels, windows=windows, **sizes
        ),
        [sds(flat)] * 3,
        diffusion, error_var, x, mult, own, south, north, east, west,
        after, later_south, later_north, later_east, later_west, forcing, prior, *chained,
        smem=(0, 1), hbm=(2, 3), hbm_outs=(0, 1, 2), vmem=60, name="final", flops=COST["final"],
        scratch=(
            *[pltpu.VMEM(flat, F32)] * 5, planes(3), planes(3), stage, stage, dma((2,)), dma((3 * variables,)),
        ),
    )
    obs_res = call(
        finish_obs_kernel, sds(row), state_res, back, rank, base, name="finish_obs", flops=COST["finish_obs"], loose=(0,), vmem=60,
    )
    whole = increment.shape
    return (model_res.reshape(whole), obs_res.reshape(count), state_res.reshape(whole), summed.reshape(whole))


def solution(mesh):
    fields = P("tm", None, None, "lat", "lon")
    winds = P("tm", None, "lat", "lon")
    everyone = ("tm", "lat", "lon")
    in_specs = (
        fields, fields, winds, winds, P(), P(),
        P(everyone, None), P(everyone), P(everyone), P(everyone, None), P(everyone), P(everyone),
    )
    out_specs = (fields, P(everyone), fields, fields)
    return jax.shard_map(shards, mesh=mesh, in_specs=in_specs, out_specs=out_specs, check_vma=False)
```

```python
import functools
import jax
import jax.numpy as jnp
from jax import lax
from jax.experimental import pallas as pl
from jax.experimental.pallas import tpu as pltpu
from jax.sharding import PartitionSpec as P

STEPS = 3
F32 = jnp.float32
BF16 = jnp.bfloat16
LANES = 128
TILE = 8

COST = {
    "entry": 6 * 10**9, "columns": 10**9, "scatter": 5 * 10**9, "rows": 2 * 10**9, "forward": 4 * 10**9,
    "gather": 5 * 10**9, "chain": 4 * 10**9, "final": 30 * 10**9, "finish_obs": 10**9,
}


def ring(axis, by):
    count = lax.axis_size(axis)
    return [(i, (i + by) % count) for i in range(count)]


def from_behind(shard, axis, by):
    size = lax.axis_size(axis)
    pairs = [(i, i + by) for i in range(size) if 0 <= i + by < size]
    return lax.ppermute(shard, axis, pairs)


def call(kernel, out_shape, *args, name, flops=0, smem=(), hbm=(), loose=(), hbm_outs=(), scratch=(), vmem=16):
    def spec(num, far, free=()):
        space = pltpu.HBM if num in far else pl.ANY if num in free else pltpu.VMEM
        return pl.BlockSpec(memory_space=space)

    specs = [
        pl.BlockSpec(memory_space=pltpu.SMEM) if i in smem else spec(i, hbm, loose) for i in range(len(args))
    ]
    several = isinstance(out_shape, (tuple, list))
    return pl.pallas_call(
        kernel,
        out_shape=out_shape,
        in_specs=specs,
        out_specs=[spec(i, hbm_outs) for i in range(len(out_shape))] if several else spec(0, hbm_outs),
        scratch_shapes=list(scratch),
        compiler_params=pltpu.CompilerParams(vmem_limit_bytes=vmem * 1024 * 1024),
        cost_estimate=pl.CostEstimate(flops=flops, bytes_accessed=0, transcendentals=0),
        name=name,
    )(*args)


def sds(shape, dtype=F32):
    return jax.ShapeDtypeStruct(shape, dtype)


def iota(shape, dim):
    return lax.broadcasted_iota(jnp.int32, shape, dim)


def split_two(value):
    high = value.astype(BF16).astype(F32)
    return high, value - high


def route(owner_ref, cell_ref, layer_ref, weight_ref, dual_ref, send_ref, rank_ref, fields_ref, acc_ref, blocks, cap, rows, cols):
    count = owner_ref.shape[1]
    chunk = min(256, count)
    cell = cell_ref[...]
    row = ((cell.astype(F32) + 0.5) * (1.0 / (cols - 1))).astype(jnp.int32)
    layer = layer_ref[...]
    key = (layer // TILE * rows + row) * TILE + layer % TILE
    col = cell - row * (cols - 1)
    for half in range(2):
        base = half * TILE
        fields_ref[base : base + 4, :] = weight_ref[...] if half == 0 else jnp.zeros((4, count), F32)
        if half == 1:
            fields_ref[base : base + 1, :] = dual_ref[...]
            fields_ref[base + 1 : base + 2, :] = key.astype(F32)
            fields_ref[base + 2 : base + 3, :] = col.astype(F32)
        fields_ref[base + 4 : base + 8, :] = fields_ref[base : base + 4, :]
    tri = (iota((chunk, chunk), 0) < iota((chunk, chunk), 1)).astype(F32)
    tri_ones = jnp.concatenate([tri, jnp.ones((chunk, LANES), F32)], axis=1).astype(BF16)
    running = jnp.zeros((blocks, 1), F32)
    acc_ref[...] = jnp.zeros_like(acc_ref)
    pair = 2 * iota((blocks // 2, TILE, chunk), 0) + iota((blocks // 2, TILE, chunk), 1) // 4
    for part in range(count // chunk):
        here = slice(part * chunk, (part + 1) * chunk)
        owner = owner_ref[:, here]
        hit = iota((blocks, chunk), 0) == owner
        hit_f = jnp.where(hit, 1.0, 0.0)
        counted = jnp.dot(hit_f.astype(BF16), tri_ones, preferred_element_type=F32)
        before = counted[:, :chunk] + running
        running = running + counted[:, chunk : chunk + 1]
        rank = jnp.sum(jnp.where(hit, before, 0.0), axis=0, keepdims=True).astype(jnp.int32)
        rank_ref[0:1, here] = rank
        rank_ref[1:2, here] = owner
        ranks = iota((2 * cap, chunk), 0)
        right = jnp.concatenate(
            [jnp.where(ranks == rank, 1.0, 0.0), jnp.where(ranks == rank + cap, 1.0, 0.0)], axis=1
        ).astype(BF16)
        mine = pair == owner[None]
        highs, lows = [], []
        for half in range(2):
            high, low = split_two(fields_ref[half * TILE : (half + 1) * TILE, here])
            highs.append(jnp.where(mine, high[None], 0.0).reshape(4 * blocks, chunk).astype(BF16))
            lows.append(jnp.where(mine, low[None], 0.0).reshape(4 * blocks, chunk).astype(BF16))
        for left in (jnp.concatenate(highs, axis=1), jnp.concatenate(lows, axis=1)):
            acc_ref[...] += lax.dot_general(
                left, right, (((1,), (1,)), ((), ())), preferred_element_type=F32
            )
    send_ref[...] = acc_ref[...]


def unshuffle(got_ref, slots_ref):
    tiles = slots_ref.shape[0]
    keep = (iota((TILE, LANES), 0) < 4) == (iota((TILE, LANES), 1) < 64)
    for tile in range(tiles):
        value = got_ref[tile * TILE : (tile + 1) * TILE, :]
        other = pltpu.roll(pltpu.roll(value, 4, 0), 64, 1)
        slots_ref[tile] = jnp.where(keep, value, other)


def slot_rows(slots_ref, part, tiles_each):
    def field(num):
        return jnp.concatenate(
            [slots_ref[part * tiles_each + t, num : num + 1, :] for t in range(tiles_each)], axis=1
        )

    return field


def corner_rows(row4, tops, bottoms, j):
    zero = jnp.zeros_like(tops)
    return jnp.where(row4 == j, tops, jnp.where(row4 + 1 == j, bottoms, zero))


def slot_places(field, rows):
    key = field(5).astype(jnp.int32)
    line = key // TILE
    group = line // 4 * TILE + key % TILE
    return group, line % 4, field(6).astype(jnp.int32)


def scatter_kernel(got_ref, forcing_ref, slots_ref, acc_ref, *, groups, width, rows):
    unshuffle(got_ref, slots_ref)
    tiles = slots_ref.shape[0]
    tiles_each = min(4, tiles)
    chunk = tiles_each * LANES
    dims = (((1,), (1,)), ((), ()))
    for part in range(tiles // tiles_each):
        field = slot_rows(slots_ref, part, tiles_each)
        group, row4, col = slot_places(field, rows)
        dual = field(4)
        left = jnp.where(iota((groups, chunk), 0) == group, 1.0, 0.0).astype(BF16)
        cells = iota((width, chunk), 0)
        here, beside = cells == col, cells == col + 1
        corners = [field(num) * dual for num in range(4)]
        rights = [[], []]
        for j in range(5):
            first = split_two(corner_rows(row4, corners[0], corners[2], j))
            second = split_two(corner_rows(row4, corners[1], corners[3], j))
            for term in range(2):
                rights[term].append(
                    jnp.where(here, first[term], jnp.where(beside, second[term], 0.0)).astype(BF16)
                )
        added = lax.dot_general(
            left, jnp.concatenate(rights[0] + rights[1], axis=0), dims, preferred_element_type=F32
        )
        if part == 0:
            acc_ref[...] = added
        else:
            acc_ref[...] += added
    fields = forcing_ref.shape[0] // rows
    per = rows // 4

    def term_sum(start, j):
        span = slice(start, start + TILE)
        return acc_ref[span, j * width : (j + 1) * width] + acc_ref[span, (j + 5) * width : (j + 6) * width]

    for place in range(fields):
        for four in range(per):
            start = (place * per + four) * TILE
            for j in range(4):
                value = term_sum(start, j)
                if j == 0 and four > 0:
                    value = value + term_sum(start - TILE, 4)
                forcing_ref[place * rows + four * 4 + j] = value


def gather_kernel(got_ref, traj_ref, earlier_ref, unused_ref, out_ref, slots_ref, picked_ref, *, groups, width, rows, half):
    unshuffle(got_ref, slots_ref)
    tiles = slots_ref.shape[0]
    tiles_each = min(4, tiles // 2)
    chunk = tiles_each * LANES
    size = 2 * tiles_each
    if half == 1:
        out_ref[:tiles, :] = earlier_ref[...]
    parts = tiles // tiles_each // 2
    for part in range(half * parts, (half + 1) * parts):
        field = slot_rows(slots_ref, part, tiles_each)
        group, row4, col = slot_places(field, rows)
        right = jnp.where(iota((groups, chunk), 0) == group, 1.0, 0.0).astype(BF16)
        cells = iota((width, chunk), 0)
        here, beside = cells == col, cells == col + 1
        total = jnp.zeros((width, chunk), F32)
        picked_ref[part % 2] = jnp.dot(traj_ref[...], right, preferred_element_type=F32)
        for j in range(5):
            picked = (
                picked_ref[part % 2, j * width : (j + 1) * width]
                + picked_ref[part % 2, (j + 5) * width : (j + 6) * width]
            )
            first = corner_rows(row4, field(0), field(2), j)
            second = corner_rows(row4, field(1), field(3), j)
            total = total + picked * jnp.where(here, first, jnp.where(beside, second, 0.0))
        value = jnp.sum(total, axis=0, keepdims=True)
        lines = []
        for t in range(tiles_each):
            line = value[:, t * LANES : (t + 1) * LANES]
            lines += [line, pltpu.roll(line, 64, 1)]
        out_ref[part * size : (part + 1) * size, :] = jnp.concatenate(lines, axis=0)


def finish_obs_kernel(unused_ref, back_ref, rank_ref, base_ref, out_ref):
    blocks = back_ref.shape[0]
    count = base_ref.shape[1]
    chunk = min(512, count)
    high, low = split_two(back_ref[...].T)
    high, low = high.astype(BF16), low.astype(BF16)
    for part in range(count // chunk):
        here = slice(part * chunk, (part + 1) * chunk)
        hit = jnp.where(iota((blocks, chunk), 0) == rank_ref[1:2, here], 1.0, 0.0).astype(BF16)
        picked = jnp.dot(high, hit, preferred_element_type=F32) + jnp.dot(
            low, hit, preferred_element_type=F32
        )
        wanted = iota((LANES, chunk), 0) == rank_ref[0:1, here]
        value = jnp.sum(jnp.where(wanted, picked, 0.0), axis=0, keepdims=True)
        out_ref[:, here] = base_ref[:, here] + value


class Plan:
    def __init__(self, fields):
        self.fields = {}
        tile = 0
        for name, num, source, wide in fields:
            self.fields[name, num] = (source, wide, tile, tile)
            tile += wide
        self.tiles = tile
        self.deep = max(wide for name, num, source, wide in fields)


def own_plan(variables):
    fields = [("x", var, ("own", var), 3) for var in range(variables)]
    fields += [("u", 0, ("own", variables), 3), ("v", 0, ("own", variables + 1), 3)]
    return Plan(fields)


def later_plan(variables, windows):
    fields = [("next", var, ("next", var), 3) for var in range(variables)]
    for window, wide in ((0, 9), (1, 6), (2, 3)):
        fields.append(("mult", window, ("dealt", window), wide))
    for window, wide in ((0, 8), (1, 5), (2, 2)):
        fields.append(("du", window, ("dealt", windows + 2 * window), wide))
        fields.append(("dv", window, ("dealt", windows + 2 * window + 1), wide))
    for step in (2, 1):
        for var in range(variables):
            fields.append((("force", step), var, ("forcing", step * variables + var), step))
    return Plan(fields)


def by_comp(shape, value_of):
    sub = iota(shape, 0)
    result = jnp.zeros(shape, F32)
    for comp in range(TILE):
        result = jnp.where(sub == comp, value_of(comp), result)
    return result


def sides(lat_count):
    lat = lax.axis_index("lat")
    return jnp.where(lat > 0, 1.0, 0.0), jnp.where(lat < lat_count - 1, 1.0, 0.0)


def unpack(east, west, lane0, wide):
    lane = iota(east.shape, 2)
    from_east = pltpu.roll(east, (LANES - lane0) % LANES, 2)
    from_west = pltpu.roll(west, (LANES - lane0 - wide) % LANES, 2)
    return jnp.where(lane < wide, from_east, jnp.where(lane >= LANES - wide, from_west, 0.0))


def spans(rows, ring, edge_masks):
    result = []
    if ring:
        result.append((0, ring, edge_masks[0]))
    result += [(ring + start, 4, None) for start in range(0, rows, 4)]
    if ring:
        result.append((ring + rows, ring, edge_masks[1]))
    return result


def masked(value, mask):
    return value if mask is None else value * mask


def load_field(dst_ref, plan, name, num, refs, rows, edge_masks, scale=None):
    (kind, place), wide, tile, lane0 = plan.fields[name, num]
    source_ref = refs[kind]
    for start, size, mask in spans(rows, wide, edge_masks):
        if start < wide:
            centre = refs["south"][tile : tile + wide]
        elif start >= wide + rows:
            centre = refs["north"][tile : tile + wide]
        else:
            first = place * rows + start - wide
            centre = source_ref[first : first + size]
        at = plan.deep - wide + start
        beside = unpack(refs["east"][at : at + size], refs["west"][at : at + size], lane0, wide)
        for part, value in enumerate((centre, beside)):
            if scale is not None:
                value = value * scale
            dst_ref[part, start : start + size] = masked(value, mask)


def east_west(centre_e, halo_e, centre_w, halo_w):
    lane = iota(centre_e.shape, 2)
    ce, he = pltpu.roll(centre_e, LANES - 1, 2), pltpu.roll(halo_e, LANES - 1, 2)
    cw, hw = pltpu.roll(centre_w, 1, 2), pltpu.roll(halo_w, 1, 2)
    last, start = lane == LANES - 1, lane == 0
    east = (jnp.where(last, he, ce), jnp.where(last, ce, he))
    west = (jnp.where(start, hw, cw), jnp.where(start, cw, hw))
    return east, west


def tangent(src_ref, dst_ref, u_ref, v_ref, wind_ring, rate, rows, ring, edge_masks):
    parts = 1 if ring == 0 else 2
    for start, size, mask in spans(rows, ring, edge_masks):
        field = [src_ref[part, start : start + size + 2] for part in range(2)]
        middle = [part[1:-1] for part in field]
        east, west = east_west(*middle, *middle)
        wind = slice(wind_ring - ring + start, wind_ring - ring + start + size)
        for part in range(parts):
            north, south = field[part][2:], field[part][:-2]
            e, w, f = east[part], west[part], middle[part]
            value = (
                f
                + rate * ((e + w) + (north + south) - 4.0 * f)
                - u_ref[part, wind] * (e - w)
                - v_ref[part, wind] * (north - south)
            )
            dst_ref[part, start : start + size] = masked(value, mask)


def adjoint(src_ref, dst_ref, u_ref, v_ref, wind_ring, rate, rows, ring, edge_masks, add):
    parts = 1 if ring == 0 else 2
    for start, size, mask in spans(rows, ring, edge_masks):
        first = wind_ring - ring - 1 + start
        eastward, westward, result = [], [], []
        for part in range(2):
            field = src_ref[part, start : start + size + 2]
            thin = rate * field
            across = v_ref[part, first : first + size + 2] * field
            along = u_ref[part, first + 1 : first + 1 + size] * field[1:-1]
            eastward.append(thin[1:-1] + along)
            westward.append(thin[1:-1] - along)
            result.append(
                field[1:-1] - 4.0 * thin[1:-1] + (thin[2:] + across[2:]) + (thin[:-2] - across[:-2])
            )
        east, west = east_west(*eastward, *westward)
        extra = add(start, size)
        for part in range(parts):
            value = result[part] + (east[part] + west[part]) + extra[part]
            dst_ref[part, start : start + size] = masked(value, mask)


def edges(plan, sources, rows, low_ref, high_ref, west_ref, east_ref):
    def tile_at(kind, place, row):
        at = (place * rows + row) * TILE
        return sources[kind][at : at + TILE, :]

    for (kind, place), wide, tile, lane0 in plan.fields.values():
        for num in range(wide):
            low_ref[tile + num] = tile_at(kind, place, num)
            high_ref[tile + num] = tile_at(kind, place, rows - wide + num)
    for row in range(rows):
        packed = None
        for (kind, place), wide, tile, lane0 in plan.fields.values():
            packed = pack(packed, tile_at(kind, place, row), lane0, wide)
        west_ref[row], east_ref[row] = packed


def entry_kernel(
    error_ref, owner_hbm, cell_hbm, layer_hbm, weight_hbm, dual_hbm, noise_hbm, mult_hbm, u_hbm, v_hbm, x_hbm,
    send_ref, rank_ref, base_ref, own_ref, low_ref, high_ref, west_ref, east_ref, *refs,
    plan, rows, variables, levels, windows, blocks, cap
):
    part_refs, refs = refs[:windows], refs[windows:]
    (owner_ref, cell_ref, layer_ref, weight_ref, dual_ref, noise_ref, mult_ref, u_ref, v_ref, x_ref) = refs[:10]
    fields_ref, acc_ref, sems = refs[10:]
    pairs = (
        (owner_hbm, owner_ref), (cell_hbm, cell_ref), (layer_hbm, layer_ref), (weight_hbm, weight_ref),
        (dual_hbm, dual_ref), (noise_hbm, noise_ref), (mult_hbm, mult_ref), (u_hbm, u_ref), (v_hbm, v_ref),
        (x_hbm, x_ref),
    )
    copies = [pltpu.make_async_copy(src, dst, sems.at[num]) for num, (src, dst) in enumerate(pairs)]
    for copy in copies:
        copy.start()
    for copy in copies[:6]:
        copy.wait()
    width = mult_ref.shape[1]
    base_ref[...] = noise_ref[...] * dual_ref[...]
    route(
        owner_ref, cell_ref, layer_ref, weight_ref, dual_ref, send_ref, rank_ref, fields_ref, acc_ref,
        blocks, cap, rows, width,
    )
    for copy in copies[6:]:
        copy.wait()
    share = levels // windows
    for shift, part_ref in enumerate(part_refs):
        target = lax.rem(lax.axis_index("tm") + shift, windows)
        whole = shift == windows - 1
        first = variables * levels * rows if whole else rows * TILE
        if whole:
            part_ref[:first, :] = mult_ref[...]
        for near in range(share):
            level = target * share + near
            for var in range(0 if whole else variables):
                start = pl.multiple_of((var * levels + level) * rows, TILE)
                value = mult_ref[pl.ds(start, rows), :] * error_ref[var, level]
                part_ref[pl.ds(near * variables + var, rows, stride=TILE), :] = value
            start = pl.multiple_of(level * rows, TILE)
            for num, ref in enumerate((u_ref, v_ref)):
                part_ref[pl.ds(first + num * share + near, rows, stride=2 * share), :] = ref[
                    pl.ds(start, rows), :
                ]
    place = 0
    for ref, count in ((x_ref, variables), (u_ref, 1), (v_ref, 1)):
        for num in range(count):
            for level in range(levels):
                value = ref[(num * levels + level) * rows : (num * levels + level + 1) * rows, :]
                own_ref[pl.ds(place * rows * TILE + level, rows, stride=TILE), :] = value
            place += 1
    edges(plan, {"own": own_ref}, rows, low_ref, high_ref, west_ref, east_ref)


def rows_kernel(error_ref, forcing_ref, *refs, plan, rows, variables, levels, windows):
    part_refs, (next_ref, dealt_ref, low_ref, high_ref, west_ref, east_ref) = refs[:windows], refs[windows:]
    share = levels // windows
    has_next = jnp.where(lax.axis_index("tm") < windows - 1, 1.0, 0.0)
    after_ref = part_refs[-1]
    for var in range(variables):
        for level in range(levels):
            start = (var * levels + level) * rows
            next_ref[pl.ds(var * rows * TILE + level, rows, stride=TILE), :] = (
                after_ref[start : start + rows, :] * has_next
            )
    whole = rows * TILE
    sub = iota((TILE, LANES), 0)
    for shift, ref in enumerate(part_refs):
        window = lax.rem(lax.axis_index("tm") - shift + windows, windows)
        start = pl.multiple_of(window * whole, TILE)
        if ref is after_ref:
            first = variables * levels * rows
            for near in range(share):
                level = lax.axis_index("tm") * share + near
                for var in range(variables):
                    at = pl.multiple_of((var * levels + level) * rows, TILE)
                    dealt_ref[pl.ds(start + near * variables + var, rows, stride=TILE), :] = (
                        ref[pl.ds(at, rows), :] * error_ref[var, level]
                    )
        else:
            first = whole
            dealt_ref[pl.ds(start, whole), :] = ref[:whole, :]
        start = (windows + 2 * window) * whole
        for row in range(rows):
            line = first + row * 2 * share
            for num in range(2):
                near, far = ref[line + num * share : line + num * share + 1, :], ref[
                    line + num * share + share - 1 : line + num * share + share, :
                ]
                at = pl.multiple_of(start + num * whole + row * TILE, TILE)
                dealt_ref[pl.ds(at, TILE), :] = jnp.where(sub < TILE // share, near, far)
    sources = {"next": next_ref, "dealt": dealt_ref, "forcing": forcing_ref}
    edges(plan, sources, rows, low_ref, high_ref, west_ref, east_ref)


def pack(packed, field, lane0, wide):
    lane = iota(field.shape, 1)
    inside = (lane >= lane0) & (lane < lane0 + wide)
    if packed is None:
        packed = (jnp.zeros_like(field), jnp.zeros_like(field))
    west = jnp.where(inside, pltpu.roll(field, lane0, 1), packed[0])
    east = jnp.where(inside, pltpu.roll(field, (lane0 + wide) % LANES, 1), packed[1])
    return west, east


def columns_kernel(unused_ref, south_ref, north_ref, west_inner_ref, east_inner_ref, west_ref, east_ref, *, plan, rows):
    deep = plan.deep
    west_ref[deep : deep + rows] = west_inner_ref[...]
    east_ref[deep : deep + rows] = east_inner_ref[...]
    for away in range(deep):
        low = high = None
        for source, wide, tile, lane0 in plan.fields.values():
            if away < wide:
                low = pack(low, south_ref[tile + wide - 1 - away], lane0, wide)
                high = pack(high, north_ref[tile + away], lane0, wide)
        west_ref[deep - 1 - away], east_ref[deep - 1 - away] = low
        west_ref[deep + rows + away], east_ref[deep + rows + away] = high


def chain_kernel(
    rate_ref, unused_ref, dealt_ref, south_ref, north_ref, east_ref, west_ref, *refs, plan, lat_count, rows, variables, windows
):
    out_refs, (u_ref, v_ref, a_ref, b_ref, m_ref, q_ref) = refs[:windows], refs[windows:]
    share = TILE // variables
    masks = sides(lat_count)
    rate = by_comp(
        (TILE, LANES), lambda comp: rate_ref[comp % variables, lax.axis_index("tm") * share + comp // variables]
    )[None]
    refs = {"dealt": dealt_ref, "south": south_ref, "north": north_ref, "east": east_ref, "west": west_ref}
    load_field(a_ref, plan, "mult", 0, refs, rows, masks)
    here, there = a_ref, b_ref
    q_ref[0] = dealt_ref[0:rows]
    for window in range(windows - 1):
        ring = 3 * (windows - 1 - window)
        load_field(u_ref, plan, "du", window, refs, rows, masks, 0.5)
        load_field(v_ref, plan, "dv", window, refs, rows, masks, 0.5)
        wind_ring = ring - 1
        for step in range(STEPS):
            ring -= 1
            tangent(here, there, u_ref, v_ref, wind_ring, rate, rows, ring, masks)
            here, there = there, here
        if window + 1 < windows - 1:
            load_field(m_ref, plan, "mult", window + 1, refs, rows, masks)
            for start in range(0, rows + 2 * ring, 2):
                for part in range(2):
                    here[part, start : start + 2] = (
                        here[part, start : start + 2] + m_ref[part, start : start + 2]
                    )
            q_ref[window + 1] = here[0, ring : ring + rows]
        else:
            q_ref[window + 1] = here[0, 0:rows] + dealt_ref[(window + 1) * rows : (window + 2) * rows]
    for shift, out_ref in enumerate(out_refs):
        out_ref[...] = q_ref[lax.rem(lax.axis_index("tm") + shift, windows)]


def forward_kernel(
    rate_ref, unused_ref, own_ref, south_ref, north_ref, east_ref, west_ref,
    terms_ref, end_ref, traj_ref, u_ref, v_ref, a_ref, b_ref, *, plan, lat_count, rows, variables
):
    masks = sides(lat_count)
    refs = {"own": own_ref, "south": south_ref, "north": north_ref, "east": east_ref, "west": west_ref}
    load_field(u_ref, plan, "u", 0, refs, rows, masks, 0.5)
    load_field(v_ref, plan, "v", 0, refs, rows, masks, 0.5)
    for var in range(variables):
        rate = by_comp((TILE, LANES), lambda level: rate_ref[var, level])[None]
        load_field(a_ref.at[var], plan, "x", var, refs, rows, masks)
        here, there = a_ref.at[var], b_ref.at[var]
        for step in range(STEPS):
            ring = STEPS - 1 - step
            traj_ref[(step * variables + var) * rows : (step * variables + var + 1) * rows] = here[
                0, ring + 1 : ring + 1 + rows
            ]
            tangent(here, there, u_ref, v_ref, 3, rate, rows, ring, masks)
            here, there = there, here
        end_ref[var * rows : (var + 1) * rows] = here[0, 0:rows]
    groups = terms_ref.shape[1]
    for j in range(5):
        if j < 4:
            tiles = [traj_ref[place * 4 + j] for place in range(groups // TILE)]
            turned = jnp.concatenate(tiles, axis=0).T
            if j == 0:
                initial = turned
        else:
            turned = pltpu.roll(initial, groups - TILE, 1)
        high = turned.astype(BF16)
        terms_ref[j * LANES : (j + 1) * LANES, :] = high
        low = (turned - high.astype(F32)).astype(BF16)
        terms_ref[(j + 5) * LANES : (j + 6) * LANES, :] = low


def final_kernel(
    rate_ref, error_ref, x_hbm, mult_hbm, own_hbm, south_ref, north_ref, east_ref, west_ref,
    next_hbm, later_south_ref, later_north_ref, later_east_ref, later_west_ref, forcing_hbm, prior_ref, *refs,
    plan, later, lat_count, rows, variables, levels, windows
):
    chain_refs, refs = refs[:windows], refs[windows:]
    out_hbms, stages, refs = refs[:3], refs[3:6], refs[6:]
    (x_ref, mult_ref, own_ref, next_ref, forcing_ref), refs = refs[:5], refs[5:]
    state_ref, model_ref, sum_ref = stages
    u_ref, v_ref, a_ref, b_ref, in_sems, out_sems = refs
    copies = [
        pltpu.make_async_copy(src, dst, in_sems.at[num])
        for num, (src, dst) in enumerate(
            (
                (x_hbm, x_ref), (mult_hbm, mult_ref), (own_hbm, own_ref), (next_hbm, next_ref),
                (forcing_hbm, forcing_ref),
            )
        )
    ]
    for copy in copies:
        copy.start()
    sent = []

    def send(num, var):
        span = pl.ds(var * levels * rows, levels * rows)
        copy = pltpu.make_async_copy(
            stages[num].at[span], out_hbms[num].at[span], out_sems.at[num * variables + var]
        )
        copy.start()
        sent.append(copy)

    masks = sides(lat_count)
    refs = {"own": own_ref, "south": south_ref, "north": north_ref, "east": east_ref, "west": west_ref}
    later_refs = {
        "next": next_ref, "south": later_south_ref, "north": later_north_ref, "east": later_east_ref, "west": later_west_ref,
    }
    for copy in copies[:2]:
        copy.wait()
    share = levels // windows
    has_prior = jnp.where(lax.axis_index("tm") > 0, 1.0, 0.0)
    for var in range(variables):
        for level in range(levels):
            span = slice((var * levels + level) * rows, (var * levels + level + 1) * rows)
            prior = prior_ref[pl.ds(var * rows * TILE + level, rows, stride=TILE), :]
            model_ref[span, :] = mult_ref[span, :] * error_ref[var, level] + x_ref[span, :] - has_prior * prior
        send(1, var)
    for shift, ref in enumerate(chain_refs):
        source = lax.rem(lax.axis_index("tm") - shift + windows, windows)
        for near in range(share):
            for var in range(variables):
                start = pl.multiple_of((var * levels + source * share + near) * rows, TILE)
                sum_ref[pl.ds(start, rows), :] = (
                    x_ref[pl.ds(start, rows), :] + ref[pl.ds(near * variables + var, rows, stride=TILE), :]
                )
    for var in range(variables):
        send(2, var)
    for copy in copies[2:]:
        copy.wait()
    load_field(u_ref, plan, "u", 0, refs, rows, masks, 0.5)
    load_field(v_ref, plan, "v", 0, refs, rows, masks, 0.5)
    for var in range(variables):
        rate = by_comp((TILE, LANES), lambda level: rate_ref[var, level])[None]
        here, there = a_ref.at[var], b_ref.at[var]
        load_field(here, later, "next", var, later_refs, rows, masks, -1.0)
        for step in (2, 1, 0):

            def add(start, size, step=step, var=var):
                base = (step * variables + var) * rows
                if step == 0:
                    return (forcing_ref[base + start : base + start + size],)
                tile = later.fields[("force", step), var][2]
                if start < step:
                    centre = later_south_ref[tile : tile + size]
                elif start >= step + rows:
                    centre = later_north_ref[tile : tile + size]
                else:
                    centre = forcing_ref[base + start - step : base + start - step + size]
                span = slice(later.deep - step + start, later.deep - step + start + size)
                beside = unpack(later_east_ref[span], later_west_ref[span], tile, step)
                return centre, beside

            adjoint(here, there, u_ref, v_ref, 3, rate, rows, step, masks, add)
            here, there = there, here
        for row in range(rows):
            span = pl.ds(var * levels * rows + row, levels, stride=rows)
            state_ref[span, :] = mult_ref[span, :] + here[0, row]
        send(0, var)
    for copy in sent:
        copy.wait()


def shards(
    increment, multiplier, u_wind, v_wind, diffusion, error_var, obs_owner, obs_cell, obs_layer, obs_weight, obs_dual, obs_error
):
    variables, levels, rows, width = increment.shape[1:]
    flat = (variables * levels * rows, width)
    x, mult = increment.reshape(flat), multiplier.reshape(flat)
    u, v = u_wind.reshape(levels * rows, width), v_wind.reshape(levels * rows, width)
    lat_count, windows = lax.axis_size("lat"), lax.axis_size("tm")
    blocks = lat_count * lax.axis_size("lon")
    plan, later = own_plan(variables), later_plan(variables, lax.axis_size("tm"))
    own_fields = variables + 2
    count = obs_owner.shape[0]
    cap = 2 * count // blocks
    groups = STEPS * variables * levels * rows // 4

    def planes(ring):
        return pltpu.VMEM((2, rows + 2 * ring, TILE, LANES), F32)

    def tiles(array):
        return array.reshape(array.shape[0] // TILE, TILE, width)

    def lines(array):
        return array.reshape(array.shape[0] * TILE, width)

    row = (1, count)
    share = levels // windows
    part_rows = rows * (TILE + 2 * share)
    wholes = [sds((part_rows, width))] * (windows - 1) + [sds((flat[0] + rows * 2 * share, width))]
    def buffers(plan):
        row_edges, inner = sds((plan.tiles, TILE, width)), sds((rows, TILE, width))
        return [row_edges, row_edges, inner, inner]

    def over(axis, low, high):
        return lax.ppermute(high, axis, ring(axis, 1)), lax.ppermute(low, axis, ring(axis, -1))

    def columns(plan, unused, south, north, west_inner, east_inner):
        return call(
            functools.partial(columns_kernel, plan=plan, rows=rows),
            (sds((rows + 2 * plan.deep, TILE, width)),) * 2,
            unused, south, north, west_inner, east_inner, name="columns", flops=COST["columns"], loose=(0,),
        )

    send, rank, base, own, low, high, west_inner, east_inner, *parts = call(
        functools.partial(
            entry_kernel, plan=plan, rows=rows, variables=variables, levels=levels, windows=windows, blocks=blocks, cap=cap
        ),
        [
            sds((4 * blocks, 2 * cap)), sds((2, count), jnp.int32), sds(row), sds((own_fields * rows * TILE, width)),
            *buffers(plan), *wholes,
        ],
        error_var, obs_owner.reshape(row), obs_cell.reshape(row), obs_layer.reshape(row), obs_weight.T,
        obs_dual.reshape(row), obs_error.reshape(row), mult, u, v, x,
        name="entry", flops=COST["entry"], smem=(0,), hbm=range(1, 11), vmem=60,
        scratch=(
            *[pltpu.VMEM(row, jnp.int32)] * 3, pltpu.VMEM((4, count), F32), *[pltpu.VMEM(row, F32)] * 2,
            pltpu.VMEM(flat, F32), *[pltpu.VMEM((levels * rows, width), F32)] * 2, pltpu.VMEM(flat, F32),
            pltpu.VMEM((2 * TILE, count), F32), pltpu.VMEM((4 * blocks, 2 * cap), F32), pltpu.SemaphoreType.DMA((10,)),
        ),
    )
    south, north = over("lat", low, high)
    got = lax.all_to_all(send, ("lat", "lon"), split_axis=0, concat_axis=0, tiled=True)
    parts = [lax.ppermute(part, "tm", ring("tm", shift)) if shift else part for shift, part in enumerate(parts)]
    west, east = over("lon", *columns(plan, got, south, north, west_inner, east_inner))

    slots = pltpu.VMEM((4 * blocks // TILE, TILE, LANES), F32)
    forcing = call(
        functools.partial(scatter_kernel, groups=groups, width=width, rows=rows),
        sds((4 * groups // TILE, TILE, width)),
        got, name="scatter", flops=COST["scatter"],
        scratch=(slots, pltpu.VMEM((groups, 10 * width), F32)),
    )
    after, dealt, low, high, west_inner, east_inner = call(
        functools.partial(rows_kernel, plan=later, rows=rows, variables=variables, levels=levels, windows=windows),
        [sds(flat), sds((3 * windows * rows * TILE, width)), *buffers(later)],
        error_var, lines(forcing), *parts, smem=(0,), name="rows", flops=COST["rows"],
    )
    own, after, dealt = tiles(own), tiles(after), tiles(dealt)
    later_south, later_north = over("lat", low, high)

    stage = pltpu.VMEM((variables, 2, rows + 6, TILE, LANES), F32)
    sizes = dict(lat_count=lat_count, rows=rows, variables=variables)
    terms, end = call(
        functools.partial(forward_kernel, plan=plan, **sizes),
        (sds((10 * width, groups), BF16), sds((variables * rows, TILE, width))),
        diffusion, low, own, south, north, east, west, smem=(0,), loose=(1,), name="forward", flops=COST["forward"],
        scratch=(pltpu.VMEM((4 * groups // TILE, TILE, width), F32), planes(3), planes(3), stage, stage),
    )
    prior = lax.ppermute(lines(end), "tm", ring("tm", 1))
    edges_later = columns(later, terms, later_south, later_north, west_inner, east_inner)
    later_west, later_east = over("lon", *edges_later)

    def gather(half, earlier, unused):
        return call(
            functools.partial(gather_kernel, groups=groups, width=width, rows=rows, half=half),
            sds((blocks // 2 * (half + 1), LANES)),
            got, terms, earlier, unused, name="gather", flops=COST["gather"], loose=(2, 3) if half == 0 else (3,),
            scratch=(slots, pltpu.VMEM((2, 10 * width, min(512, cap * blocks // 2)), F32)),
        )

    observed = gather(0, edges_later[0], edges_later[0])
    chained = call(
        functools.partial(chain_kernel, plan=later, windows=windows, **sizes),
        [sds((rows, TILE, width))] * windows,
        diffusion, observed, dealt, later_south, later_north, later_east, later_west,
        smem=(0,), loose=(1,), name="chain", flops=COST["chain"],
        scratch=(planes(8), planes(8), planes(9), planes(9), planes(6), pltpu.VMEM((windows, rows, TILE, LANES), F32)),
    )
    observed = gather(1, observed, chained[0])
    chained = [
        lax.ppermute(lines(part), "tm", ring("tm", shift)) if shift else lines(part)
        for shift, part in enumerate(chained)
    ]
    back = lax.all_to_all(observed, ("lat", "lon"), split_axis=0, concat_axis=0, tiled=True)

    dma = pltpu.SemaphoreType.DMA
    state_res, model_res, summed = call(
        functools.partial(
            final_kernel, plan=plan, later=later, levels=levels, windows=windows, **sizes
        ),
        [sds(flat)] * 3,
        diffusion, error_var, x, mult, own, south, north, east, west,
        after, later_south, later_north, later_east, later_west, forcing, prior, *chained,
        smem=(0, 1), hbm=(2, 3, 4, 9, 14), hbm_outs=(0, 1, 2), vmem=60, name="final", flops=COST["final"],
        scratch=(
            *[pltpu.VMEM(flat, F32)] * 5, pltpu.VMEM(own.shape, F32), pltpu.VMEM(after.shape, F32),
            pltpu.VMEM(forcing.shape, F32), planes(3), planes(3), stage, stage, dma((5,)), dma((3 * variables,)),
        ),
    )
    obs_res = call(
        finish_obs_kernel, sds(row), state_res, back, rank, base, name="finish_obs", flops=COST["finish_obs"], loose=(0,), vmem=60,
    )
    whole = increment.shape
    return (model_res.reshape(whole), obs_res.reshape(count), state_res.reshape(whole), summed.reshape(whole))


def solution(mesh):
    fields = P("tm", None, None, "lat", "lon")
    winds = P("tm", None, "lat", "lon")
    everyone = ("tm", "lat", "lon")
    in_specs = (
        fields, fields, winds, winds, P(), P(),
        P(everyone, None), P(everyone), P(everyone), P(everyone, None), P(everyone), P(everyone),
    )
    out_specs = (fields, P(everyone), fields, fields)
    return jax.shard_map(shards, mesh=mesh, in_specs=in_specs, out_specs=out_specs, check_vma=False)
```
